32 devices in a mesh: section: 2 (over x), rep: 4 (over y, core), shard: 4 (over z).
Axes of the slice: x: 2, y: 2, z: 4, core: 2. Of those that a mesh axis runs over, the one named last changes fastest.
Arguments:
- tokens: bfloat16 [8, 1024, 2048], P('rep', 'shard'), may hold values from -6 to 6
- cotangent: bfloat16 [8, 1024, 2048], P('rep', 'shard'), may hold values from -6 to 6
- live_counts: int32 [4], P('rep'), may hold values from 1 to 2, as said below
- w_query: bfloat16 [2, 2048, 2048], P('section', 'shard'), may hold values from -0.125 to 0.125
- w_key: bfloat16 [2, 2048, 256], P('section', 'shard'), may hold values from -0.125 to 0.125
- w_value: bfloat16 [2, 2048, 256], P('section', 'shard'), may hold values from -0.125 to 0.125
- w_out: bfloat16 [2, 2048, 2048], P('section', 'shard'), may hold values from -1.5 to 1.5
- w_gate: bfloat16 [2, 2048, 5632], P('section', 'shard'), may hold values from -0.125 to 0.125
- w_up: bfloat16 [2, 2048, 5632], P('section', 'shard'), may hold values from -0.125 to 0.125
- w_down: bfloat16 [2, 5632, 2048], P('section', 'shard'), may hold values from -0.078125 to 0.078125
- norm_gains: bfloat16 [2, 2, 2048], P('section', None, 'shard'), may hold values from 0.5 to 1.5
Outputs:
- acts: bfloat16 [2, 8, 1024, 2048], P('section', 'rep', 'shard')
- grad_in: float32 [2, 8, 1024, 2048], P('section', 'rep', 'shard')
- grad_query: float32 [2, 2048, 2048], P('section', 'shard')
- grad_key: float32 [2, 2048, 256], P('section', 'shard')
- grad_value: float32 [2, 2048, 256], P('section', 'shard')
- grad_w_out: float32 [2, 2048, 2048], P('section', 'shard')
- grad_gate: float32 [2, 2048, 5632], P('section', 'shard')
- grad_up: float32 [2, 2048, 5632], P('section', 'shard')
- grad_down: float32 [2, 5632, 2048], P('section', 'shard')
- grad_gains: float32 [2, 2, 2048], P('section', None, 'shard')
The draws below stay inside these ranges and needn't reach their ends.
Inputs may be any that keep to these rules, and one draw needn't show every extreme that they name: `live_counts`: each replica group's live sequences fill its first slots; some group holds 2 live sequences and some other group only 1.
All inputs are finite; a program needn't handle non-finite values.
Results may differ from the reference program's by a relative error of at most 0.025.
Values may be sent and summed in bfloat16 or wider, within the bound.
A program may use at most 512 MiB of HBM per device.

```python
import jax
import jax.numpy as jnp
from jax import lax

D = 2048
HEADS = 32
KV_HEADS = 4
HEAD = 64
FF = 5632
SEQ_LEN = 1024
SLOTS = 2
SEQS = 8
KV = 256
N_REP = 4


def draw_live_counts(key, part):
    count_key = jax.random.fold_in(key, 11)
    place_key = jax.random.fold_in(key, 23)
    counts = jax.random.randint(count_key, (N_REP,), 1, SLOTS + 1).astype(jnp.int32)
    order = jax.random.permutation(place_key, N_REP)
    counts = jnp.where(order == 0, SLOTS, counts)
    counts = jnp.where(order == 1, 1, counts)
    return counts.astype(jnp.int32)


def steps_of(own_key, dims, split, least, largest):
    def one(dim, parts):
        heights = jax.random.uniform(jax.random.fold_in(jax.random.fold_in(own_key, 6), dim), (parts,), jnp.float32, least / len(split), largest / len(split))
        return jnp.repeat(jnp.exp(heights), dims[dim] // parts).reshape((-1,) + (1,) * (len(dims) - dim - 1))

    level = one(*split[0])
    for cut in split[1:]:
        level = level * one(*cut)
    return level


def centred(own_key, extent, width, bound, split=(), kind=jnp.bfloat16):
    factor_of = steps_of(own_key, extent, split, -0.22, 0.18) if split else 1.0
    entries = jax.random.normal(own_key, extent, jnp.float32) * width * factor_of
    return jnp.minimum(jnp.maximum(entries, -bound), bound).astype(kind)


def setup_inputs(seed: int = 0) -> dict:
    arg_keys = jax.random.split(jax.random.key(seed), 12)
    tokens = centred(arg_keys[0], (SEQS, SEQ_LEN, D), 1.0, 6.0, ((0, 4), (1, 4)))
    cotangent = centred(arg_keys[1], (SEQS, SEQ_LEN, D), 1.0, 6.0, ((0, 4), (1, 4)))
    live_counts = draw_live_counts(jax.random.fold_in(arg_keys[11], 71), 0)
    w_query = centred(arg_keys[3], (2, D, D), D ** -0.5, 0.125, ((0, 2), (1, 4)))
    w_key = centred(arg_keys[4], (2, D, KV), D ** -0.5, 0.125, ((0, 2), (1, 4)))
    w_value = centred(arg_keys[5], (2, D, KV), D ** -0.5, 0.125, ((0, 2), (1, 4)))
    w_out = centred(arg_keys[6], (2, D, D), (D * 8 // SEQ_LEN) ** -0.5, 1.5, ((0, 2), (1, 4)))
    w_gate = centred(arg_keys[7], (2, D, FF), D ** -0.5, 0.125, ((0, 2), (1, 4)))
    w_up = centred(arg_keys[8], (2, D, FF), D ** -0.5, 0.125, ((0, 2), (1, 4)))
    w_down = centred(arg_keys[9], (2, FF, D), FF ** -0.5, 0.078125, ((0, 2), (1, 4)))
    norm_gains = jnp.clip(1.0 + 0.1 * jax.random.normal(arg_keys[10], (2, 2, D), jnp.float32), 0.5, 1.5).astype(jnp.bfloat16)
    return {"tokens": tokens, "cotangent": cotangent, "live_counts": live_counts, "w_query": w_query, "w_key": w_key, "w_value": w_value, "w_out": w_out, "w_gate": w_gate, "w_up": w_up, "w_down": w_down, "norm_gains": norm_gains}


EPSILON = 1e-05
ROPE_BASE = 10000.0
HIGH = lax.Precision.HIGHEST

@jax.custom_vjp
def low(v):
    return lax.optimization_barrier(v.astype(jnp.bfloat16)).astype(jnp.float32)

@jax.custom_vjp
def low_back(v):
    return v

def low_keep(v):
    return (low(v), None)

def low_pass(kept, grad):
    return (grad,)

def back_keep(v):
    return (v, None)

def back_low(kept, grad):
    return (low(grad),)
low.defvjp(low_keep, low_pass)
low_back.defvjp(back_keep, back_low)

def matmul(left_rows, right_cols):
    return jnp.dot(left_rows, right_cols, precision=HIGH, preferred_element_type=jnp.float32)

def angles_for(positions):
    half_dim = HEAD // 2
    inverse = ROPE_BASE ** (-(jnp.arange(half_dim, dtype=jnp.float32) * 2.0 / HEAD))
    angle_grid = positions.astype(jnp.float32)[:, None] * inverse[None, :]
    return (jnp.cos(angle_grid), jnp.sin(angle_grid))

def rotate(matrix, cos_table, sin_table):
    row_count = matrix.shape[0]
    half_dim = HEAD // 2
    pieces = matrix.reshape(row_count, -1, 2, half_dim)
    first_half = pieces[:, :, 0, :]
    second_half = pieces[:, :, 1, :]
    cos_wide = cos_table[:, None, :]
    sin_wide = sin_table[:, None, :]
    rotated = jnp.stack([first_half * cos_wide - second_half * sin_wide, second_half * cos_wide + first_half * sin_wide], axis=2)
    return rotated.reshape(row_count, -1)

def apply_layer(stream, w_q, w_k, w_v, w_o, w_g, w_u, w_d, gain_vals, cos_table, sin_table, causal):
    length = stream.shape[0]
    group_size = HEADS // KV_HEADS
    scale_factor = HEAD ** (-0.5)
    inv_one = lax.rsqrt(lax.optimization_barrier(jnp.mean(stream * stream, axis=-1, keepdims=True)) + EPSILON)
    normed = low(stream * inv_one * gain_vals[0])
    queries = low_back(matmul(normed, w_q))
    key_rows = low_back(matmul(normed, w_k))
    values = low(low_back(matmul(normed, w_v)))
    queries = low(rotate(queries, cos_table, sin_table))
    key_rows = low(rotate(key_rows, cos_table, sin_table))
    query4 = queries.reshape(length, KV_HEADS, group_size, HEAD)
    key_heads = key_rows.reshape(length, KV_HEADS, HEAD)
    value3 = values.reshape(length, KV_HEADS, HEAD)
    scores = low_back(jnp.einsum('qhgd,khd->hgqk', query4, key_heads, precision=HIGH) * scale_factor)
    scores = jnp.where(causal, scores, -1e+30)
    prob_vals = low(jax.nn.softmax(scores, axis=-1))
    attended = jnp.einsum('hgqk,khd->qhgd', prob_vals, value3, precision=HIGH).reshape(length, D)
    attended = low(low_back(attended))
    branch = low_back(matmul(attended, w_o))
    middle = stream + branch
    inv_two = lax.rsqrt(lax.optimization_barrier(jnp.mean(middle * middle, axis=-1, keepdims=True)) + EPSILON)
    normed_two = low(middle * inv_two * gain_vals[1])
    gate_proj = low_back(matmul(normed_two, w_g))
    upward = low_back(matmul(normed_two, w_u))
    hidden = low(jax.nn.silu(gate_proj) * upward)
    return middle + low_back(matmul(hidden, w_d))

def forward(stream_in, extra_in, params, cos_table, sin_table, causal):
    w_q, w_k, w_v, w_o, w_g, w_u, w_d, gain_vals = params
    first_out = apply_layer(stream_in, w_q[0], w_k[0], w_v[0], w_o[0], w_g[0], w_u[0], w_d[0], gain_vals[0], cos_table, sin_table, causal)
    passed = low_back(low(first_out)) + extra_in
    second_out = apply_layer(passed, w_q[1], w_k[1], w_v[1], w_o[1], w_g[1], w_u[1], w_d[1], gain_vals[1], cos_table, sin_table, causal)
    return (low(second_out), passed)

def reference(tokens, cotangent, live_counts, w_query, w_key, w_value, w_out, w_gate, w_up, w_down, norm_gains):
    params = tuple((arg_array.astype(jnp.float32) for arg_array in (w_query, w_key, w_value, w_out, w_gate, w_up, w_down, norm_gains)))
    positions = jnp.arange(SEQ_LEN)
    cos_table, sin_table = angles_for(positions)
    causal = positions[None, :] <= positions[:, None]
    seq_index = jnp.arange(SEQS)
    live_mask = (seq_index % SLOTS < live_counts[seq_index // SLOTS]).astype(jnp.float32)

    def run_forward(stream_in, extra_in, weights_in):
        return forward(stream_in, extra_in, weights_in, cos_table, sin_table, causal)

    def one_sequence(totals, seq_item):
        seq_tokens, seq_cot, alive = seq_item
        stream_in = seq_tokens.astype(jnp.float32) * alive
        extra_in = jnp.zeros((SEQ_LEN, D), jnp.float32)
        outputs, pullback = jax.vjp(run_forward, stream_in, extra_in, params)
        grad_x, grad_mid, grad_params = pullback((seq_cot.astype(jnp.float32) * alive, jnp.zeros_like(extra_in)))
        totals = jax.tree.map(jnp.add, totals, grad_params)
        return (totals, (outputs[1].astype(jnp.bfloat16), outputs[0].astype(jnp.bfloat16), grad_x, grad_mid))
    zero_grads = tuple((jnp.zeros_like(arg_array) for arg_array in params))
    totals, (firsts, seconds, grad_xs, grad_mids) = lax.scan(one_sequence, zero_grads, (tokens, cotangent, live_mask))
    acts = jnp.stack([firsts, seconds])
    grad_in = jnp.stack([grad_xs, grad_mids])
    return (acts, grad_in, totals[0], totals[1], totals[2], totals[3], totals[4], totals[5], totals[6], totals[7])
```

```python
import functools, math
import jax
import jax.numpy as jnp
from jax import lax
from jax.sharding import PartitionSpec as P
from jax.experimental import pallas as pl
from jax.experimental.pallas import tpu as pltpu

HEADS = 32
KV_HEADS = 4
HEAD = 64
LOG2E = math.log2(math.e)
NEG_FILL = -1e30
F32, BF16 = jnp.float32, jnp.bfloat16


def mm(a, b):
    return jnp.dot(a, b, preferred_element_type=F32)


def attn_fwd_kernel(axis, pairs, q_ref, k_ref, v_ref, o_ref, lse_ref, bias_ref):
    keys, queries = bias_ref.shape
    offset = lax.axis_index(axis) * queries

    @pl.when(pl.program_id(0) == 0)
    def _():
        key_pos = lax.broadcasted_iota(jnp.int32, (keys, queries), 0)
        query_pos = lax.broadcasted_iota(jnp.int32, (keys, queries), 1) + offset
        bias_ref[...] = jnp.where(key_pos <= query_pos, 0.0, NEG_FILL)

    for half in range(2):
        key = k_ref[:, half * HEAD:(half + 1) * HEAD]
        value_t = v_ref[...].T[half * HEAD:(half + 1) * HEAD, :]
        for pair in range(pairs):
            col = (half * pairs + pair) * 2 * HEAD
            q_t = q_ref[:, col:col + 2 * HEAD].T
            outs = []
            for sub in range(2):
                head = (half * pairs + pair) * 2 + sub
                scores = mm(key, q_t[sub * HEAD:(sub + 1) * HEAD, :]) * (LOG2E * HEAD ** -0.5) + bias_ref[...]
                top = jnp.max(scores, axis=0, keepdims=True)
                prob = jnp.exp2(scores - top)
                total = jnp.sum(prob, axis=0, keepdims=True)
                outs.append(mm(value_t, prob.astype(BF16)) / total)
                lse_ref[0, head:head + 1, :] = top + jnp.log2(total)
            o_ref[:, col:col + 2 * HEAD] = jnp.concatenate(outs, axis=0).T.astype(BF16)


def attn_fwd(q, k, v, axis):
    queries, width = q.shape
    keys = k.shape[0]
    pairs = HEADS // KV_HEADS // 2
    steps = KV_HEADS // 2
    heads = HEADS // steps
    return pl.pallas_call(
        functools.partial(attn_fwd_kernel, axis, pairs),
        grid=(steps,),
        in_specs=[
            pl.BlockSpec((queries, width // steps), lambda i: (0, i)),
            pl.BlockSpec((keys, 2 * HEAD), lambda i: (0, i)),
            pl.BlockSpec((keys, 2 * HEAD), lambda i: (0, i)),
        ],
        out_specs=[
            pl.BlockSpec((queries, width // steps), lambda i: (0, i)),
            pl.BlockSpec((1, heads, queries), lambda i: (i, 0, 0)),
        ],
        out_shape=[
            jax.ShapeDtypeStruct((queries, width), BF16),
            jax.ShapeDtypeStruct((steps, heads, queries), F32),
        ],
        scratch_shapes=[pltpu.VMEM((keys, queries), F32)],
        compiler_params=pltpu.CompilerParams(vmem_limit_bytes=50 * 1024 * 1024),
        cost_estimate=pl.CostEstimate(
            flops=4 * queries * keys * width, bytes_accessed=4 * queries * width * 2,
            transcendentals=queries * keys * HEADS),
        name="attn_fwd",
    )(q, k, v)


def attn_bwd_kernel(axis, pairs, q_ref, k_ref, v_ref, o_ref, do_ref, lse_ref, dq_ref, dk_ref, dv_ref, bias_ref, dk_acc, dv_acc):
    keys, queries = bias_ref.shape
    offset = lax.axis_index(axis) * queries

    @pl.when(pl.program_id(0) == 0)
    def _():
        key_pos = lax.broadcasted_iota(jnp.int32, (keys, queries), 0)
        query_pos = lax.broadcasted_iota(jnp.int32, (keys, queries), 1) + offset
        bias_ref[...] = jnp.where(key_pos <= query_pos, 0.0, NEG_FILL)

    low_lane = lax.broadcasted_iota(jnp.int32, (queries, 2 * HEAD), 1) < HEAD
    for half in range(2):
        key = k_ref[:, half * HEAD:(half + 1) * HEAD]
        value = v_ref[:, half * HEAD:(half + 1) * HEAD]
        key_t = k_ref[...].T[half * HEAD:(half + 1) * HEAD, :]
        for pair in range(pairs):
            col = (half * pairs + pair) * 2 * HEAD
            q_rows = q_ref[:, col:col + 2 * HEAD]
            do_rows = do_ref[:, col:col + 2 * HEAD]
            q_t = q_rows.T
            do_t = do_rows.T
            delta_t = (o_ref[:, col:col + 2 * HEAD].astype(F32) * do_rows.astype(F32)).T
            dqs = []
            for sub in range(2):
                head = (half * pairs + pair) * 2 + sub
                rows = slice(sub * HEAD, (sub + 1) * HEAD)
                lane = low_lane if sub == 0 else jnp.logical_not(low_lane)
                scores = mm(key, q_t[rows, :]) * (LOG2E * HEAD ** -0.5) + bias_ref[...]
                prob = jnp.exp2(scores - lse_ref[0, head:head + 1, :])
                grad_prob = mm(value, do_t[rows, :])
                delta = jnp.sum(delta_t[rows, :], axis=0, keepdims=True)
                grad_score = (prob * (grad_prob - delta)).astype(BF16)
                prob = prob.astype(BF16)
                dqs.append(mm(key_t, grad_score))
                dk_term = mm(grad_score, jnp.where(lane, q_rows, jnp.zeros_like(q_rows)))
                dv_term = mm(prob, jnp.where(lane, do_rows, jnp.zeros_like(do_rows)))
                if pair == 0 and sub == 0:
                    dk_acc[...] = dk_term
                    dv_acc[...] = dv_term
                else:
                    dk_acc[...] += dk_term
                    dv_acc[...] += dv_term
            dq_ref[:, col:col + 2 * HEAD] = jnp.concatenate(dqs, axis=0).T * HEAD ** -0.5
        dk_sum = (dk_acc[:, :HEAD] + dk_acc[:, HEAD:]) * HEAD ** -0.5
        dv_sum = dv_acc[:, :HEAD] + dv_acc[:, HEAD:]
        dk_ref[:, half * HEAD:(half + 1) * HEAD] = dk_sum.astype(dk_ref.dtype)
        dv_ref[:, half * HEAD:(half + 1) * HEAD] = dv_sum.astype(dv_ref.dtype)


def attn_bwd(q, k, v, o, do, lse, axis):
    queries, width = q.shape
    keys = k.shape[0]
    pairs = HEADS // KV_HEADS // 2
    steps = KV_HEADS // 2
    heads = HEADS // steps
    wide = pl.BlockSpec((queries, width // steps), lambda i: (0, i))
    narrow = pl.BlockSpec((keys, 2 * HEAD), lambda i: (0, i))
    return pl.pallas_call(
        functools.partial(attn_bwd_kernel, axis, pairs),
        grid=(steps,),
        in_specs=[wide, narrow, narrow, wide, wide, pl.BlockSpec((1, heads, queries), lambda i: (i, 0, 0))],
        out_specs=[wide, narrow, narrow],
        out_shape=[
            jax.ShapeDtypeStruct((queries, width), F32),
            jax.ShapeDtypeStruct((keys, k.shape[1]), BF16),
            jax.ShapeDtypeStruct((keys, k.shape[1]), BF16),
        ],
        scratch_shapes=[pltpu.VMEM((keys, queries), F32), pltpu.VMEM((keys, 2 * HEAD), F32), pltpu.VMEM((keys, 2 * HEAD), F32)],
        compiler_params=pltpu.CompilerParams(vmem_limit_bytes=50 * 1024 * 1024),
        cost_estimate=pl.CostEstimate(
            flops=10 * queries * keys * width, bytes_accessed=12 * queries * width,
            transcendentals=queries * keys * HEADS),
        name="attn_bwd",
    )(q, k, v, o, do, lse)


EPSILON = 1e-05
ROPE_BASE = 10000.0


def angles_for(positions):
    half_dim = HEAD // 2
    inverse = ROPE_BASE ** (-(jnp.arange(half_dim, dtype=F32) * 2.0 / HEAD))
    angle_grid = positions.astype(F32)[:, None] * inverse[None, :]
    return (jnp.cos(angle_grid), jnp.sin(angle_grid))


def rotate(matrix, cos_table, sin_table):
    row_count = matrix.shape[0]
    half_dim = HEAD // 2
    pieces = matrix.reshape(row_count, -1, 2, half_dim)
    first_half = pieces[:, :, 0, :]
    second_half = pieces[:, :, 1, :]
    cos_wide = cos_table[:, None, :]
    sin_wide = sin_table[:, None, :]
    rotated = jnp.stack(
        [
            first_half * cos_wide - second_half * sin_wide,
            second_half * cos_wide + first_half * sin_wide,
        ],
        axis=2,
    )
    return rotated.reshape(row_count, -1)


def times_t(left_rows, right_rows):
    return lax.dot_general(left_rows, right_rows, (((1,), (1,)), ((), ())), preferred_element_type=F32)


def inner_rows(left_rows, right_rows):
    return lax.dot_general(left_rows, right_rows, (((0,), (0,)), ((), ())), preferred_element_type=F32)


def norm_back(grad_normed, stream, inv_root, gain_row):
    scaled = grad_normed * gain_row
    cubed = inv_root * inv_root * inv_root
    return inv_root * scaled - stream * cubed * jnp.mean(scaled * stream, axis=-1, keepdims=True)


def passed_along(block, axis, by):
    length = lax.axis_size(axis)
    pairs = [(i, i + by) for i in range(length) if 0 <= i + by < length]
    return lax.ppermute(block, axis, pairs)


def gather_rows(weight):
    parts = lax.axis_size("rep")
    rows = weight.shape[0] // parts
    own = lax.dynamic_slice_in_dim(weight, lax.axis_index("rep") * rows, rows, 0)
    return lax.all_gather(own, ("shard", "rep"), axis=0, tiled=True)


def scatter_rows(term):
    part = lax.psum_scatter(term, ("shard", "rep"), scatter_dimension=0, tiled=True)
    return lax.all_gather(part, "rep", axis=0, tiled=True)


def layer_forward(stream_in, weights, cos_table, sin_table):
    w_q, w_k, w_v, w_o, w_g, w_u, w_d, gains_wide = weights
    span_len, model_width = stream_in.shape
    stream = stream_in.astype(F32)
    inv_one = lax.rsqrt(jnp.mean(stream * stream, axis=-1, keepdims=True) + EPSILON)
    normed = (stream * inv_one * gains_wide[0]).astype(BF16)
    key_rows = rotate(mm(normed, w_k), cos_table, sin_table).astype(BF16)
    values = mm(normed, w_v).astype(BF16)
    kv_width = values.shape[1]
    kv_all = lax.all_gather(jnp.concatenate([key_rows, values], axis=1), "shard", axis=0, tiled=True)
    key_all, value_all = kv_all[:, :kv_width], kv_all[:, kv_width:]
    queries = rotate(mm(normed, w_q), cos_table, sin_table).astype(BF16)
    attended, log_total = attn_fwd(queries, key_all, value_all, "shard")
    middle = stream + mm(attended, w_o)
    inv_two = lax.rsqrt(jnp.mean(middle * middle, axis=-1, keepdims=True) + EPSILON)
    normed_two = (middle * inv_two * gains_wide[1]).astype(BF16)
    gate_proj = mm(normed_two, w_g)
    upward = mm(normed_two, w_u)
    hidden = (jax.nn.silu(gate_proj) * upward).astype(BF16)
    result = (middle + mm(hidden, w_d)).astype(BF16)
    kept = (stream, inv_one, normed, queries, key_all, value_all, log_total, attended, middle, inv_two,
            normed_two, gate_proj, upward, hidden)
    return result, kept


def layer_backward(grad_bf, kept, weights, cos_table, sin_table):
    w_q, w_k, w_v, w_o, w_g, w_u, w_d, gains_wide = weights
    (stream, inv_one, normed, queries, key_all, value_all, log_total, attended, middle, inv_two,
     normed_two, gate_proj, upward, hidden) = kept
    grad_out = grad_bf.astype(F32)
    grad_hidden = times_t(grad_bf, w_d)
    sigmoid_gate = jax.nn.sigmoid(gate_proj)
    grad_gate = (grad_hidden * upward * sigmoid_gate * (1.0 + gate_proj * (1.0 - sigmoid_gate))).astype(BF16)
    grad_up = (grad_hidden * gate_proj * sigmoid_gate).astype(BF16)
    grad_normed_two = times_t(grad_gate, w_g) + times_t(grad_up, w_u)
    grad_middle = grad_out + norm_back(grad_normed_two, middle, inv_two, gains_wide[1])
    gain_two = jnp.sum(grad_normed_two * middle * inv_two, axis=0)
    grad_branch = grad_middle.astype(BF16)
    grad_attended = times_t(grad_branch, w_o).astype(BF16)
    grad_q_rot, grad_k_part, grad_v_part = attn_bwd(
        queries, key_all, value_all, attended, grad_attended, log_total, "shard")
    kv_width = grad_k_part.shape[1]
    kv_sum = lax.psum_scatter(
        jnp.concatenate([grad_k_part, grad_v_part], axis=1), "shard", scatter_dimension=0, tiled=True).astype(F32)
    grad_query = rotate(grad_q_rot, cos_table, -sin_table).astype(BF16)
    grad_key = rotate(kv_sum[:, :kv_width], cos_table, -sin_table).astype(BF16)
    grad_value = kv_sum[:, kv_width:].astype(BF16)
    grad_normed = times_t(grad_query, w_q) + times_t(grad_key, w_k) + times_t(grad_value, w_v)
    grad_stream = grad_middle + norm_back(grad_normed, stream, inv_one, gains_wide[0])
    gain_one = jnp.sum(grad_normed * stream * inv_one, axis=0)
    terms = (grad_query, grad_key, grad_value, grad_branch, grad_gate, grad_up, grad_bf)
    return grad_stream, terms, jnp.stack([gain_one, gain_two])


def body(tokens, cotangent, live_counts, w_query, w_key, w_value, w_out, w_gate, w_up, w_down, norm_gains):
    section = lax.axis_index("section")
    slot_count, span_len, model_width = tokens.shape
    query_pos = lax.axis_index("shard") * span_len + jnp.arange(span_len, dtype=jnp.int32)
    cos_table, sin_table = angles_for(query_pos)
    live_mask = (jnp.arange(slot_count) < live_counts[0]).astype(F32)
    gains_wide = lax.all_gather(norm_gains[0], "shard", axis=1, tiled=True).astype(F32)
    weights = tuple(gather_rows(w[0]) for w in (w_query, w_key, w_value, w_out, w_gate, w_up, w_down))
    weights = weights + (gains_wide,)
    masked_in = (tokens.astype(F32) * live_mask[:, None, None]).astype(BF16)
    masked_cot = (cotangent.astype(F32) * live_mask[:, None, None]).astype(BF16)
    zero_slot = jnp.zeros((span_len, model_width), BF16)
    ticks = slot_count + 1
    results, kept_all = [], []
    received = zero_slot
    for tick in range(ticks):
        slot_in = masked_in[tick] if tick < slot_count else zero_slot
        own_in = jnp.where(section == 0, slot_in, received)
        result, kept = layer_forward(own_in, weights, cos_table, sin_table)
        received = passed_along(result, "section", 1)
        results.append(result)
        kept_all.append(kept)
    first = section == 0
    acts = jnp.stack([jnp.where(first, results[j], results[j + 1]) for j in range(slot_count)])
    received = zero_slot
    streams, term_list, gain_total = [], [], 0.0
    for tick in range(ticks):
        slot_cot = masked_cot[slot_count - 1 - tick] if tick < slot_count else zero_slot
        grad_bf = jnp.where(first, received, slot_cot)
        grad_stream, terms, gain_grad = layer_backward(grad_bf, kept_all[ticks - 1 - tick], weights, cos_table, sin_table)
        received = passed_along(grad_stream.astype(BF16), "section", -1)
        streams.append(grad_stream)
        term_list.append(terms)
        gain_total = gain_total + gain_grad
    grad_in = jnp.stack([
        jnp.where(first, streams[slot_count - j], streams[slot_count - 1 - j]) for j in range(slot_count)])

    def rows_of(pick_kept, pick_term):
        lefts, rights = [], []
        for j in range(slot_count):
            f0, f1 = pick_kept(kept_all[j]), pick_kept(kept_all[j + 1])
            lefts.append(jnp.where(first, f0, f1))
            b0, b1 = pick_term(term_list[ticks - 1 - j]), pick_term(term_list[ticks - 2 - j])
            rights.append(jnp.where(first, b0, b1))
        return jnp.concatenate(lefts, axis=0), jnp.concatenate(rights, axis=0)

    def weight_term(index, pick_term):
        left, right = rows_of(lambda k: k[index], pick_term)
        return inner_rows(left, right).astype(BF16)

    down_sum = scatter_rows(weight_term(13, lambda t: t[6]))
    ff_sum = scatter_rows(weight_term(10, lambda t: jnp.concatenate([t[4], t[5]], axis=1)))
    out_sum = scatter_rows(weight_term(7, lambda t: t[3]))
    qkv_sum = scatter_rows(weight_term(2, lambda t: jnp.concatenate([t[0], t[1], t[2]], axis=1)))
    kv_width = w_key.shape[2]
    ff_width = w_gate.shape[2]
    gain_part = lax.psum_scatter(gain_total, "shard", scatter_dimension=1, tiled=True)
    gain_sum = lax.psum(gain_part, "rep")
    outs = (
        qkv_sum[:, :model_width],
        qkv_sum[:, model_width:model_width + kv_width],
        qkv_sum[:, model_width + kv_width:],
        out_sum,
        ff_sum[:, :ff_width],
        ff_sum[:, ff_width:],
        down_sum,
        gain_sum,
    )
    return (acts[None], grad_in[None]) + tuple(out.astype(F32)[None] for out in outs)


def solution(mesh):
    tall = P("section", "shard", None)
    per_slot = P("section", "rep", "shard", None)
    return jax.shard_map(
        body,
        mesh=mesh,
        in_specs=(P("rep", "shard", None), P("rep", "shard", None), P("rep")) + (tall,) * 7 + (P("section", None, "shard"),),
        out_specs=(per_slot, per_slot) + (tall,) * 7 + (P("section", None, "shard"),),
        check_vma=False,
    )
```

```python
import functools, math
import jax
import jax.numpy as jnp
from jax import lax
from jax.sharding import PartitionSpec as P
from jax.experimental import pallas as pl
from jax.experimental.pallas import tpu as pltpu

HEADS = 32
KV_HEADS = 4
HEAD = 64
LOG2E = math.log2(math.e)
NEG_FILL = -1e30
F32, BF16 = jnp.float32, jnp.bfloat16


def mm(a, b):
    return jnp.dot(a, b, preferred_element_type=F32)


def attn_fwd_kernel(axis, pairs, q_ref, k_ref, v_ref, o_ref, lse_ref, bias_ref):
    keys, queries = bias_ref.shape
    offset = lax.axis_index(axis) * queries

    @pl.when(pl.program_id(0) == 0)
    def _():
        key_pos = lax.broadcasted_iota(jnp.int32, (keys, queries), 0)
        query_pos = lax.broadcasted_iota(jnp.int32, (keys, queries), 1) + offset
        bias_ref[...] = jnp.where(key_pos <= query_pos, 0.0, NEG_FILL)

    for half in range(2):
        key = k_ref[:, half * HEAD:(half + 1) * HEAD]
        value_t = v_ref[...].T[half * HEAD:(half + 1) * HEAD, :]
        for pair in range(pairs):
            col = (half * pairs + pair) * 2 * HEAD
            q_t = q_ref[:, col:col + 2 * HEAD].T
            outs = []
            for sub in range(2):
                head = (half * pairs + pair) * 2 + sub
                scores = mm(key, q_t[sub * HEAD:(sub + 1) * HEAD, :]) * (LOG2E * HEAD ** -0.5) + bias_ref[...]
                top = jnp.max(scores, axis=0, keepdims=True)
                prob = jnp.exp2(scores - top)
                total = jnp.sum(prob, axis=0, keepdims=True)
                outs.append(mm(value_t, prob.astype(BF16)) / total)
                lse_ref[0, head:head + 1, :] = top + jnp.log2(total)
            o_ref[:, col:col + 2 * HEAD] = jnp.concatenate(outs, axis=0).T.astype(BF16)


def attn_fwd(q, k, v, axis):
    queries, width = q.shape
    keys = k.shape[0]
    pairs = HEADS // KV_HEADS // 2
    steps = KV_HEADS // 2
    heads = HEADS // steps
    return pl.pallas_call(
        functools.partial(attn_fwd_kernel, axis, pairs),
        grid=(steps,),
        in_specs=[
            pl.BlockSpec((queries, width // steps), lambda i: (0, i)),
            pl.BlockSpec((keys, 2 * HEAD), lambda i: (0, i)),
            pl.BlockSpec((keys, 2 * HEAD), lambda i: (0, i)),
        ],
        out_specs=[
            pl.BlockSpec((queries, width // steps), lambda i: (0, i)),
            pl.BlockSpec((1, heads, queries), lambda i: (i, 0, 0)),
        ],
        out_shape=[
            jax.ShapeDtypeStruct((queries, width), BF16),
            jax.ShapeDtypeStruct((steps, heads, queries), F32),
        ],
        scratch_shapes=[pltpu.VMEM((keys, queries), F32)],
        compiler_params=pltpu.CompilerParams(vmem_limit_bytes=50 * 1024 * 1024),
        cost_estimate=pl.CostEstimate(
            flops=4 * queries * keys * width, bytes_accessed=4 * queries * width * 2,
            transcendentals=queries * keys * HEADS),
        name="attn_fwd",
    )(q, k, v)


def attn_bwd_kernel(axis, pairs, q_ref, k_ref, v_ref, o_ref, do_ref, lse_ref, dq_ref, dk_ref, dv_ref, bias_ref, dk_acc, dv_acc):
    keys, queries = bias_ref.shape
    offset = lax.axis_index(axis) * queries

    @pl.when(pl.program_id(0) == 0)
    def _():
        key_pos = lax.broadcasted_iota(jnp.int32, (keys, queries), 0)
        query_pos = lax.broadcasted_iota(jnp.int32, (keys, queries), 1) + offset
        bias_ref[...] = jnp.where(key_pos <= query_pos, 0.0, NEG_FILL)

    low_lane = lax.broadcasted_iota(jnp.int32, (queries, 2 * HEAD), 1) < HEAD
    for half in range(2):
        key = k_ref[:, half * HEAD:(half + 1) * HEAD]
        value = v_ref[:, half * HEAD:(half + 1) * HEAD]
        key_t = k_ref[...].T[half * HEAD:(half + 1) * HEAD, :]
        for pair in range(pairs):
            col = (half * pairs + pair) * 2 * HEAD
            q_rows = q_ref[:, col:col + 2 * HEAD]
            do_rows = do_ref[:, col:col + 2 * HEAD]
            q_t = q_rows.T
            do_t = do_rows.T
            delta_t = (o_ref[:, col:col + 2 * HEAD].astype(F32) * do_rows.astype(F32)).T
            dqs = []
            for sub in range(2):
                head = (half * pairs + pair) * 2 + sub
                rows = slice(sub * HEAD, (sub + 1) * HEAD)
                lane = low_lane if sub == 0 else jnp.logical_not(low_lane)
                scores = mm(key, q_t[rows, :]) * (LOG2E * HEAD ** -0.5) + bias_ref[...]
                prob = jnp.exp2(scores - lse_ref[0, head:head + 1, :])
                grad_prob = mm(value, do_t[rows, :])
                delta = jnp.sum(delta_t[rows, :], axis=0, keepdims=True)
                grad_score = (prob * (grad_prob - delta)).astype(BF16)
                prob = prob.astype(BF16)
                dqs.append(mm(key_t, grad_score))
                dk_term = mm(grad_score, jnp.where(lane, q_rows, jnp.zeros_like(q_rows)))
                dv_term = mm(prob, jnp.where(lane, do_rows, jnp.zeros_like(do_rows)))
                if pair == 0 and sub == 0:
                    dk_acc[...] = dk_term
                    dv_acc[...] = dv_term
                else:
                    dk_acc[...] += dk_term
                    dv_acc[...] += dv_term
            dq_ref[:, col:col + 2 * HEAD] = jnp.concatenate(dqs, axis=0).T * HEAD ** -0.5
        dk_sum = (dk_acc[:, :HEAD] + dk_acc[:, HEAD:]) * HEAD ** -0.5
        dv_sum = dv_acc[:, :HEAD] + dv_acc[:, HEAD:]
        dk_ref[:, half * HEAD:(half + 1) * HEAD] = dk_sum.astype(dk_ref.dtype)
        dv_ref[:, half * HEAD:(half + 1) * HEAD] = dv_sum.astype(dv_ref.dtype)


def attn_bwd(q, k, v, o, do, lse, axis):
    queries, width = q.shape
    keys = k.shape[0]
    pairs = HEADS // KV_HEADS // 2
    steps = KV_HEADS // 2
    heads = HEADS // steps
    wide = pl.BlockSpec((queries, width // steps), lambda i: (0, i))
    narrow = pl.BlockSpec((keys, 2 * HEAD), lambda i: (0, i))
    return pl.pallas_call(
        functools.partial(attn_bwd_kernel, axis, pairs),
        grid=(steps,),
        in_specs=[wide, narrow, narrow, wide, wide, pl.BlockSpec((1, heads, queries), lambda i: (i, 0, 0))],
        out_specs=[wide, narrow, narrow],
        out_shape=[
            jax.ShapeDtypeStruct((queries, width), F32),
            jax.ShapeDtypeStruct((keys, k.shape[1]), BF16),
            jax.ShapeDtypeStruct((keys, k.shape[1]), BF16),
        ],
        scratch_shapes=[pltpu.VMEM((keys, queries), F32), pltpu.VMEM((keys, 2 * HEAD), F32), pltpu.VMEM((keys, 2 * HEAD), F32)],
        compiler_params=pltpu.CompilerParams(vmem_limit_bytes=50 * 1024 * 1024),
        cost_estimate=pl.CostEstimate(
            flops=10 * queries * keys * width, bytes_accessed=12 * queries * width,
            transcendentals=queries * keys * HEADS),
        name="attn_bwd",
    )(q, k, v, o, do, lse)


MESH_IDS = pl.DeviceIdType.MESH
DELAY = 3
LANES = 128
BUFS = 26


def remote(src, dst, send_sem, recv_sem, peer):
    return pltpu.make_async_remote_copy(src, dst, send_sem, recv_sem, device_id=peer, device_id_type=MESH_IDS)


def reduce_stages(z_first, blocks, segments, place, a_ref, b_ref, bufs):
    n, me, rep, right, core_peer, y_peer = place
    own_core, own_y = lax.rem(rep, 2), rep // 2
    (send_c, own, land_c, keep, send_y, land_y, send_z, land_z, send_f,
     sc_sem, rc_sem, cr_c, sy_sem, ry_sem, cr_y, sz_sem, rz_sem, ly_sem, sfy_sem, sfc_sem,
     rfy_sem, rfc_sem, sfw_sem, rfw_sem) = bufs
    rows = own.shape[2]
    depth = land_z.shape[1]
    items = b_ref.shape[2] // LANES * blocks
    starts = [first for _, _, first in segments]
    ends = starts[1:] + [items // blocks]

    def spot_of(out, first, r, p):
        width = out.shape[1] // 4
        column = pl.multiple_of(r * width + (p // blocks - first) * LANES, LANES)
        row = pl.multiple_of(lax.rem(p, blocks) * rows, 16)
        return out.at[pl.ds(row, rows), pl.ds(column, LANES)]

    def each_segment(p, fn):
        for (out, _, first), last in zip(segments, ends):
            if len(segments) == 1:
                fn(lambda r, out=out, first=first: spot_of(out, first, r, p))
                continue
            group = p // blocks

            @pl.when(jnp.logical_and(group >= first, group < last))
            def _(out=out, first=first):
                fn(lambda r: spot_of(out, first, r, p))

    def c_copy(a, s):
        return remote(send_c.at[a], land_c.at[s], sc_sem.at[a], rc_sem.at[s], core_peer)

    def y_copy(a, s):
        return remote(send_y.at[a], land_y.at[s], sy_sem.at[a], ry_sem.at[s], y_peer)

    def z_copy(a, s, p):
        b = lax.rem(p, depth)
        return remote(send_z.at[a], land_z.at[s, b], sz_sem.at[a], rz_sem.at[s, b], right)

    def f_local(a, spot):
        return pltpu.make_async_copy(send_f.at[a], spot(rep), ly_sem.at[a])

    def f_y(a, p, spot):
        return remote(send_f.at[a], spot(rep), sfy_sem.at[a], rfy_sem.at[p], y_peer)

    def f_core(a, p, spot):
        return remote(send_f.at[a], spot(rep), sfc_sem.at[a], rfc_sem.at[p], core_peer)

    def f_turn(a, p, spot):
        there = spot(rep + 2 - 4 * own_y)
        return remote(there, there, sfw_sem.at[a], rfw_sem.at[p], core_peer)

    def stage_zero(a, s, p):
        dest = lax.rem(me + 2 * n - 1 - s, n)
        row = pl.multiple_of((dest * blocks + lax.rem(p, blocks)) * rows, 16)
        which = 0
        for (_, index, first) in segments[1:]:
            which = jnp.where(p // blocks >= first, index, which)
        block = a_ref[which, pl.ds(row, rows), :]
        column = pl.ds(pl.multiple_of(p // blocks * LANES, LANES), LANES)
        for y in range(2):
            send_c[a, y] = mm(block, b_ref[2 * y + 1 - own_core, :, column]).astype(BF16)

        @pl.when(p >= 1)
        def _():
            pl.semaphore_wait(cr_c.at[s], 1)
        c_copy(a, s).start()
        for y in range(2):
            own[a, y] = mm(block, b_ref[2 * y + own_core, :, column])

    def credit(sem, s, p, peer):
        @pl.when(p + 1 < items)
        def _():
            pl.semaphore_signal(sem.at[s], inc=1, device_id=peer, device_id_type=MESH_IDS)

    def start_y(a, s, p):
        y_copy(a, s).start()

    def finish(a, p, total):
        send_f[a] = total.astype(BF16)

        def send(spot):
            f_y(a, p, spot).start()
            f_core(a, p, spot).start()
            f_local(a, spot).start()
        each_segment(p, send)

    def stage_one_y(a, s, p):
        c_copy(a, s).wait()
        send_y[a] = (own[a, 1 - own_y] + land_c[s, 1 - own_y].astype(F32)).astype(BF16)

        @pl.when(p >= 1)
        def _():
            pl.semaphore_wait(cr_y.at[s], 1)
        y_copy(a, s).start()
        keep[a] = own[a, own_y] + land_c[s, own_y].astype(F32)
        credit(cr_c, s, p, core_peer)

    def stage_two_y(a, s, p):
        y_copy(a, s).wait()
        keep[a] = keep[a] + land_y[s].astype(F32)
        credit(cr_y, s, p, y_peer)

        @pl.when(s > 0)
        def _():
            z_copy(a, s - 1, p).wait_recv()
            keep[a] = keep[a] + land_z[s - 1, lax.rem(p, depth)].astype(F32)

        @pl.when(s < n - 1)
        def _():
            send_z[a] = keep[a].astype(BF16)
            z_copy(a, s, p).start()

        @pl.when(s == n - 1)
        def _():
            finish(a, p, keep[a])

    def stage_one_z(a, s, p):
        c_copy(a, s).wait()
        for y in range(2):
            own[a, y] = own[a, y] + land_c[s, y].astype(F32)
        credit(cr_c, s, p, core_peer)

        @pl.when(s > 0)
        def _():
            z_copy(a, s - 1, p).wait_recv()
            for y in range(2):
                own[a, y] = own[a, y] + land_z[s - 1, lax.rem(p, depth), y].astype(F32)

        @pl.when(s < n - 1)
        def _():
            send_z[a] = own[a].astype(BF16)
            z_copy(a, s, p).start()

        @pl.when(s == n - 1)
        def _():
            send_y[a] = own[a, 1 - own_y].astype(BF16)

            @pl.when(p >= 1)
            def _():
                pl.semaphore_wait(cr_y.at[0], 1)
            y_copy(a, 0).start()
            keep[a] = own[a, own_y]

    def stage_two_z(a, s, p):
        @pl.when(s < n - 1)
        def _():
            z_copy(a, s, p).wait_send()

        @pl.when(s == n - 1)
        def _():
            y_copy(a, 0).wait()
            finish(a, p, keep[a] + land_y[0].astype(F32))
            credit(cr_y, 0, p, y_peer)

    def stage_three(a, s, p):
        if not z_first:
            @pl.when(s < n - 1)
            def _():
                z_copy(a, s, p).wait_send()

        @pl.when(s == n - 1)
        def _():
            def turn(spot):
                f_local(a, spot).wait()
                f_core(a, p, spot).wait_send()
                f_y(a, p, spot).wait()
                f_turn(a, p, spot).start()
            each_segment(p, turn)

    def stage_four(a, s, p):
        @pl.when(s == n - 1)
        def _():
            def end(spot):
                f_core(a, p, spot).wait_recv()
                f_turn(a, p, spot).wait()
            each_segment(p, end)

    fns = (stage_zero, stage_one_z if z_first else stage_one_y, stage_two_z if z_first else stage_two_y,
           stage_three, stage_four)
    return items, fns


def reduce_kernel(streams, slots, *refs):
    n = lax.axis_size("shard")
    me = lax.axis_index("shard")
    rep = lax.axis_index("rep")
    section = lax.axis_index("section")
    right = {"shard": lax.rem(me + 1, n)}
    left = {"shard": lax.rem(me + n - 1, n)}
    core_peer = {"rep": rep + 1 - 2 * lax.rem(rep, 2)}
    y_peer = {"rep": rep + 2 - 4 * (rep // 2)}
    place = (n, me, rep, right, core_peer, y_peer)

    refs = list(refs)
    lefts = [[refs.pop(0) for _ in stream["lefts"]] for stream in streams]
    rights = [[[[refs.pop(0) for _ in range(slots + 1)] for _ in segment] for segment in stream["rights"]] for stream in streams]
    outs = [[refs.pop(0) for _ in stream["rights"]] for stream in streams]
    per = [[refs.pop(0) for _ in range(BUFS)] for _ in streams]
    load_sem = refs.pop(0)

    barrier = pltpu.get_barrier_semaphore()
    for peer in (left, right, core_peer, y_peer):
        pl.semaphore_signal(barrier, inc=1, device_id=peer, device_id_type=MESH_IDS)

    def load_all(at_section):
        loads = []

        def load(src, dst):
            loads.append(pltpu.make_async_copy(src, dst, load_sem.at[len(loads)]))
            loads[-1].start()
        for left_refs, right_refs, bufs in zip(lefts, rights, per):
            a_ref, b_ref = bufs[0], bufs[1]
            for k, src in enumerate(left_refs):
                load(src, a_ref.at[k])
            base = 0
            for segment in right_refs:
                quarter = sum(ticks[0].shape[1] for ticks in segment) // 4
                for r in range(4):
                    at = 0
                    for ticks in segment:
                        width = ticks[0].shape[1]
                        lo, hi = max(r * quarter, at), min((r + 1) * quarter, at + width)
                        if lo < hi:
                            for j in range(slots):
                                tick = ticks[slots - j if at_section == 0 else slots - 1 - j]
                                span = tick.shape[0]
                                load(tick.at[:, lo - at:hi - at],
                                     b_ref.at[r, j * span:(j + 1) * span, base + lo - r * quarter:base + hi - r * quarter])
                        at += width
                base += quarter
        for copy in loads:
            copy.wait()

    for value in range(2):
        @pl.when(section == value)
        def _(value=value):
            load_all(value)
    pl.semaphore_wait(barrier, 4)

    work, last = [], 0
    for stream, segs, bufs in zip(streams, outs, per):
        items, fns = reduce_stages(
            stream["z_first"], stream["blocks"],
            [(out, index, first) for out, index, first in zip(segs, stream["which"], stream["firsts"])],
            place, bufs[0], bufs[1], bufs[2:])
        pace = stream["pace"]
        total = n * (items + n - 1)
        work.append((pace, items, fns))
        last = max(last, pace * (total + 4 * DELAY))

    def step(i, carry):
        for k in (4, 3, 2, 1, 0):
            for pace, items, fns in work:
                v = i // pace - DELAY * k
                s = lax.rem(v + n * DELAY * 4, n)
                p = (v - s) // n - s
                fine = jnp.logical_and(jnp.logical_and(v >= 0, lax.rem(i, pace) == 0), jnp.logical_and(p >= 0, p < items))

                @pl.when(fine)
                def _(s=s, p=p, v=v, fn=fns[k]):
                    fn(lax.rem(v, DELAY), s, p)
        return carry

    lax.fori_loop(0, last, step, 0)


def reduce_weights(streams, slots, collective_id, name):
    n = lax.axis_size("shard")
    operands, out_shapes, scratch, flops, moved, plans, loads = [], [], [], 0, 0, [], 0
    dma, regular = pltpu.SemaphoreType.DMA, pltpu.SemaphoreType.REGULAR
    for stream in streams:
        operands += stream["lefts"]
    for stream in streams:
        firsts, at = [], 0
        tokens = stream["lefts"][0].shape[1]
        height = stream["lefts"][0].shape[0] // n
        loads += len(stream["lefts"])
        for segment in stream["rights"]:
            width = 0
            for ticks in segment:
                operands += ticks
                width += ticks[0].shape[1]
                loads += 4 * slots
            firsts.append(at)
            at += width // 4 // LANES
            out_shapes.append(jax.ShapeDtypeStruct((height, width), BF16))
            flops += 2 * tokens * height * n * width
            moved += height * width * 4
        z_first, blocks = stream["z_first"], stream["blocks"]
        items = at * blocks
        rows = height // blocks
        pair = (2,) if z_first else ()
        depth = min(items, n + 2)
        tile = (rows, LANES)
        land_y = 1 if z_first else n
        scratch += [
            pltpu.VMEM((len(stream["lefts"]), height * n, tokens), BF16),
            pltpu.VMEM((4, tokens, at * LANES), BF16),
            pltpu.VMEM((DELAY, 2) + tile, BF16),
            pltpu.VMEM((DELAY, 2) + tile, F32),
            pltpu.VMEM((n, 2) + tile, BF16),
            pltpu.VMEM((DELAY,) + tile, F32),
            pltpu.VMEM((DELAY,) + tile, BF16),
            pltpu.VMEM((land_y,) + tile, BF16),
            pltpu.VMEM((DELAY,) + pair + tile, BF16),
            pltpu.VMEM((n - 1, depth) + pair + tile, BF16),
            pltpu.VMEM((DELAY,) + tile, BF16),
            dma((DELAY,)), dma((n,)), regular((n,)),
            dma((DELAY,)), dma((land_y,)), regular((land_y,)),
            dma((DELAY,)), dma((n - 1, depth)),
            dma((DELAY,)), dma((DELAY,)), dma((DELAY,)),
            dma((items,)), dma((items,)), dma((DELAY,)), dma((items,)),
        ]
        plans.append({
            "z_first": z_first, "blocks": blocks, "pace": stream["pace"], "which": tuple(stream["which"]), "firsts": tuple(firsts),
            "lefts": [None] * len(stream["lefts"]), "rights": [[None] * len(segment) for segment in stream["rights"]]})
    scratch.append(dma((loads,)))
    anywhere = pl.BlockSpec(memory_space=pl.ANY)
    return pl.pallas_call(
        functools.partial(reduce_kernel, plans, slots),
        in_specs=[anywhere] * len(operands),
        out_specs=[anywhere] * len(out_shapes),
        out_shape=out_shapes,
        scratch_shapes=scratch,
        compiler_params=pltpu.CompilerParams(
            collective_id=collective_id, has_side_effects=True, vmem_limit_bytes=60 * 1024 * 1024),
        cost_estimate=pl.CostEstimate(flops=flops, bytes_accessed=moved, transcendentals=0),
        name=name,
    )(*operands)


EPSILON = 1e-05
ROPE_BASE = 10000.0


def angles_for(positions):
    half_dim = HEAD // 2
    inverse = ROPE_BASE ** (-(jnp.arange(half_dim, dtype=F32) * 2.0 / HEAD))
    angle_grid = positions.astype(F32)[:, None] * inverse[None, :]
    return (jnp.cos(angle_grid), jnp.sin(angle_grid))


def rotate(matrix, cos_table, sin_table):
    row_count = matrix.shape[0]
    half_dim = HEAD // 2
    pieces = matrix.reshape(row_count, -1, 2, half_dim)
    first_half = pieces[:, :, 0, :]
    second_half = pieces[:, :, 1, :]
    cos_wide = cos_table[:, None, :]
    sin_wide = sin_table[:, None, :]
    rotated = jnp.stack(
        [
            first_half * cos_wide - second_half * sin_wide,
            second_half * cos_wide + first_half * sin_wide,
        ],
        axis=2,
    )
    return rotated.reshape(row_count, -1)


def times_t(left_rows, right_rows):
    return lax.dot_general(left_rows, right_rows, (((1,), (1,)), ((), ())), preferred_element_type=F32)


def inner_rows(left_rows, right_rows):
    return lax.dot_general(left_rows, right_rows, (((0,), (0,)), ((), ())), preferred_element_type=F32)


def norm_back(grad_normed, stream, inv_root, gain_row):
    scaled = grad_normed * gain_row
    cubed = inv_root * inv_root * inv_root
    return inv_root * scaled - stream * cubed * jnp.mean(scaled * stream, axis=-1, keepdims=True)


def passed_along(block, axis, by):
    length = lax.axis_size(axis)
    pairs = [(i, i + by) for i in range(length) if 0 <= i + by < length]
    return lax.ppermute(block, axis, pairs)


def gather_rows(weight):
    parts = lax.axis_size("rep")
    rows = weight.shape[0] // parts
    own = lax.dynamic_slice_in_dim(weight, lax.axis_index("rep") * rows, rows, 0)
    return lax.all_gather(own, ("shard", "rep"), axis=0, tiled=True)


def layer_forward(stream_in, weights, cos_table, sin_table):
    w_q, w_k, w_v, w_o, w_g, w_u, w_d, gains_wide = weights
    span_len, model_width = stream_in.shape
    stream = stream_in.astype(F32)
    inv_one = lax.rsqrt(jnp.mean(stream * stream, axis=-1, keepdims=True) + EPSILON)
    normed = (stream * inv_one * gains_wide[0]).astype(BF16)
    key_rows = rotate(mm(normed, w_k), cos_table, sin_table).astype(BF16)
    values = mm(normed, w_v).astype(BF16)
    kv_width = values.shape[1]
    kv_all = lax.all_gather(jnp.concatenate([key_rows, values], axis=1), "shard", axis=0, tiled=True)
    key_all, value_all = kv_all[:, :kv_width], kv_all[:, kv_width:]
    queries = rotate(mm(normed, w_q), cos_table, sin_table).astype(BF16)
    attended, log_total = attn_fwd(queries, key_all, value_all, "shard")
    middle = stream + mm(attended, w_o)
    inv_two = lax.rsqrt(jnp.mean(middle * middle, axis=-1, keepdims=True) + EPSILON)
    normed_two = (middle * inv_two * gains_wide[1]).astype(BF16)
    gate_proj = mm(normed_two, w_g)
    upward = mm(normed_two, w_u)
    hidden = (jax.nn.silu(gate_proj) * upward).astype(BF16)
    result = (middle + mm(hidden, w_d)).astype(BF16)
    kept = (stream, inv_one, normed, queries, key_all, value_all, log_total, attended, middle, inv_two,
            normed_two, gate_proj, upward, hidden)
    return result, kept


def layer_backward(grad_bf, kept, weights, cos_table, sin_table):
    w_q, w_k, w_v, w_o, w_g, w_u, w_d, gains_wide = weights
    (stream, inv_one, normed, queries, key_all, value_all, log_total, attended, middle, inv_two,
     normed_two, gate_proj, upward, hidden) = kept
    grad_out = grad_bf.astype(F32)
    grad_hidden = times_t(grad_bf, w_d)
    sigmoid_gate = jax.nn.sigmoid(gate_proj)
    grad_gate = (grad_hidden * upward * sigmoid_gate * (1.0 + gate_proj * (1.0 - sigmoid_gate))).astype(BF16)
    grad_up = (grad_hidden * gate_proj * sigmoid_gate).astype(BF16)
    grad_normed_two = times_t(grad_gate, w_g) + times_t(grad_up, w_u)
    grad_middle = grad_out + norm_back(grad_normed_two, middle, inv_two, gains_wide[1])
    gain_two = jnp.sum(grad_normed_two * middle * inv_two, axis=0)
    grad_branch = grad_middle.astype(BF16)
    grad_attended = times_t(grad_branch, w_o).astype(BF16)
    grad_q_rot, grad_k_part, grad_v_part = attn_bwd(
        queries, key_all, value_all, attended, grad_attended, log_total, "shard")
    kv_width = grad_k_part.shape[1]
    kv_sum = lax.psum_scatter(
        jnp.concatenate([grad_k_part, grad_v_part], axis=1), "shard", scatter_dimension=0, tiled=True).astype(F32)
    grad_query = rotate(grad_q_rot, cos_table, -sin_table).astype(BF16)
    grad_key = rotate(kv_sum[:, :kv_width], cos_table, -sin_table).astype(BF16)
    grad_value = kv_sum[:, kv_width:].astype(BF16)
    grad_normed = times_t(grad_query, w_q) + times_t(grad_key, w_k) + times_t(grad_value, w_v)
    grad_stream = grad_middle + norm_back(grad_normed, stream, inv_one, gains_wide[0])
    gain_one = jnp.sum(grad_normed * stream * inv_one, axis=0)
    terms = (grad_query, grad_key, grad_value, grad_branch, grad_gate, grad_up, grad_bf)
    return grad_stream, terms, jnp.stack([gain_one, gain_two])


def body(tokens, cotangent, live_counts, w_query, w_key, w_value, w_out, w_gate, w_up, w_down, norm_gains):
    section = lax.axis_index("section")
    slot_count, span_len, model_width = tokens.shape
    query_pos = lax.axis_index("shard") * span_len + jnp.arange(span_len, dtype=jnp.int32)
    cos_table, sin_table = angles_for(query_pos)
    live_mask = (jnp.arange(slot_count) < live_counts[0]).astype(F32)
    gains_wide = lax.all_gather(norm_gains[0], "shard", axis=1, tiled=True).astype(F32)
    weights = tuple(gather_rows(w[0]) for w in (w_query, w_key, w_value, w_out, w_gate, w_up, w_down))
    weights = weights + (gains_wide,)
    masked_in = (tokens.astype(F32) * live_mask[:, None, None]).astype(BF16)
    masked_cot = (cotangent.astype(F32) * live_mask[:, None, None]).astype(BF16)
    zero_slot = jnp.zeros((span_len, model_width), BF16)
    ticks = slot_count + 1
    results, kept_all = [], []
    received = zero_slot
    for tick in range(ticks):
        slot_in = masked_in[tick] if tick < slot_count else zero_slot
        own_in = jnp.where(section == 0, slot_in, received)
        result, kept = layer_forward(own_in, weights, cos_table, sin_table)
        received = passed_along(result, "section", 1)
        results.append(result)
        kept_all.append(kept)
    first = section == 0
    acts = jnp.stack([jnp.where(first, results[j], results[j + 1]) for j in range(slot_count)])
    received = zero_slot
    streams, term_list, gain_total = [], [], 0.0
    for tick in range(ticks):
        slot_cot = masked_cot[slot_count - 1 - tick] if tick < slot_count else zero_slot
        grad_bf = jnp.where(first, received, slot_cot)
        grad_stream, terms, gain_grad = layer_backward(grad_bf, kept_all[ticks - 1 - tick], weights, cos_table, sin_table)
        received = passed_along(grad_stream.astype(BF16), "section", -1)
        streams.append(grad_stream)
        term_list.append(terms)
        gain_total = gain_total + gain_grad
    grad_in = jnp.stack([
        jnp.where(first, streams[slot_count - j], streams[slot_count - 1 - j]) for j in range(slot_count)])

    def turned(index):
        picks = [jnp.where(first, kept_all[j][index], kept_all[j + 1][index]) for j in range(slot_count)]
        return jnp.concatenate(picks, axis=0).T

    def by_tick(index):
        return [terms[index] for terms in term_list]

    gate_sum, up_sum, qkv_sum, out_sum, down_sum = reduce_weights(
        [
            {"lefts": [turned(10), turned(2), turned(7)], "which": [0, 0, 1, 2], "z_first": False, "blocks": 1, "pace": 1,
             "rights": [[by_tick(4)], [by_tick(5)], [by_tick(0), by_tick(1), by_tick(2)], [by_tick(3)]]},
            {"lefts": [turned(13)], "which": [0], "z_first": True, "blocks": 2, "pace": 3, "rights": [[by_tick(6)]]},
        ],
        slot_count, 1, "reduce_weights")
    kv_width = w_key.shape[2]
    gain_part = lax.psum_scatter(gain_total, "shard", scatter_dimension=1, tiled=True)
    gain_sum = lax.psum(gain_part, "rep")
    outs = (
        qkv_sum[:, :model_width],
        qkv_sum[:, model_width:model_width + kv_width],
        qkv_sum[:, model_width + kv_width:],
        out_sum,
        gate_sum,
        up_sum,
        down_sum,
        gain_sum,
    )
    return (acts[None], grad_in[None]) + tuple(out.astype(F32)[None] for out in outs)


def solution(mesh):
    tall = P("section", "shard", None)
    per_slot = P("section", "rep", "shard", None)
    return jax.shard_map(
        body,
        mesh=mesh,
        in_specs=(P("rep", "shard", None), P("rep", "shard", None), P("rep")) + (tall,) * 7 + (P("section", None, "shard"),),
        out_specs=(per_slot, per_slot) + (tall,) * 7 + (P("section", None, "shard"),),
        check_vma=False,
    )
```

```python
import functools, math
import jax
import jax.numpy as jnp
from jax import lax
from jax.sharding import PartitionSpec as P
from jax.experimental import pallas as pl
from jax.experimental.pallas import tpu as pltpu

HEADS = 32
KV_HEADS = 4
HEAD = 64
LOG2E = math.log2(math.e)
NEG_FILL = -1e30
F32, BF16 = jnp.float32, jnp.bfloat16


def mm(a, b):
    return jnp.dot(a, b, preferred_element_type=F32)


def attn_fwd_kernel(axis, pairs, q_ref, k_ref, v_ref, o_ref, lse_ref, bias_ref):
    keys, queries = bias_ref.shape
    offset = lax.axis_index(axis) * queries

    @pl.when(pl.program_id(0) == 0)
    def _():
        key_pos = lax.broadcasted_iota(jnp.int32, (keys, queries), 0)
        query_pos = lax.broadcasted_iota(jnp.int32, (keys, queries), 1) + offset
        bias_ref[...] = jnp.where(key_pos <= query_pos, 0.0, NEG_FILL)

    for half in range(2):
        key = k_ref[:, half * HEAD:(half + 1) * HEAD]
        value_t = v_ref[...].T[half * HEAD:(half + 1) * HEAD, :]
        for pair in range(pairs):
            col = (half * pairs + pair) * 2 * HEAD
            q_t = q_ref[:, col:col + 2 * HEAD].T
            outs = []
            for sub in range(2):
                head = (half * pairs + pair) * 2 + sub
                scores = mm(key, q_t[sub * HEAD:(sub + 1) * HEAD, :]) * (LOG2E * HEAD ** -0.5) + bias_ref[...]
                top = jnp.max(scores, axis=0, keepdims=True)
                prob = jnp.exp2(scores - top)
                total = jnp.sum(prob, axis=0, keepdims=True)
                outs.append(mm(value_t, prob.astype(BF16)) / total)
                lse_ref[0, head:head + 1, :] = top + jnp.log2(total)
            o_ref[:, col:col + 2 * HEAD] = jnp.concatenate(outs, axis=0).T.astype(BF16)


def attn_fwd(q, k, v, axis):
    queries, width = q.shape
    keys = k.shape[0]
    pairs = HEADS // KV_HEADS // 2
    steps = KV_HEADS // 2
    heads = HEADS // steps
    return pl.pallas_call(
        functools.partial(attn_fwd_kernel, axis, pairs),
        grid=(steps,),
        in_specs=[
            pl.BlockSpec((queries, width // steps), lambda i: (0, i)),
            pl.BlockSpec((keys, 2 * HEAD), lambda i: (0, i)),
            pl.BlockSpec((keys, 2 * HEAD), lambda i: (0, i)),
        ],
        out_specs=[
            pl.BlockSpec((queries, width // steps), lambda i: (0, i)),
            pl.BlockSpec((1, heads, queries), lambda i: (i, 0, 0)),
        ],
        out_shape=[
            jax.ShapeDtypeStruct((queries, width), BF16),
            jax.ShapeDtypeStruct((steps, heads, queries), F32),
        ],
        scratch_shapes=[pltpu.VMEM((keys, queries), F32)],
        compiler_params=pltpu.CompilerParams(vmem_limit_bytes=50 * 1024 * 1024),
        cost_estimate=pl.CostEstimate(
            flops=4 * queries * keys * width, bytes_accessed=4 * queries * width * 2,
            transcendentals=queries * keys * HEADS),
        name="attn_fwd",
    )(q, k, v)


def attn_bwd_kernel(axis, pairs, q_ref, k_ref, v_ref, o_ref, do_ref, lse_ref, dq_ref, dk_ref, dv_ref, bias_ref, dk_acc, dv_acc):
    keys, queries = bias_ref.shape
    offset = lax.axis_index(axis) * queries

    @pl.when(pl.program_id(0) == 0)
    def _():
        key_pos = lax.broadcasted_iota(jnp.int32, (keys, queries), 0)
        query_pos = lax.broadcasted_iota(jnp.int32, (keys, queries), 1) + offset
        bias_ref[...] = jnp.where(key_pos <= query_pos, 0.0, NEG_FILL)

    low_lane = lax.broadcasted_iota(jnp.int32, (queries, 2 * HEAD), 1) < HEAD
    for half in range(2):
        key = k_ref[:, half * HEAD:(half + 1) * HEAD]
        value = v_ref[:, half * HEAD:(half + 1) * HEAD]
        key_t = k_ref[...].T[half * HEAD:(half + 1) * HEAD, :]
        for pair in range(pairs):
            col = (half * pairs + pair) * 2 * HEAD
            q_rows = q_ref[:, col:col + 2 * HEAD]
            do_rows = do_ref[:, col:col + 2 * HEAD]
            q_t = q_rows.T
            do_t = do_rows.T
            delta_t = (o_ref[:, col:col + 2 * HEAD].astype(F32) * do_rows.astype(F32)).T
            dqs = []
            for sub in range(2):
                head = (half * pairs + pair) * 2 + sub
                rows = slice(sub * HEAD, (sub + 1) * HEAD)
                lane = low_lane if sub == 0 else jnp.logical_not(low_lane)
                scores = mm(key, q_t[rows, :]) * (LOG2E * HEAD ** -0.5) + bias_ref[...]
                prob = jnp.exp2(scores - lse_ref[0, head:head + 1, :])
                grad_prob = mm(value, do_t[rows, :])
                delta = jnp.sum(delta_t[rows, :], axis=0, keepdims=True)
                grad_score = (prob * (grad_prob - delta)).astype(BF16)
                prob = prob.astype(BF16)
                dqs.append(mm(key_t, grad_score))
                dk_term = mm(grad_score, jnp.where(lane, q_rows, jnp.zeros_like(q_rows)))
                dv_term = mm(prob, jnp.where(lane, do_rows, jnp.zeros_like(do_rows)))
                if pair == 0 and sub == 0:
                    dk_acc[...] = dk_term
                    dv_acc[...] = dv_term
                else:
                    dk_acc[...] += dk_term
                    dv_acc[...] += dv_term
            dq_ref[:, col:col + 2 * HEAD] = jnp.concatenate(dqs, axis=0).T * HEAD ** -0.5
        dk_sum = (dk_acc[:, :HEAD] + dk_acc[:, HEAD:]) * HEAD ** -0.5
        dv_sum = dv_acc[:, :HEAD] + dv_acc[:, HEAD:]
        dk_ref[:, half * HEAD:(half + 1) * HEAD] = dk_sum.astype(dk_ref.dtype)
        dv_ref[:, half * HEAD:(half + 1) * HEAD] = dv_sum.astype(dv_ref.dtype)


def attn_bwd(q, k, v, o, do, lse, axis):
    queries, width = q.shape
    keys = k.shape[0]
    pairs = HEADS // KV_HEADS // 2
    steps = KV_HEADS // 2
    heads = HEADS // steps
    wide = pl.BlockSpec((queries, width // steps), lambda i: (0, i))
    narrow = pl.BlockSpec((keys, 2 * HEAD), lambda i: (0, i))
    return pl.pallas_call(
        functools.partial(attn_bwd_kernel, axis, pairs),
        grid=(steps,),
        in_specs=[wide, narrow, narrow, wide, wide, pl.BlockSpec((1, heads, queries), lambda i: (i, 0, 0))],
        out_specs=[wide, narrow, narrow],
        out_shape=[
            jax.ShapeDtypeStruct((queries, width), F32),
            jax.ShapeDtypeStruct((keys, k.shape[1]), BF16),
            jax.ShapeDtypeStruct((keys, k.shape[1]), BF16),
        ],
        scratch_shapes=[pltpu.VMEM((keys, queries), F32), pltpu.VMEM((keys, 2 * HEAD), F32), pltpu.VMEM((keys, 2 * HEAD), F32)],
        compiler_params=pltpu.CompilerParams(vmem_limit_bytes=50 * 1024 * 1024),
        cost_estimate=pl.CostEstimate(
            flops=10 * queries * keys * width, bytes_accessed=12 * queries * width,
            transcendentals=queries * keys * HEADS),
        name="attn_bwd",
    )(q, k, v, o, do, lse)


MESH_IDS = pl.DeviceIdType.MESH
DELAY = 3
LANES = 128
BUFS = 26


def remote(src, dst, send_sem, recv_sem, peer):
    return pltpu.make_async_remote_copy(src, dst, send_sem, recv_sem, device_id=peer, device_id_type=MESH_IDS)


def reduce_stages(z_first, blocks, segments, place, a_ref, b_ref, bufs):
    n, me, rep, right, core_peer, y_peer = place
    own_core, own_y = lax.rem(rep, 2), rep // 2
    (send_c, own, land_c, keep, send_y, land_y, send_z, land_z, send_f,
     sc_sem, rc_sem, cr_c, sy_sem, ry_sem, cr_y, sz_sem, rz_sem, ly_sem, sfy_sem, sfc_sem,
     rfy_sem, rfc_sem, sfw_sem, rfw_sem) = bufs
    rows = own.shape[2]
    depth = land_z.shape[1]
    items = b_ref.shape[2] // LANES * blocks
    starts = [first for _, _, first in segments]
    ends = starts[1:] + [items // blocks]

    def spot_of(out, first, r, p):
        width = out.shape[1] // 4
        column = pl.multiple_of(r * width + (p // blocks - first) * LANES, LANES)
        row = pl.multiple_of(lax.rem(p, blocks) * rows, 16)
        return out.at[pl.ds(row, rows), pl.ds(column, LANES)]

    def each_segment(p, fn):
        for (out, _, first), last in zip(segments, ends):
            if len(segments) == 1:
                fn(lambda r, out=out, first=first: spot_of(out, first, r, p))
                continue
            group = p // blocks

            @pl.when(jnp.logical_and(group >= first, group < last))
            def _(out=out, first=first):
                fn(lambda r: spot_of(out, first, r, p))

    def c_copy(a, s):
        return remote(send_c.at[a], land_c.at[s], sc_sem.at[a], rc_sem.at[s], core_peer)

    def y_copy(a, s):
        return remote(send_y.at[a], land_y.at[s], sy_sem.at[a], ry_sem.at[s], y_peer)

    def z_copy(a, s, p):
        b = lax.rem(p, depth)
        return remote(send_z.at[a], land_z.at[s, b], sz_sem.at[a], rz_sem.at[s, b], right)

    def f_local(a, spot):
        return pltpu.make_async_copy(send_f.at[a], spot(rep), ly_sem.at[a])

    def f_y(a, p, spot):
        return remote(send_f.at[a], spot(rep), sfy_sem.at[a], rfy_sem.at[p], y_peer)

    def f_core(a, p, spot):
        return remote(send_f.at[a], spot(rep), sfc_sem.at[a], rfc_sem.at[p], core_peer)

    def f_turn(a, p, spot):
        there = spot(rep + 2 - 4 * own_y)
        return remote(there, there, sfw_sem.at[a], rfw_sem.at[p], core_peer)

    def stage_zero(a, s, p):
        dest = lax.rem(me + 2 * n - 1 - s, n)
        row = pl.multiple_of((dest * blocks + lax.rem(p, blocks)) * rows, 16)
        which = 0
        for (_, index, first) in segments[1:]:
            which = jnp.where(p // blocks >= first, index, which)
        block = a_ref[which, pl.ds(row, rows), :]
        column = pl.ds(pl.multiple_of(p // blocks * LANES, LANES), LANES)
        for y in range(2):
            send_c[a, y] = mm(block, b_ref[2 * y + 1 - own_core, :, column]).astype(BF16)

        @pl.when(p >= 1)
        def _():
            pl.semaphore_wait(cr_c.at[s], 1)
        c_copy(a, s).start()
        for y in range(2):
            own[a, y] = mm(block, b_ref[2 * y + own_core, :, column])

    def credit(sem, s, p, peer):
        @pl.when(p + 1 < items)
        def _():
            pl.semaphore_signal(sem.at[s], inc=1, device_id=peer, device_id_type=MESH_IDS)

    def start_y(a, s, p):
        y_copy(a, s).start()

    def finish(a, p, total):
        send_f[a] = total.astype(BF16)

        def send(spot):
            f_y(a, p, spot).start()
            f_core(a, p, spot).start()
            f_local(a, spot).start()
        each_segment(p, send)

    def stage_one_y(a, s, p):
        c_copy(a, s).wait()
        send_y[a] = (own[a, 1 - own_y] + land_c[s, 1 - own_y].astype(F32)).astype(BF16)

        @pl.when(p >= 1)
        def _():
            pl.semaphore_wait(cr_y.at[s], 1)
        y_copy(a, s).start()
        keep[a] = own[a, own_y] + land_c[s, own_y].astype(F32)
        credit(cr_c, s, p, core_peer)

    def stage_two_y(a, s, p):
        y_copy(a, s).wait()
        keep[a] = keep[a] + land_y[s].astype(F32)
        credit(cr_y, s, p, y_peer)

        @pl.when(s > 0)
        def _():
            z_copy(a, s - 1, p).wait_recv()
            keep[a] = keep[a] + land_z[s - 1, lax.rem(p, depth)].astype(F32)

        @pl.when(s < n - 1)
        def _():
            send_z[a] = keep[a].astype(BF16)
            z_copy(a, s, p).start()

        @pl.when(s == n - 1)
        def _():
            finish(a, p, keep[a])

    def stage_one_z(a, s, p):
        c_copy(a, s).wait()
        for y in range(2):
            own[a, y] = own[a, y] + land_c[s, y].astype(F32)
        credit(cr_c, s, p, core_peer)

        @pl.when(s > 0)
        def _():
            z_copy(a, s - 1, p).wait_recv()
            for y in range(2):
                own[a, y] = own[a, y] + land_z[s - 1, lax.rem(p, depth), y].astype(F32)

        @pl.when(s < n - 1)
        def _():
            send_z[a] = own[a].astype(BF16)
            z_copy(a, s, p).start()

        @pl.when(s == n - 1)
        def _():
            send_y[a] = own[a, 1 - own_y].astype(BF16)

            @pl.when(p >= 1)
            def _():
                pl.semaphore_wait(cr_y.at[0], 1)
            y_copy(a, 0).start()
            keep[a] = own[a, own_y]

    def stage_two_z(a, s, p):
        @pl.when(s < n - 1)
        def _():
            z_copy(a, s, p).wait_send()

        @pl.when(s == n - 1)
        def _():
            y_copy(a, 0).wait()
            finish(a, p, keep[a] + land_y[0].astype(F32))
            credit(cr_y, 0, p, y_peer)

    def stage_three(a, s, p):
        if not z_first:
            @pl.when(s < n - 1)
            def _():
                z_copy(a, s, p).wait_send()

        @pl.when(s == n - 1)
        def _():
            def turn(spot):
                f_local(a, spot).wait()
                f_core(a, p, spot).wait_send()
                f_y(a, p, spot).wait()
                f_turn(a, p, spot).start()
            each_segment(p, turn)

    def stage_four(a, s, p):
        @pl.when(s == n - 1)
        def _():
            def end(spot):
                f_core(a, p, spot).wait_recv()
                f_turn(a, p, spot).wait()
            each_segment(p, end)

    fns = (stage_zero, stage_one_z if z_first else stage_one_y, stage_two_z if z_first else stage_two_y,
           stage_three, stage_four)
    return items, fns


def reduce_kernel(streams, slots, *refs):
    n = lax.axis_size("shard")
    me = lax.axis_index("shard")
    rep = lax.axis_index("rep")
    section = lax.axis_index("section")
    right = {"shard": lax.rem(me + 1, n)}
    left = {"shard": lax.rem(me + n - 1, n)}
    core_peer = {"rep": rep + 1 - 2 * lax.rem(rep, 2)}
    y_peer = {"rep": rep + 2 - 4 * (rep // 2)}
    place = (n, me, rep, right, core_peer, y_peer)

    refs = list(refs)
    lefts = [[refs.pop(0) for _ in stream["lefts"]] for stream in streams]
    rights = [[[[refs.pop(0) for _ in range(slots + 1)] for _ in segment] for segment in stream["rights"]] for stream in streams]
    outs = [[refs.pop(0) for _ in stream["rights"]] for stream in streams]
    per = [[refs.pop(0) for _ in range(BUFS)] for _ in streams]
    load_sem = refs.pop(0)

    barrier = pltpu.get_barrier_semaphore()
    for peer in (left, right, core_peer, y_peer):
        pl.semaphore_signal(barrier, inc=1, device_id=peer, device_id_type=MESH_IDS)

    def load_all(at_section):
        loads = []

        def load(src, dst):
            loads.append(pltpu.make_async_copy(src, dst, load_sem.at[len(loads)]))
            loads[-1].start()
        for left_refs, right_refs, bufs in zip(lefts, rights, per):
            a_ref, b_ref = bufs[0], bufs[1]
            for k, src in enumerate(left_refs):
                load(src, a_ref.at[k])
            base = 0
            for segment in right_refs:
                quarter = sum(ticks[0].shape[1] for ticks in segment) // 4
                for r in range(4):
                    at = 0
                    for ticks in segment:
                        width = ticks[0].shape[1]
                        lo, hi = max(r * quarter, at), min((r + 1) * quarter, at + width)
                        if lo < hi:
                            for j in range(slots):
                                tick = ticks[slots - j if at_section == 0 else slots - 1 - j]
                                span = tick.shape[0]
                                load(tick.at[:, lo - at:hi - at],
                                     b_ref.at[r, j * span:(j + 1) * span, base + lo - r * quarter:base + hi - r * quarter])
                        at += width
                base += quarter
        for copy in loads:
            copy.wait()

    for value in range(2):
        @pl.when(section == value)
        def _(value=value):
            load_all(value)
    pl.semaphore_wait(barrier, 4)

    work, last = [], 0
    for stream, segs, bufs in zip(streams, outs, per):
        items, fns = reduce_stages(
            stream["z_first"], stream["blocks"],
            [(out, index, first) for out, index, first in zip(segs, stream["which"], stream["firsts"])],
            place, bufs[0], bufs[1], bufs[2:])
        pace = stream["pace"]
        total = n * (items + n - 1)
        work.append((pace, items, fns))
        last = max(last, pace * (total + 4 * DELAY))

    def step(i, carry):
        for k in (4, 3, 2, 1, 0):
            for pace, items, fns in work:
                v = i // pace - DELAY * k
                s = lax.rem(v + n * DELAY * 4, n)
                p = (v - s) // n - s
                fine = jnp.logical_and(jnp.logical_and(v >= 0, lax.rem(i, pace) == 0), jnp.logical_and(p >= 0, p < items))

                @pl.when(fine)
                def _(s=s, p=p, v=v, fn=fns[k]):
                    fn(lax.rem(v, DELAY), s, p)
        return carry

    lax.fori_loop(0, last, step, 0)


def reduce_weights(streams, slots, collective_id, name):
    n = lax.axis_size("shard")
    operands, out_shapes, scratch, flops, moved, plans, loads = [], [], [], 0, 0, [], 0
    dma, regular = pltpu.SemaphoreType.DMA, pltpu.SemaphoreType.REGULAR
    for stream in streams:
        operands += stream["lefts"]
    for stream in streams:
        firsts, at = [], 0
        tokens = stream["lefts"][0].shape[1]
        height = stream["lefts"][0].shape[0] // n
        loads += len(stream["lefts"])
        for segment in stream["rights"]:
            width = 0
            for ticks in segment:
                operands += ticks
                width += ticks[0].shape[1]
                loads += 4 * slots
            firsts.append(at)
            at += width // 4 // LANES
            out_shapes.append(jax.ShapeDtypeStruct((height, width), BF16))
            flops += 2 * tokens * height * n * width
            moved += height * width * 4
        z_first, blocks = stream["z_first"], stream["blocks"]
        items = at * blocks
        rows = height // blocks
        pair = (2,) if z_first else ()
        depth = min(items, n + 2)
        tile = (rows, LANES)
        land_y = 1 if z_first else n
        scratch += [
            pltpu.VMEM((len(stream["lefts"]), height * n, tokens), BF16),
            pltpu.VMEM((4, tokens, at * LANES), BF16),
            pltpu.VMEM((DELAY, 2) + tile, BF16),
            pltpu.VMEM((DELAY, 2) + tile, F32),
            pltpu.VMEM((n, 2) + tile, BF16),
            pltpu.VMEM((DELAY,) + tile, F32),
            pltpu.VMEM((DELAY,) + tile, BF16),
            pltpu.VMEM((land_y,) + tile, BF16),
            pltpu.VMEM((DELAY,) + pair + tile, BF16),
            pltpu.VMEM((n - 1, depth) + pair + tile, BF16),
            pltpu.VMEM((DELAY,) + tile, BF16),
            dma((DELAY,)), dma((n,)), regular((n,)),
            dma((DELAY,)), dma((land_y,)), regular((land_y,)),
            dma((DELAY,)), dma((n - 1, depth)),
            dma((DELAY,)), dma((DELAY,)), dma((DELAY,)),
            dma((items,)), dma((items,)), dma((DELAY,)), dma((items,)),
        ]
        plans.append({
            "z_first": z_first, "blocks": blocks, "pace": stream["pace"], "which": tuple(stream["which"]), "firsts": tuple(firsts),
            "lefts": [None] * len(stream["lefts"]), "rights": [[None] * len(segment) for segment in stream["rights"]]})
    scratch.append(dma((loads,)))
    anywhere = pl.BlockSpec(memory_space=pl.ANY)
    return pl.pallas_call(
        functools.partial(reduce_kernel, plans, slots),
        in_specs=[anywhere] * len(operands),
        out_specs=[anywhere] * len(out_shapes),
        out_shape=out_shapes,
        scratch_shapes=scratch,
        compiler_params=pltpu.CompilerParams(
            collective_id=collective_id, has_side_effects=True, vmem_limit_bytes=60 * 1024 * 1024),
        cost_estimate=pl.CostEstimate(flops=flops, bytes_accessed=moved, transcendentals=0),
        name=name,
    )(*operands)


def gather_kernel(splits, *refs):
    n = lax.axis_size("shard")
    me = lax.axis_index("shard")
    rep = lax.axis_index("rep")
    right = {"shard": lax.rem(me + 1, n)}
    left = {"shard": lax.rem(me + n - 1, n)}
    core_peer = {"rep": rep + 1 - 2 * lax.rem(rep, 2)}
    y_rep = rep + 2 - 4 * (rep // 2)
    y_peer = {"rep": y_rep}
    count = len(splits)
    ins, outs = refs[:count], refs[count:2 * count]
    holds = refs[2 * count:3 * count]
    zs, zr, ys, yr, cs, cr, ts, tr, local = refs[3 * count:]

    barrier = pltpu.get_barrier_semaphore()
    for peer in (left, right, core_peer, y_peer):
        pl.semaphore_signal(barrier, inc=1, device_id=peer, device_id_type=MESH_IDS)

    pieces = []
    for k, split in enumerate(splits):
        at = 0
        for width in split:
            pieces.append((k, at, width))
            at += width

    def own_load(k):
        return pltpu.make_async_copy(ins[k], holds[k], local.at[0, k])

    def own_store(k):
        rows = ins[k].shape[0]
        return pltpu.make_async_copy(holds[k], outs[k].at[pl.ds(pl.multiple_of(me * rows, 16), rows), :], local.at[1, k])

    def spot(piece, back, r):
        k, at, width = pieces[piece]
        rows = ins[k].shape[0]
        block = lax.rem(me + n - back, n)
        column = pl.multiple_of(r * (ins[k].shape[1] // 4) + at, LANES)
        return outs[k].at[pl.ds(pl.multiple_of(block * rows, 16), rows), pl.ds(column, width)]

    def z_copy(piece, s):
        k, at, width = pieces[piece]
        there = spot(piece, s, rep)
        column = pl.multiple_of(rep * (ins[k].shape[1] // 4) + at, LANES)
        here = ins[k].at[:, pl.ds(column, width)] if s == 0 else there
        return remote(here, there, zs.at[piece, s], zr.at[piece, s], right)

    def y_copy(piece, s):
        there = spot(piece, s, rep)
        return remote(there, there, ys.at[piece, s - 1], yr.at[piece, s - 1], y_peer)

    def c_copy(piece, s):
        there = spot(piece, s, rep)
        return remote(there, there, cs.at[piece, s - 1], cr.at[piece, s - 1], core_peer)

    def t_copy(piece, s):
        there = spot(piece, s, y_rep)
        return remote(there, there, ts.at[piece, s - 1], tr.at[piece, s - 1], core_peer)

    def turn(piece, s):
        y_copy(piece, s).wait_recv()
        t_copy(piece, s).start()

    pl.semaphore_wait(barrier, 4)
    for piece in range(len(pieces)):
        z_copy(piece, 0).start()
    for k in range(count):
        own_load(k).start()
    for k in range(count):
        own_load(k).wait()
        own_store(k).start()
    before = []
    for s in range(1, n):
        for piece in range(len(pieces)):
            z_copy(piece, s - 1).wait_recv()
            if s < n - 1:
                z_copy(piece, s).start()
            y_copy(piece, s).start()
            c_copy(piece, s).start()
            before.append((piece, s))
            if len(before) > 1:
                turn(*before[-2])
    turn(*before[-1])
    for k in range(count):
        own_store(k).wait()
    for piece, s in before:
        z_copy(piece, s - 1).wait_send()
        y_copy(piece, s).wait_send()
        c_copy(piece, s).wait()
        t_copy(piece, s).wait()


def gather_weights(shards, splits, collective_id, name):
    n = lax.axis_size("shard")
    dma = pltpu.SemaphoreType.DMA
    pieces = sum(len(split) for split in splits)
    pair = dma((pieces, n - 1))
    anywhere = pl.BlockSpec(memory_space=pl.ANY)
    moved = 2 * n * sum(shard.shape[0] * shard.shape[1] for shard in shards)
    return pl.pallas_call(
        functools.partial(gather_kernel, splits),
        in_specs=[anywhere] * len(shards),
        out_specs=[anywhere] * len(shards),
        out_shape=[jax.ShapeDtypeStruct((n * shard.shape[0], shard.shape[1]), BF16) for shard in shards],
        scratch_shapes=[pltpu.VMEM(shard.shape, BF16) for shard in shards] + [pair] * 8 + [dma((2, len(shards)))],
        compiler_params=pltpu.CompilerParams(collective_id=collective_id, has_side_effects=True, vmem_limit_bytes=40 * 1024 * 1024),
        cost_estimate=pl.CostEstimate(flops=0, bytes_accessed=moved * 4, transcendentals=0),
        name=name,
    )(*shards)


def halves(width):
    quarter = width // 4
    first = (quarter // LANES + 1) // 2 * LANES
    return (first, quarter - first) if quarter > first else (quarter,)


EPSILON = 1e-05
ROPE_BASE = 10000.0


def angles_for(positions):
    half_dim = HEAD // 2
    inverse = ROPE_BASE ** (-(jnp.arange(half_dim, dtype=F32) * 2.0 / HEAD))
    angle_grid = positions.astype(F32)[:, None] * inverse[None, :]
    return (jnp.cos(angle_grid), jnp.sin(angle_grid))


def rotate(matrix, cos_table, sin_table):
    row_count = matrix.shape[0]
    half_dim = HEAD // 2
    pieces = matrix.reshape(row_count, -1, 2, half_dim)
    first_half = pieces[:, :, 0, :]
    second_half = pieces[:, :, 1, :]
    cos_wide = cos_table[:, None, :]
    sin_wide = sin_table[:, None, :]
    rotated = jnp.stack(
        [
            first_half * cos_wide - second_half * sin_wide,
            second_half * cos_wide + first_half * sin_wide,
        ],
        axis=2,
    )
    return rotated.reshape(row_count, -1)


def times_t(left_rows, right_rows):
    return lax.dot_general(left_rows, right_rows, (((1,), (1,)), ((), ())), preferred_element_type=F32)


def inner_rows(left_rows, right_rows):
    return lax.dot_general(left_rows, right_rows, (((0,), (0,)), ((), ())), preferred_element_type=F32)


def norm_back(grad_normed, stream, inv_root, gain_row):
    scaled = grad_normed * gain_row
    cubed = inv_root * inv_root * inv_root
    return inv_root * scaled - stream * cubed * jnp.mean(scaled * stream, axis=-1, keepdims=True)


def passed_along(block, axis, by):
    length = lax.axis_size(axis)
    pairs = [(i, i + by) for i in range(length) if 0 <= i + by < length]
    return lax.ppermute(block, axis, pairs)


def gather_rows(weight):
    parts = lax.axis_size("rep")
    rows = weight.shape[0] // parts
    own = lax.dynamic_slice_in_dim(weight, lax.axis_index("rep") * rows, rows, 0)
    return lax.all_gather(own, ("shard", "rep"), axis=0, tiled=True)


def layer_forward(stream_in, weights, cos_table, sin_table):
    w_q, w_kv, w_o, w_g, w_u, w_d, gains_wide = weights
    span_len, model_width = stream_in.shape
    stream = stream_in.astype(F32)
    inv_one = lax.rsqrt(jnp.mean(stream * stream, axis=-1, keepdims=True) + EPSILON)
    normed = (stream * inv_one * gains_wide[0]).astype(BF16)
    kv_rows = mm(normed, w_kv)
    kv_width = kv_rows.shape[1] // 2
    kv_rows = jnp.concatenate(
        [rotate(kv_rows[:, :kv_width], cos_table, sin_table).astype(BF16), kv_rows[:, kv_width:].astype(BF16)], axis=1)
    kv_all = lax.all_gather(kv_rows, "shard", axis=0, tiled=True)
    key_all, value_all = kv_all[:, :kv_width], kv_all[:, kv_width:]
    queries = rotate(mm(normed, w_q), cos_table, sin_table).astype(BF16)
    attended, log_total = attn_fwd(queries, key_all, value_all, "shard")
    middle = stream + mm(attended, w_o)
    inv_two = lax.rsqrt(jnp.mean(middle * middle, axis=-1, keepdims=True) + EPSILON)
    normed_two = (middle * inv_two * gains_wide[1]).astype(BF16)
    gate_proj = mm(normed_two, w_g)
    upward = mm(normed_two, w_u)
    hidden = (jax.nn.silu(gate_proj) * upward).astype(BF16)
    result = (middle + mm(hidden, w_d)).astype(BF16)
    kept = (stream, inv_one, normed, queries, key_all, value_all, log_total, attended, middle, inv_two,
            normed_two, gate_proj, upward, hidden)
    return result, kept


def layer_backward(grad_bf, kept, weights, cos_table, sin_table):
    w_q, w_kv, w_o, w_g, w_u, w_d, gains_wide = weights
    (stream, inv_one, normed, queries, key_all, value_all, log_total, attended, middle, inv_two,
     normed_two, gate_proj, upward, hidden) = kept
    grad_out = grad_bf.astype(F32)
    grad_hidden = times_t(grad_bf, w_d)
    sigmoid_gate = jax.nn.sigmoid(gate_proj)
    grad_gate = (grad_hidden * upward * sigmoid_gate * (1.0 + gate_proj * (1.0 - sigmoid_gate))).astype(BF16)
    grad_up = (grad_hidden * gate_proj * sigmoid_gate).astype(BF16)
    grad_normed_two = times_t(grad_gate, w_g) + times_t(grad_up, w_u)
    grad_middle = grad_out + norm_back(grad_normed_two, middle, inv_two, gains_wide[1])
    gain_two = jnp.sum(grad_normed_two * middle * inv_two, axis=0)
    grad_branch = grad_middle.astype(BF16)
    grad_attended = times_t(grad_branch, w_o).astype(BF16)
    grad_q_rot, grad_k_part, grad_v_part = attn_bwd(
        queries, key_all, value_all, attended, grad_attended, log_total, "shard")
    kv_width = grad_k_part.shape[1]
    kv_sum = lax.psum_scatter(
        jnp.concatenate([grad_k_part, grad_v_part], axis=1), "shard", scatter_dimension=0, tiled=True).astype(F32)
    grad_query = rotate(grad_q_rot, cos_table, -sin_table).astype(BF16)
    grad_key = rotate(kv_sum[:, :kv_width], cos_table, -sin_table).astype(BF16)
    grad_value = kv_sum[:, kv_width:].astype(BF16)
    grad_kv = jnp.concatenate([grad_key, grad_value], axis=1)
    grad_normed = times_t(grad_query, w_q) + times_t(grad_kv, w_kv)
    grad_stream = grad_middle + norm_back(grad_normed, stream, inv_one, gains_wide[0])
    gain_one = jnp.sum(grad_normed * stream * inv_one, axis=0)
    terms = (grad_query, grad_kv, grad_kv, grad_branch, grad_gate, grad_up, grad_bf)
    return grad_stream, terms, jnp.stack([gain_one, gain_two])


def body(tokens, cotangent, live_counts, w_query, w_key, w_value, w_out, w_gate, w_up, w_down, norm_gains):
    section = lax.axis_index("section")
    slot_count, span_len, model_width = tokens.shape
    query_pos = lax.axis_index("shard") * span_len + jnp.arange(span_len, dtype=jnp.int32)
    cos_table, sin_table = angles_for(query_pos)
    live_mask = (jnp.arange(slot_count) < live_counts[0]).astype(F32)
    gain_rows = jnp.pad(norm_gains[0], ((0, 14), (0, -norm_gains.shape[2] % (4 * LANES))))
    shards = [w_query[0], jnp.concatenate([w_key[0], w_value[0]], axis=1), w_out[0], gain_rows, w_gate[0], w_up[0]]
    w_q, w_kv, w_o, gains, w_g, w_u = gather_weights(shards, [halves(shard.shape[1]) for shard in shards], 2, "gather_weights")
    down_shard, w_q = lax.optimization_barrier((w_down[0], w_q))
    w_d = gather_rows(down_shard)
    gain_blocks = gains.reshape(-1, 16, gain_rows.shape[1])[:, :2, :norm_gains.shape[2]]
    gains_wide = gain_blocks.transpose(1, 0, 2).reshape(2, model_width).astype(F32)
    weights = (w_q, w_kv, w_o, w_g, w_u, w_d, gains_wide)
    masked_in = (tokens.astype(F32) * live_mask[:, None, None]).astype(BF16)
    masked_cot = (cotangent.astype(F32) * live_mask[:, None, None]).astype(BF16)
    zero_slot = jnp.zeros((span_len, model_width), BF16)
    ticks = slot_count + 1
    results, kept_all = [], []
    received = zero_slot
    for tick in range(ticks):
        slot_in = masked_in[tick] if tick < slot_count else zero_slot
        own_in = jnp.where(section == 0, slot_in, received)
        result, kept = layer_forward(own_in, weights, cos_table, sin_table)
        received = passed_along(result, "section", 1)
        results.append(result)
        kept_all.append(kept)
    first = section == 0
    acts = jnp.stack([jnp.where(first, results[j], results[j + 1]) for j in range(slot_count)])
    received = zero_slot
    streams, term_list, gain_total = [], [], 0.0
    for tick in range(ticks):
        slot_cot = masked_cot[slot_count - 1 - tick] if tick < slot_count else zero_slot
        grad_bf = jnp.where(first, received, slot_cot)
        grad_stream, terms, gain_grad = layer_backward(grad_bf, kept_all[ticks - 1 - tick], weights, cos_table, sin_table)
        received = passed_along(grad_stream.astype(BF16), "section", -1)
        streams.append(grad_stream)
        term_list.append(terms)
        gain_total = gain_total + gain_grad
    grad_in = jnp.stack([
        jnp.where(first, streams[slot_count - j], streams[slot_count - 1 - j]) for j in range(slot_count)])

    def turned(index):
        picks = [jnp.where(first, kept_all[j][index], kept_all[j + 1][index]) for j in range(slot_count)]
        return jnp.concatenate(picks, axis=0).T

    def by_tick(index):
        return [terms[index] for terms in term_list]

    gate_sum, up_sum, qkv_sum, out_sum, down_sum = reduce_weights(
        [
            {"lefts": [turned(10), turned(2), turned(7)], "which": [0, 0, 1, 2], "z_first": False, "blocks": 1, "pace": 1,
             "rights": [[by_tick(4)], [by_tick(5)], [by_tick(0), by_tick(1)], [by_tick(3)]]},
            {"lefts": [turned(13)], "which": [0], "z_first": True, "blocks": 2, "pace": 3, "rights": [[by_tick(6)]]},
        ],
        slot_count, 1, "reduce_weights")
    kv_width = w_key.shape[2]
    gain_part = lax.psum_scatter(gain_total, "shard", scatter_dimension=1, tiled=True)
    gain_sum = lax.psum(gain_part, "rep")
    outs = (
        qkv_sum[:, :model_width],
        qkv_sum[:, model_width:model_width + kv_width],
        qkv_sum[:, model_width + kv_width:],
        out_sum,
        gate_sum,
        up_sum,
        down_sum,
        gain_sum,
    )
    return (acts[None], grad_in[None]) + tuple(out.astype(F32)[None] for out in outs)


def solution(mesh):
    tall = P("section", "shard", None)
    per_slot = P("section", "rep", "shard", None)
    return jax.shard_map(
        body,
        mesh=mesh,
        in_specs=(P("rep", "shard", None), P("rep", "shard", None), P("rep")) + (tall,) * 7 + (P("section", None, "shard"),),
        out_specs=(per_slot, per_slot) + (tall,) * 7 + (P("section", None, "shard"),),
        check_vma=False,
    )
```

```python
import functools, math
import jax
import jax.numpy as jnp
from jax import lax
from jax.sharding import PartitionSpec as P
from jax.experimental import pallas as pl
from jax.experimental.pallas import tpu as pltpu

HEADS = 32
KV_HEADS = 4
HEAD = 64
LOG2E = math.log2(math.e)
NEG_FILL = -1e30
F32, BF16 = jnp.float32, jnp.bfloat16


def mm(a, b):
    return jnp.dot(a, b, preferred_element_type=F32)


MESH_IDS = pl.DeviceIdType.MESH
DELAY = 3
LANES = 128
BUFS = 26


def remote(src, dst, send_sem, recv_sem, peer):
    return pltpu.make_async_remote_copy(src, dst, send_sem, recv_sem, device_id=peer, device_id_type=MESH_IDS)


def reduce_stages(z_first, blocks, segments, place, a_ref, b_ref, bufs):
    n, me, rep, right, core_peer, y_peer = place
    own_core, own_y = lax.rem(rep, 2), rep // 2
    (send_c, own, land_c, keep, send_y, land_y, send_z, land_z, send_f,
     sc_sem, rc_sem, cr_c, sy_sem, ry_sem, cr_y, sz_sem, rz_sem, ly_sem, sfy_sem, sfc_sem,
     rfy_sem, rfc_sem, sfw_sem, rfw_sem) = bufs
    rows = own.shape[2]
    depth = land_z.shape[1]
    items = b_ref.shape[2] // LANES * blocks
    starts = [first for _, _, first in segments]
    ends = starts[1:] + [items // blocks]

    def spot_of(out, first, r, p):
        width = out.shape[1] // 4
        column = pl.multiple_of(r * width + (p // blocks - first) * LANES, LANES)
        row = pl.multiple_of(lax.rem(p, blocks) * rows, 16)
        return out.at[pl.ds(row, rows), pl.ds(column, LANES)]

    def each_segment(p, fn):
        for (out, _, first), last in zip(segments, ends):
            if len(segments) == 1:
                fn(lambda r, out=out, first=first: spot_of(out, first, r, p))
                continue
            group = p // blocks

            @pl.when(jnp.logical_and(group >= first, group < last))
            def _(out=out, first=first):
                fn(lambda r: spot_of(out, first, r, p))

    def c_copy(a, s):
        return remote(send_c.at[a], land_c.at[s], sc_sem.at[a], rc_sem.at[s], core_peer)

    def y_copy(a, s):
        return remote(send_y.at[a], land_y.at[s], sy_sem.at[a], ry_sem.at[s], y_peer)

    def z_copy(a, s, p):
        b = lax.rem(p, depth)
        return remote(send_z.at[a], land_z.at[s, b], sz_sem.at[a], rz_sem.at[s, b], right)

    def f_local(a, spot):
        return pltpu.make_async_copy(send_f.at[a], spot(rep), ly_sem.at[a])

    def f_y(a, p, spot):
        return remote(send_f.at[a], spot(rep), sfy_sem.at[a], rfy_sem.at[p], y_peer)

    def f_core(a, p, spot):
        return remote(send_f.at[a], spot(rep), sfc_sem.at[a], rfc_sem.at[p], core_peer)

    def f_turn(a, p, spot):
        there = spot(rep + 2 - 4 * own_y)
        return remote(there, there, sfw_sem.at[a], rfw_sem.at[p], core_peer)

    def stage_zero(a, s, p):
        dest = lax.rem(me + 2 * n - 1 - s, n)
        row = pl.multiple_of((dest * blocks + lax.rem(p, blocks)) * rows, 16)
        which = 0
        for (_, index, first) in segments[1:]:
            which = jnp.where(p // blocks >= first, index, which)
        block = a_ref[which, pl.ds(row, rows), :]
        column = pl.ds(pl.multiple_of(p // blocks * LANES, LANES), LANES)
        for y in range(2):
            send_c[a, y] = mm(block, b_ref[2 * y + 1 - own_core, :, column]).astype(BF16)

        @pl.when(p >= 1)
        def _():
            pl.semaphore_wait(cr_c.at[s], 1)
        c_copy(a, s).start()
        for y in range(2):
            own[a, y] = mm(block, b_ref[2 * y + own_core, :, column])

    def credit(sem, s, p, peer):
        @pl.when(p + 1 < items)
        def _():
            pl.semaphore_signal(sem.at[s], inc=1, device_id=peer, device_id_type=MESH_IDS)

    def start_y(a, s, p):
        y_copy(a, s).start()

    def finish(a, p, total):
        send_f[a] = total.astype(BF16)

        def send(spot):
            f_y(a, p, spot).start()
            f_core(a, p, spot).start()
            f_local(a, spot).start()
        each_segment(p, send)

    def stage_one_y(a, s, p):
        c_copy(a, s).wait()
        send_y[a] = (own[a, 1 - own_y] + land_c[s, 1 - own_y].astype(F32)).astype(BF16)

        @pl.when(p >= 1)
        def _():
            pl.semaphore_wait(cr_y.at[s], 1)
        y_copy(a, s).start()
        keep[a] = own[a, own_y] + land_c[s, own_y].astype(F32)
        credit(cr_c, s, p, core_peer)

    def stage_two_y(a, s, p):
        y_copy(a, s).wait()
        keep[a] = keep[a] + land_y[s].astype(F32)
        credit(cr_y, s, p, y_peer)

        @pl.when(s > 0)
        def _():
            z_copy(a, s - 1, p).wait_recv()
            keep[a] = keep[a] + land_z[s - 1, lax.rem(p, depth)].astype(F32)

        @pl.when(s < n - 1)
        def _():
            send_z[a] = keep[a].astype(BF16)
            z_copy(a, s, p).start()

        @pl.when(s == n - 1)
        def _():
            finish(a, p, keep[a])

    def stage_one_z(a, s, p):
        c_copy(a, s).wait()
        for y in range(2):
            own[a, y] = own[a, y] + land_c[s, y].astype(F32)
        credit(cr_c, s, p, core_peer)

        @pl.when(s > 0)
        def _():
            z_copy(a, s - 1, p).wait_recv()
            for y in range(2):
                own[a, y] = own[a, y] + land_z[s - 1, lax.rem(p, depth), y].astype(F32)

        @pl.when(s < n - 1)
        def _():
            send_z[a] = own[a].astype(BF16)
            z_copy(a, s, p).start()

        @pl.when(s == n - 1)
        def _():
            send_y[a] = own[a, 1 - own_y].astype(BF16)

            @pl.when(p >= 1)
            def _():
                pl.semaphore_wait(cr_y.at[0], 1)
            y_copy(a, 0).start()
            keep[a] = own[a, own_y]

    def stage_two_z(a, s, p):
        @pl.when(s < n - 1)
        def _():
            z_copy(a, s, p).wait_send()

        @pl.when(s == n - 1)
        def _():
            y_copy(a, 0).wait()
            finish(a, p, keep[a] + land_y[0].astype(F32))
            credit(cr_y, 0, p, y_peer)

    def stage_three(a, s, p):
        if not z_first:
            @pl.when(s < n - 1)
            def _():
                z_copy(a, s, p).wait_send()

        @pl.when(s == n - 1)
        def _():
            def turn(spot):
                f_local(a, spot).wait()
                f_core(a, p, spot).wait_send()
                f_y(a, p, spot).wait()
                f_turn(a, p, spot).start()
            each_segment(p, turn)

    def stage_four(a, s, p):
        @pl.when(s == n - 1)
        def _():
            def end(spot):
                f_core(a, p, spot).wait_recv()
                f_turn(a, p, spot).wait()
            each_segment(p, end)

    fns = (stage_zero, stage_one_z if z_first else stage_one_y, stage_two_z if z_first else stage_two_y,
           stage_three, stage_four)
    return items, fns


def reduce_kernel(streams, slots, *refs):
    n = lax.axis_size("shard")
    me = lax.axis_index("shard")
    rep = lax.axis_index("rep")
    section = lax.axis_index("section")
    right = {"shard": lax.rem(me + 1, n)}
    left = {"shard": lax.rem(me + n - 1, n)}
    core_peer = {"rep": rep + 1 - 2 * lax.rem(rep, 2)}
    y_peer = {"rep": rep + 2 - 4 * (rep // 2)}
    place = (n, me, rep, right, core_peer, y_peer)

    refs = list(refs)
    lefts = [[refs.pop(0) for _ in stream["lefts"]] for stream in streams]
    rights = [[[[refs.pop(0) for _ in range(slots + 1)] for _ in segment] for segment in stream["rights"]] for stream in streams]
    outs = [[refs.pop(0) for _ in stream["rights"]] for stream in streams]
    per = [[refs.pop(0) for _ in range(BUFS)] for _ in streams]
    load_sem = refs.pop(0)

    barrier = pltpu.get_barrier_semaphore()
    for peer in (left, right, core_peer, y_peer):
        pl.semaphore_signal(barrier, inc=1, device_id=peer, device_id_type=MESH_IDS)

    def load_all(at_section):
        loads = []

        def load(src, dst):
            loads.append(pltpu.make_async_copy(src, dst, load_sem.at[len(loads)]))
            loads[-1].start()
        for left_refs, right_refs, bufs in zip(lefts, rights, per):
            a_ref, b_ref = bufs[0], bufs[1]
            for k, src in enumerate(left_refs):
                load(src, a_ref.at[k])
            base = 0
            for segment in right_refs:
                quarter = sum(ticks[0].shape[1] for ticks in segment) // 4
                for r in range(4):
                    at = 0
                    for ticks in segment:
                        width = ticks[0].shape[1]
                        lo, hi = max(r * quarter, at), min((r + 1) * quarter, at + width)
                        if lo < hi:
                            for j in range(slots):
                                tick = ticks[slots - j if at_section == 0 else slots - 1 - j]
                                span = tick.shape[0]
                                load(tick.at[:, lo - at:hi - at],
                                     b_ref.at[r, j * span:(j + 1) * span, base + lo - r * quarter:base + hi - r * quarter])
                        at += width
                base += quarter
        for copy in loads:
            copy.wait()

    for value in range(2):
        @pl.when(section == value)
        def _(value=value):
            load_all(value)
    pl.semaphore_wait(barrier, 4)

    work, last = [], 0
    for stream, segs, bufs in zip(streams, outs, per):
        items, fns = reduce_stages(
            stream["z_first"], stream["blocks"],
            [(out, index, first) for out, index, first in zip(segs, stream["which"], stream["firsts"])],
            place, bufs[0], bufs[1], bufs[2:])
        pace = stream["pace"]
        total = n * (items + n - 1)
        work.append((pace, items, fns))
        last = max(last, pace * (total + 4 * DELAY))

    def step(i, carry):
        for k in (4, 3, 2, 1, 0):
            for pace, items, fns in work:
                v = i // pace - DELAY * k
                s = lax.rem(v + n * DELAY * 4, n)
                p = (v - s) // n - s
                fine = jnp.logical_and(jnp.logical_and(v >= 0, lax.rem(i, pace) == 0), jnp.logical_and(p >= 0, p < items))

                @pl.when(fine)
                def _(s=s, p=p, v=v, fn=fns[k]):
                    fn(lax.rem(v, DELAY), s, p)
        return carry

    lax.fori_loop(0, last, step, 0)


def reduce_weights(streams, slots, collective_id, name):
    n = lax.axis_size("shard")
    operands, out_shapes, scratch, flops, moved, plans, loads = [], [], [], 0, 0, [], 0
    dma, regular = pltpu.SemaphoreType.DMA, pltpu.SemaphoreType.REGULAR
    for stream in streams:
        operands += stream["lefts"]
    for stream in streams:
        firsts, at = [], 0
        tokens = stream["lefts"][0].shape[1]
        height = stream["lefts"][0].shape[0] // n
        loads += len(stream["lefts"])
        for segment in stream["rights"]:
            width = 0
            for ticks in segment:
                operands += ticks
                width += ticks[0].shape[1]
                loads += 4 * slots
            firsts.append(at)
            at += width // 4 // LANES
            out_shapes.append(jax.ShapeDtypeStruct((height, width), BF16))
            flops += 2 * tokens * height * n * width
            moved += height * width * 4
        z_first, blocks = stream["z_first"], stream["blocks"]
        items = at * blocks
        rows = height // blocks
        pair = (2,) if z_first else ()
        depth = min(items, n + 2)
        tile = (rows, LANES)
        land_y = 1 if z_first else n
        scratch += [
            pltpu.VMEM((len(stream["lefts"]), height * n, tokens), BF16),
            pltpu.VMEM((4, tokens, at * LANES), BF16),
            pltpu.VMEM((DELAY, 2) + tile, BF16),
            pltpu.VMEM((DELAY, 2) + tile, F32),
            pltpu.VMEM((n, 2) + tile, BF16),
            pltpu.VMEM((DELAY,) + tile, F32),
            pltpu.VMEM((DELAY,) + tile, BF16),
            pltpu.VMEM((land_y,) + tile, BF16),
            pltpu.VMEM((DELAY,) + pair + tile, BF16),
            pltpu.VMEM((n - 1, depth) + pair + tile, BF16),
            pltpu.VMEM((DELAY,) + tile, BF16),
            dma((DELAY,)), dma((n,)), regular((n,)),
            dma((DELAY,)), dma((land_y,)), regular((land_y,)),
            dma((DELAY,)), dma((n - 1, depth)),
            dma((DELAY,)), dma((DELAY,)), dma((DELAY,)),
            dma((items,)), dma((items,)), dma((DELAY,)), dma((items,)),
        ]
        plans.append({
            "z_first": z_first, "blocks": blocks, "pace": stream["pace"], "which": tuple(stream["which"]), "firsts": tuple(firsts),
            "lefts": [None] * len(stream["lefts"]), "rights": [[None] * len(segment) for segment in stream["rights"]]})
    scratch.append(dma((loads,)))
    anywhere = pl.BlockSpec(memory_space=pl.ANY)
    return pl.pallas_call(
        functools.partial(reduce_kernel, plans, slots),
        in_specs=[anywhere] * len(operands),
        out_specs=[anywhere] * len(out_shapes),
        out_shape=out_shapes,
        scratch_shapes=scratch,
        compiler_params=pltpu.CompilerParams(
            collective_id=collective_id, has_side_effects=True, vmem_limit_bytes=60 * 1024 * 1024),
        cost_estimate=pl.CostEstimate(flops=flops, bytes_accessed=moved, transcendentals=0),
        name=name,
    )(*operands)


def gather_kernel(splits, *refs):
    n = lax.axis_size("shard")
    me = lax.axis_index("shard")
    rep = lax.axis_index("rep")
    right = {"shard": lax.rem(me + 1, n)}
    left = {"shard": lax.rem(me + n - 1, n)}
    core_peer = {"rep": rep + 1 - 2 * lax.rem(rep, 2)}
    y_rep = rep + 2 - 4 * (rep // 2)
    y_peer = {"rep": y_rep}
    count = len(splits)
    ins, outs = refs[:count], refs[count:2 * count]
    holds = refs[2 * count:3 * count]
    zs, zr, ys, yr, cs, cr, ts, tr, local = refs[3 * count:]

    barrier = pltpu.get_barrier_semaphore()
    for peer in (left, right, core_peer, y_peer):
        pl.semaphore_signal(barrier, inc=1, device_id=peer, device_id_type=MESH_IDS)

    pieces = []
    for k, split in enumerate(splits):
        at = 0
        for width in split:
            pieces.append((k, at, width))
            at += width

    def own_load(k):
        return pltpu.make_async_copy(ins[k], holds[k], local.at[0, k])

    def own_store(k):
        rows = ins[k].shape[0]
        return pltpu.make_async_copy(holds[k], outs[k].at[pl.ds(pl.multiple_of(me * rows, 16), rows), :], local.at[1, k])

    def spot(piece, back, r):
        k, at, width = pieces[piece]
        rows = ins[k].shape[0]
        block = lax.rem(me + n - back, n)
        column = pl.multiple_of(r * (ins[k].shape[1] // 4) + at, LANES)
        return outs[k].at[pl.ds(pl.multiple_of(block * rows, 16), rows), pl.ds(column, width)]

    def z_copy(piece, s):
        k, at, width = pieces[piece]
        there = spot(piece, s, rep)
        column = pl.multiple_of(rep * (ins[k].shape[1] // 4) + at, LANES)
        here = ins[k].at[:, pl.ds(column, width)] if s == 0 else there
        return remote(here, there, zs.at[piece, s], zr.at[piece, s], right)

    def y_copy(piece, s):
        there = spot(piece, s, rep)
        return remote(there, there, ys.at[piece, s - 1], yr.at[piece, s - 1], y_peer)

    def c_copy(piece, s):
        there = spot(piece, s, rep)
        return remote(there, there, cs.at[piece, s - 1], cr.at[piece, s - 1], core_peer)

    def t_copy(piece, s):
        there = spot(piece, s, y_rep)
        return remote(there, there, ts.at[piece, s - 1], tr.at[piece, s - 1], core_peer)

    def turn(piece, s):
        y_copy(piece, s).wait_recv()
        t_copy(piece, s).start()

    pl.semaphore_wait(barrier, 4)
    for piece in range(len(pieces)):
        z_copy(piece, 0).start()
    for k in range(count):
        own_load(k).start()
    for k in range(count):
        own_load(k).wait()
        own_store(k).start()
    before = []
    for s in range(1, n):
        for piece in range(len(pieces)):
            z_copy(piece, s - 1).wait_recv()
            if s < n - 1:
                z_copy(piece, s).start()
            y_copy(piece, s).start()
            c_copy(piece, s).start()
            before.append((piece, s))
            if len(before) > 1:
                turn(*before[-2])
    turn(*before[-1])
    for k in range(count):
        own_store(k).wait()
    for piece, s in before:
        z_copy(piece, s - 1).wait_send()
        y_copy(piece, s).wait_send()
        c_copy(piece, s).wait()
        t_copy(piece, s).wait()


def gather_weights(shards, splits, collective_id, name):
    n = lax.axis_size("shard")
    dma = pltpu.SemaphoreType.DMA
    pieces = sum(len(split) for split in splits)
    pair = dma((pieces, n - 1))
    anywhere = pl.BlockSpec(memory_space=pl.ANY)
    moved = 2 * n * sum(shard.shape[0] * shard.shape[1] for shard in shards)
    return pl.pallas_call(
        functools.partial(gather_kernel, splits),
        in_specs=[anywhere] * len(shards),
        out_specs=[anywhere] * len(shards),
        out_shape=[jax.ShapeDtypeStruct((n * shard.shape[0], shard.shape[1]), BF16) for shard in shards],
        scratch_shapes=[pltpu.VMEM(shard.shape, BF16) for shard in shards] + [pair] * 8 + [dma((2, len(shards)))],
        compiler_params=pltpu.CompilerParams(collective_id=collective_id, has_side_effects=True, vmem_limit_bytes=40 * 1024 * 1024),
        cost_estimate=pl.CostEstimate(flops=0, bytes_accessed=moved * 4, transcendentals=0),
        name=name,
    )(*shards)


def halves(width):
    quarter = width // 4
    first = (quarter // LANES + 1) // 2 * LANES
    return (first, quarter - first) if quarter > first else (quarter,)


EPSILON = 1e-05
FF_TILE = 512


def mm_t(a, b):
    return lax.dot_general(a, b, (((1,), (1,)), ((), ())), preferred_element_type=F32)


def inv_root_of(rows):
    return lax.rsqrt(jnp.mean(rows * rows, axis=-1, keepdims=True) + EPSILON)


def ffn_fwd_kernel(mid_ref, gain_ref, w_g, w_u, w_d, out_ref, normed_ref, hidden_ref, gate_fac, up_fac, acc):
    step = pl.program_id(0)

    @pl.when(step == 0)
    def _():
        mid = mid_ref[...]
        normed_ref[...] = (mid * inv_root_of(mid) * gain_ref[...]).astype(BF16)
        acc[...] = mid

    gate = mm(normed_ref[...], w_g[...])
    up = mm(normed_ref[...], w_u[...])
    sig = jax.nn.sigmoid(gate)
    act = gate * sig
    hidden = (act * up).astype(BF16)
    hidden_ref[...] = hidden
    up_fac[...] = act.astype(BF16)
    gate_fac[...] = (up * sig * (1.0 + gate * (1.0 - sig))).astype(BF16)
    acc[...] += mm(hidden, w_d[...])

    @pl.when(step == pl.num_programs(0) - 1)
    def _():
        out_ref[...] = acc[...].astype(BF16)


def ffn_fwd(middle, gain, w_g, w_u, w_d):
    rows, width = middle.shape
    ff = w_g.shape[1]
    whole = pl.BlockSpec((rows, width), lambda i: (0, 0))
    part = pl.BlockSpec((rows, FF_TILE), lambda i: (0, i))
    tall = pl.BlockSpec((width, FF_TILE), lambda i: (0, i))
    wide = jax.ShapeDtypeStruct((rows, ff), BF16)
    return pl.pallas_call(
        ffn_fwd_kernel,
        grid=(ff // FF_TILE,),
        in_specs=[whole, pl.BlockSpec((1, width), lambda i: (0, 0)), tall, tall, pl.BlockSpec((FF_TILE, width), lambda i: (i, 0))],
        out_specs=[whole, whole, part, part, part],
        out_shape=[jax.ShapeDtypeStruct((rows, width), BF16)] * 2 + [wide] * 3,
        scratch_shapes=[pltpu.VMEM((rows, width), F32)],
        compiler_params=pltpu.CompilerParams(vmem_limit_bytes=58 * 1024 * 1024),
        cost_estimate=pl.CostEstimate(flops=6 * rows * width * ff, bytes_accessed=6 * width * ff, transcendentals=rows * ff),
        name="ffn_fwd",
    )(middle, gain, w_g, w_u, w_d)


def ffn_bwd_kernel(grad_ref, mid_ref, gain_ref, gate_fac, up_fac, w_g, w_u, w_d,
                   dgate_ref, dup_ref, dmid_ref, da_ref, dgain_ref, acc):
    step = pl.program_id(0)
    dhidden = mm_t(grad_ref[...], w_d[...])
    dgate = (dhidden * gate_fac[...].astype(F32)).astype(BF16)
    dup = (dhidden * up_fac[...].astype(F32)).astype(BF16)
    dgate_ref[...] = dgate
    dup_ref[...] = dup
    term = mm_t(dgate, w_g[...]) + mm_t(dup, w_u[...])

    @pl.when(step == 0)
    def _():
        acc[...] = term

    @pl.when(step > 0)
    def _():
        acc[...] += term

    @pl.when(step == pl.num_programs(0) - 1)
    def _():
        mid = mid_ref[...]
        root = inv_root_of(mid)
        dnormed = acc[...]
        scaled = dnormed * gain_ref[...]
        dmid = grad_ref[...].astype(F32) + root * scaled - mid * (root * root * root * jnp.mean(scaled * mid, axis=-1, keepdims=True))
        dmid_ref[...] = dmid
        da_ref[...] = dmid.astype(BF16)
        dgain_ref[...] = jnp.sum(dnormed * mid * root, axis=0, keepdims=True)


def ffn_bwd(grad, middle, gain, gate_fac, up_fac, w_g, w_u, w_d):
    rows, width = middle.shape
    ff = w_g.shape[1]
    whole = pl.BlockSpec((rows, width), lambda i: (0, 0))
    flat = pl.BlockSpec((1, width), lambda i: (0, 0))
    part = pl.BlockSpec((rows, FF_TILE), lambda i: (0, i))
    tall = pl.BlockSpec((width, FF_TILE), lambda i: (0, i))
    wide = jax.ShapeDtypeStruct((rows, ff), BF16)
    return pl.pallas_call(
        ffn_bwd_kernel,
        grid=(ff // FF_TILE,),
        in_specs=[whole, whole, flat, part, part, tall, tall, pl.BlockSpec((FF_TILE, width), lambda i: (i, 0))],
        out_specs=[part, part, whole, whole, flat],
        out_shape=[wide, wide, jax.ShapeDtypeStruct((rows, width), F32), jax.ShapeDtypeStruct((rows, width), BF16),
                   jax.ShapeDtypeStruct((1, width), F32)],
        scratch_shapes=[pltpu.VMEM((rows, width), F32)],
        compiler_params=pltpu.CompilerParams(vmem_limit_bytes=58 * 1024 * 1024),
        cost_estimate=pl.CostEstimate(flops=6 * rows * width * ff, bytes_accessed=6 * width * ff, transcendentals=0),
        name="ffn_bwd",
    )(grad, middle, gain, gate_fac, up_fac, w_g, w_u, w_d)


def rotated(rows, cos_ref, sin_ref):
    width = rows.shape[1]
    low_half = lax.rem(lax.broadcasted_iota(jnp.int32, rows.shape, 1), HEAD) < HEAD // 2
    swapped = jnp.where(low_half, pltpu.roll(rows, width - HEAD // 2, 1), pltpu.roll(rows, HEAD // 2, 1))
    reps = width // LANES
    return rows * jnp.tile(cos_ref[...], (1, reps)) + swapped * jnp.tile(sin_ref[...], (1, reps))


def attend_block_kernel(x_ref, gain_ref, cos_ref, sin_ref, w_q, w_kv, w_o,
                        normed_ref, q_ref, kv_ref, attended_ref, lse_ref, mid_ref,
                        wq_ref, wkv_ref, wo_ref, q_turn, acc, top_ref, total_ref, land,
                        load_sem, send_sem, recv_sem):
    n = lax.axis_size("shard")
    me = lax.axis_index("shard")
    rows, width = x_ref.shape
    kv_width = wkv_ref.shape[1] // 2
    group = HEADS // KV_HEADS
    scale = LOG2E * HEAD ** -0.5
    barrier = pltpu.get_barrier_semaphore()
    for d in range(1, n):
        @pl.when(me >= d)
        def _(d=d):
            pl.semaphore_signal(barrier, inc=1, device_id={"shard": me - d}, device_id_type=MESH_IDS)
    loads = [pltpu.make_async_copy(src, dst, load_sem.at[k])
             for k, (src, dst) in enumerate(((w_kv, wkv_ref), (w_q, wq_ref), (w_o, wo_ref)))]
    for load in loads:
        load.start()

    def to_later(d):
        return remote(land.at[0], land.at[d], send_sem.at[d - 1], recv_sem.at[d - 1], {"shard": me + d})

    def from_earlier(d):
        return remote(land.at[0], land.at[d], send_sem.at[d - 1], recv_sem.at[d - 1], {"shard": me - d})

    x = x_ref[...].astype(F32)
    normed_ref[...] = (x * inv_root_of(x) * gain_ref[...]).astype(BF16)
    loads[0].wait()
    kv = mm(normed_ref[...], wkv_ref[...])
    land[0, :, :kv_width] = rotated(kv[:, :kv_width], cos_ref, sin_ref).astype(BF16)
    land[0, :, kv_width:] = kv[:, kv_width:].astype(BF16)
    @pl.when(me < n - 1)
    def _():
        pl.semaphore_wait(barrier, n - 1 - me)

    for d in range(1, n):
        @pl.when(me + d < n)
        def _(d=d):
            to_later(d).start()
    loads[1].wait()
    chunk = 4 * LANES
    for at in range(0, width, chunk):
        q_chunk = rotated(mm(normed_ref[...], wq_ref[:, at:at + chunk]), cos_ref, sin_ref).astype(BF16)
        q_ref[:, at:at + chunk] = q_chunk
        q_turn[at:at + chunk, :] = q_chunk.T

    def heads_of(d):
        for h in range(KV_HEADS):
            key = land[d, :, h * HEAD:(h + 1) * HEAD]
            pair_t = land[d, :, kv_width + h // 2 * LANES:kv_width + (h // 2 + 1) * LANES].T
            value_t = pair_t[h % 2 * HEAD:(h % 2 + 1) * HEAD, :]
            for j in range(h * group, (h + 1) * group):
                yield j, key, value_t

    key_pos = lax.broadcasted_iota(jnp.int32, (rows, rows), 0)
    query_pos = lax.broadcasted_iota(jnp.int32, (rows, rows), 1)
    bias = jnp.where(key_pos <= query_pos, 0.0, NEG_FILL)
    for j, key, value_t in heads_of(0):
        span = slice(j * HEAD, (j + 1) * HEAD)
        scores = mm(key, q_turn[span, :]) * scale + bias
        top = jnp.max(scores, axis=0, keepdims=True)
        prob = jnp.exp2(scores - top)
        top_ref[j:j + 1, :] = top
        total_ref[j:j + 1, :] = jnp.sum(prob, axis=0, keepdims=True)
        acc[span, :] = mm(value_t, prob.astype(BF16))

    def earlier(d, carry):
        from_earlier(d).wait_recv()
        for j, key, value_t in heads_of(d):
            span = slice(j * HEAD, (j + 1) * HEAD)
            scores = mm(key, q_turn[span, :]) * scale
            old = top_ref[j:j + 1, :]
            top = jnp.maximum(old, jnp.max(scores, axis=0, keepdims=True))
            fade = jnp.exp2(old - top)
            prob = jnp.exp2(scores - top)
            top_ref[j:j + 1, :] = top
            total_ref[j:j + 1, :] = total_ref[j:j + 1, :] * fade + jnp.sum(prob, axis=0, keepdims=True)
            acc[span, :] = acc[span, :] * fade + mm(value_t, prob.astype(BF16))
        return carry

    lax.fori_loop(1, me + 1, earlier, 0)
    total = total_ref[...]
    lse_ref[...] = top_ref[...] + jnp.log2(total)
    total_ref[...] = 1.0 / total
    for pair in range(HEADS // 2):
        col = pair * LANES
        halves_t = [acc[col + k * HEAD:col + (k + 1) * HEAD, :] * total_ref[2 * pair + k:2 * pair + k + 1, :] for k in range(2)]
        attended_ref[:, col:col + LANES] = jnp.concatenate(halves_t, axis=0).T.astype(BF16)
    for d in range(n):
        @pl.when(me >= d)
        def _(d=d):
            kv_ref[d] = land[d]
    loads[2].wait()
    for at in range(0, width, chunk):
        mid_ref[:, at:at + chunk] = x_ref[:, at:at + chunk].astype(F32) + mm(attended_ref[...], wo_ref[:, at:at + chunk])
    for d in range(1, n):
        @pl.when(me + d < n)
        def _(d=d):
            to_later(d).wait_send()


def attend_block(x, gain, cos_table, sin_table, w_q, w_kv, w_o, collective_id):
    n = lax.axis_size("shard")
    rows, width = x.shape
    kv_both = w_kv.shape[1]
    vmem = pl.BlockSpec(memory_space=pltpu.VMEM)
    anywhere = pl.BlockSpec(memory_space=pl.ANY)
    dma = pltpu.SemaphoreType.DMA
    flops = 2 * rows * width * (2 * width + kv_both) + 4 * rows * rows * n * width
    return pl.pallas_call(
        attend_block_kernel,
        in_specs=[vmem] * 4 + [anywhere] * 3,
        out_specs=[vmem] * 6,
        out_shape=[
            jax.ShapeDtypeStruct((rows, width), BF16),
            jax.ShapeDtypeStruct((rows, width), BF16),
            jax.ShapeDtypeStruct((n, rows, kv_both), BF16),
            jax.ShapeDtypeStruct((rows, width), BF16),
            jax.ShapeDtypeStruct((HEADS, rows), F32),
            jax.ShapeDtypeStruct((rows, width), F32),
        ],
        scratch_shapes=[
            pltpu.VMEM(w_q.shape, BF16), pltpu.VMEM(w_kv.shape, BF16), pltpu.VMEM(w_o.shape, BF16),
            pltpu.VMEM((width, rows), BF16), pltpu.VMEM((width, rows), F32),
            pltpu.VMEM((HEADS, rows), F32), pltpu.VMEM((HEADS, rows), F32),
            pltpu.VMEM((n, rows, kv_both), BF16),
            dma((3,)), dma((n - 1,)), dma((n - 1,)),
        ],
        compiler_params=pltpu.CompilerParams(
            collective_id=collective_id, has_side_effects=True, vmem_limit_bytes=56 * 1024 * 1024),
        cost_estimate=pl.CostEstimate(flops=flops, bytes_accessed=2 * width * (2 * width + kv_both), transcendentals=rows * rows * n * HEADS),
        name="attend_block",
    )(x, gain, cos_table, sin_table, w_q, w_kv, w_o)


def attend_back_kernel(da_ref, dmid_ref, x_ref, gain_ref, cos_ref, sin_ref, q_ref, kv_ref, attended_ref, lse_ref, w_q, w_kv, w_o,
                       dq_ref, dkv_ref, grad_ref, grad_low_ref, dgain_ref,
                       wq_ref, wkv_ref, wo_ref, do_ref, q_turn, do_turn, delta_ref, dq_acc, dkv_acc, dn_ref, send_kv, land_kv,
                       load_sem, send_sem, recv_sem):
    n = lax.axis_size("shard")
    me = lax.axis_index("shard")
    rows, width = x_ref.shape
    kv_width = wkv_ref.shape[1] // 2
    pairs = HEADS // KV_HEADS // 2
    scale = LOG2E * HEAD ** -0.5
    barrier = pltpu.get_barrier_semaphore()
    for d in range(1, n):
        @pl.when(me + d < n)
        def _(d=d):
            pl.semaphore_signal(barrier, inc=1, device_id={"shard": me + d}, device_id_type=MESH_IDS)
    loads = [pltpu.make_async_copy(src, dst, load_sem.at[k])
             for k, (src, dst) in enumerate(((w_o, wo_ref), (w_q, wq_ref), (w_kv, wkv_ref)))]
    for load in loads:
        load.start()

    def to_earlier(d):
        return remote(send_kv.at[d - 1], land_kv.at[d - 1], send_sem.at[d - 1], recv_sem.at[d - 1], {"shard": me - d})

    def from_later(d):
        return remote(send_kv.at[d - 1], land_kv.at[d - 1], send_sem.at[d - 1], recv_sem.at[d - 1], {"shard": me + d})

    chunk = 4 * LANES
    for at in range(0, width, LANES):
        q_turn[at:at + LANES, :] = q_ref[:, at:at + LANES].T
    loads[0].wait()
    for at in range(0, width, chunk):
        do_chunk = mm_t(da_ref[...], wo_ref[at:at + chunk, :]).astype(BF16)
        do_ref[:, at:at + chunk] = do_chunk
        do_turn[at:at + chunk, :] = do_chunk.T
    for pair in range(HEADS // 2):
        cols = slice(pair * LANES, (pair + 1) * LANES)
        both = (attended_ref[:, cols].astype(F32) * do_ref[:, cols].astype(F32)).T
        for k in range(2):
            delta_ref[2 * pair + k:2 * pair + k + 1, :] = jnp.sum(both[k * HEAD:(k + 1) * HEAD, :], axis=0, keepdims=True)
    dq_acc[...] = jnp.zeros_like(dq_acc)
    low_lane = lax.broadcasted_iota(jnp.int32, (rows, LANES), 1) < HEAD
    zero_rows = jnp.zeros((rows, LANES), BF16)

    def block(d, bias):
        for h in range(KV_HEADS):
            own = slice(h * HEAD, (h + 1) * HEAD)
            key = kv_ref[d, :, own]
            value = kv_ref[d, :, kv_width + h * HEAD:kv_width + (h + 1) * HEAD]
            key_t = kv_ref[d, :, h // 2 * LANES:(h // 2 + 1) * LANES].T[h % 2 * HEAD:(h % 2 + 1) * HEAD, :]
            dk = jnp.zeros((rows, LANES), F32)
            dv = jnp.zeros((rows, LANES), F32)
            for pair in range(h * pairs, (h + 1) * pairs):
                cols = slice(pair * LANES, (pair + 1) * LANES)
                q_rows = q_ref[:, cols]
                do_rows = do_ref[:, cols]
                for k in range(2):
                    j = 2 * pair + k
                    span = slice(j * HEAD, (j + 1) * HEAD)
                    lane = low_lane if k == 0 else jnp.logical_not(low_lane)
                    scores = mm(key, q_turn[span, :]) * scale
                    if bias is not None:
                        scores = scores + bias
                    prob = jnp.exp2(scores - lse_ref[j:j + 1, :])
                    dprob = mm(value, do_turn[span, :])
                    dscore = (prob * (dprob - delta_ref[j:j + 1, :])).astype(BF16)
                    dq_acc[span, :] += mm(key_t, dscore)
                    dk = dk + mm(dscore, jnp.where(lane, q_rows, zero_rows))
                    dv = dv + mm(prob.astype(BF16), jnp.where(lane, do_rows, zero_rows))
            dkv_acc[:, own] = (dk[:, :HEAD] + dk[:, HEAD:]) * HEAD ** -0.5
            dkv_acc[:, kv_width + h * HEAD:kv_width + (h + 1) * HEAD] = dv[:, :HEAD] + dv[:, HEAD:]

    @pl.when(me > 0)
    def _():
        pl.semaphore_wait(barrier, me)

    def earlier(i, carry):
        d = me - i
        block(d, None)
        send_kv[d - 1] = dkv_acc[...].astype(BF16)
        to_earlier(d).start()
        return carry

    lax.fori_loop(0, me, earlier, 0)
    key_pos = lax.broadcasted_iota(jnp.int32, (rows, rows), 0)
    query_pos = lax.broadcasted_iota(jnp.int32, (rows, rows), 1)
    block(0, jnp.where(key_pos <= query_pos, 0.0, NEG_FILL))

    loads[1].wait()
    loads[2].wait()
    for at in range(0, width, chunk):
        for col in range(at, at + chunk, LANES):
            dq_ref[:, col:col + LANES] = rotated(dq_acc[col:col + LANES, :].T * HEAD ** -0.5, cos_ref, sin_ref).astype(BF16)
    for at in range(0, width, chunk):
        dn_ref[:, at:at + chunk] = mm_t(dq_ref[...], wq_ref[at:at + chunk, :])
    for d in range(1, n):
        @pl.when(me + d < n)
        def _(d=d):
            from_later(d).wait_recv()
            dkv_acc[...] += land_kv[d - 1].astype(F32)
    dkv_ref[:, :kv_width] = rotated(dkv_acc[:, :kv_width], cos_ref, sin_ref).astype(BF16)
    dkv_ref[:, kv_width:] = dkv_acc[:, kv_width:].astype(BF16)
    for at in range(0, width, chunk):
        dn_ref[:, at:at + chunk] += mm_t(dkv_ref[...], wkv_ref[at:at + chunk, :])
    x = x_ref[...].astype(F32)
    root = inv_root_of(x)
    dnormed = dn_ref[...]
    scaled = dnormed * gain_ref[...]
    grad = dmid_ref[...] + root * scaled - x * (root * root * root * jnp.mean(scaled * x, axis=-1, keepdims=True))
    grad_ref[...] = grad
    grad_low_ref[...] = grad.astype(BF16)
    dgain_ref[...] = jnp.sum(dnormed * x * root, axis=0, keepdims=True)
    for d in range(1, n):
        @pl.when(me >= d)
        def _(d=d):
            to_earlier(d).wait_send()


def attend_back(da, dmid, x, gain, cos_table, back_sin, q, kv, attended, lse, w_q, w_kv, w_o, collective_id):
    n = lax.axis_size("shard")
    rows, width = x.shape
    kv_both = w_kv.shape[1]
    vmem = pl.BlockSpec(memory_space=pltpu.VMEM)
    anywhere = pl.BlockSpec(memory_space=pl.ANY)
    dma = pltpu.SemaphoreType.DMA
    flops = 2 * rows * width * (2 * width + kv_both) + 10 * rows * rows * n * width
    return pl.pallas_call(
        attend_back_kernel,
        in_specs=[vmem] * 10 + [anywhere] * 3,
        out_specs=[vmem] * 5,
        out_shape=[
            jax.ShapeDtypeStruct((rows, width), BF16),
            jax.ShapeDtypeStruct((rows, kv_both), BF16),
            jax.ShapeDtypeStruct((rows, width), F32),
            jax.ShapeDtypeStruct((rows, width), BF16),
            jax.ShapeDtypeStruct((1, width), F32),
        ],
        scratch_shapes=[
            pltpu.VMEM(w_q.shape, BF16), pltpu.VMEM(w_kv.shape, BF16), pltpu.VMEM(w_o.shape, BF16),
            pltpu.VMEM((rows, width), BF16), pltpu.VMEM((width, rows), BF16), pltpu.VMEM((width, rows), BF16),
            pltpu.VMEM((HEADS, rows), F32), pltpu.VMEM((width, rows), F32), pltpu.VMEM((rows, kv_both), F32),
            pltpu.VMEM((rows, width), F32),
            pltpu.VMEM((n - 1, rows, kv_both), BF16), pltpu.VMEM((n - 1, rows, kv_both), BF16),
            dma((3,)), dma((n - 1,)), dma((n - 1,)),
        ],
        compiler_params=pltpu.CompilerParams(
            collective_id=collective_id, has_side_effects=True, vmem_limit_bytes=58 * 1024 * 1024),
        cost_estimate=pl.CostEstimate(flops=flops, bytes_accessed=2 * width * (2 * width + kv_both), transcendentals=rows * rows * n * HEADS),
        name="attend_back",
    )(da, dmid, x, gain, cos_table, back_sin, q, kv, attended, lse, w_q, w_kv, w_o)


ROPE_BASE = 10000.0


def angles_for(positions):
    half_dim = HEAD // 2
    inverse = ROPE_BASE ** (-(jnp.arange(half_dim, dtype=F32) * 2.0 / HEAD))
    angle_grid = positions.astype(F32)[:, None] * inverse[None, :]
    return (jnp.cos(angle_grid), jnp.sin(angle_grid))


def passed_along(block, axis, by):
    length = lax.axis_size(axis)
    pairs = [(i, i + by) for i in range(length) if 0 <= i + by < length]
    return lax.ppermute(block, axis, pairs)


def gather_rows(weight):
    parts = lax.axis_size("rep")
    rows = weight.shape[0] // parts
    own = lax.dynamic_slice_in_dim(weight, lax.axis_index("rep") * rows, rows, 0)
    return lax.all_gather(own, ("shard", "rep"), axis=0, tiled=True)


def layer_forward(stream_in, weights, tables):
    w_q, w_kv, w_o, w_g, w_u, w_d, gains_wide = weights
    cos_table, sin_table = tables
    normed, queries, kv, attended, lse, middle = attend_block(
        stream_in, gains_wide[0:1], cos_table, sin_table, w_q, w_kv, w_o, 3)
    result, normed_two, hidden, gate_fac, up_fac = ffn_fwd(middle, gains_wide[1:2], w_g, w_u, w_d)
    kept = {"stream": stream_in, "normed": normed, "queries": queries, "kv": kv, "attended": attended, "lse": lse,
            "middle": middle, "normed_two": normed_two, "hidden": hidden, "gate_fac": gate_fac, "up_fac": up_fac}
    return result, kept


def layer_backward(grad_bf, kept, weights, tables):
    w_q, w_kv, w_o, w_g, w_u, w_d, gains_wide = weights
    cos_table, sin_table = tables
    grad_gate, grad_up, grad_middle, grad_branch, gain_two = ffn_bwd(
        grad_bf, kept["middle"], gains_wide[1:2], kept["gate_fac"], kept["up_fac"], w_g, w_u, w_d)
    grad_query, grad_kv, grad_stream, grad_low, gain_one = attend_back(
        grad_branch, grad_middle, kept["stream"], gains_wide[0:1], cos_table, -sin_table, kept["queries"], kept["kv"],
        kept["attended"], kept["lse"], w_q, w_kv, w_o, 4)
    terms = (grad_query, grad_kv, grad_branch, grad_gate, grad_up, grad_bf)
    return grad_stream, grad_low, terms, jnp.concatenate([gain_one, gain_two], axis=0)


def body(tokens, cotangent, live_counts, w_query, w_key, w_value, w_out, w_gate, w_up, w_down, norm_gains):
    section = lax.axis_index("section")
    slot_count, span_len, model_width = tokens.shape
    query_pos = lax.axis_index("shard") * span_len + jnp.arange(span_len, dtype=jnp.int32)
    cos_half, sin_half = angles_for(query_pos)
    tables = (jnp.tile(cos_half, (1, 4)), jnp.tile(jnp.concatenate([-sin_half, sin_half], axis=1), (1, 2)))
    live_mask = (jnp.arange(slot_count) < live_counts[0]).astype(F32)
    gain_rows = jnp.pad(norm_gains[0], ((0, 14), (0, -norm_gains.shape[2] % (4 * LANES))))
    shards = [w_query[0], jnp.concatenate([w_key[0], w_value[0]], axis=1), w_out[0], gain_rows, w_gate[0], w_up[0]]
    w_q, w_kv, w_o, gains, w_g, w_u = gather_weights(shards, [halves(shard.shape[1]) for shard in shards], 2, "gather_weights")
    down_shard, w_q = lax.optimization_barrier((w_down[0], w_q))
    w_d = gather_rows(down_shard)
    gain_blocks = gains.reshape(-1, 16, gain_rows.shape[1])[:, :2, :norm_gains.shape[2]]
    gains_wide = gain_blocks.transpose(1, 0, 2).reshape(2, model_width).astype(F32)
    weights = (w_q, w_kv, w_o, w_g, w_u, w_d, gains_wide)
    masked_in = (tokens.astype(F32) * live_mask[:, None, None]).astype(BF16)
    masked_cot = (cotangent.astype(F32) * live_mask[:, None, None]).astype(BF16)
    zero_slot = jnp.zeros((span_len, model_width), BF16)
    ticks = slot_count + 1
    results, kept_all = [], []
    received = zero_slot
    for tick in range(ticks):
        slot_in = masked_in[tick] if tick < slot_count else zero_slot
        own_in = jnp.where(section == 0, slot_in, received)
        result, kept = layer_forward(own_in, weights, tables)
        received = passed_along(result, "section", 1)
        results.append(result)
        kept_all.append(kept)
    first = section == 0
    acts = jnp.stack([jnp.where(first, results[j], results[j + 1]) for j in range(slot_count)])
    received = zero_slot
    streams, term_list, gain_total = [], [], 0.0
    for tick in range(ticks):
        slot_cot = masked_cot[slot_count - 1 - tick] if tick < slot_count else zero_slot
        grad_bf = jnp.where(first, received, slot_cot)
        grad_stream, grad_low, terms, gain_grad = layer_backward(grad_bf, kept_all[ticks - 1 - tick], weights, tables)
        received = passed_along(grad_low, "section", -1)
        streams.append(grad_stream)
        term_list.append(terms)
        gain_total = gain_total + gain_grad
    grad_in = jnp.stack([
        jnp.where(first, streams[slot_count - j], streams[slot_count - 1 - j]) for j in range(slot_count)])

    def turned(index):
        picks = [jnp.where(first, kept_all[j][index], kept_all[j + 1][index]) for j in range(slot_count)]
        return jnp.concatenate(picks, axis=0).T

    def by_tick(index):
        return [terms[index] for terms in term_list]

    gate_sum, up_sum, qkv_sum, out_sum, down_sum = reduce_weights(
        [
            {"lefts": [turned("normed_two"), turned("normed"), turned("attended")], "which": [0, 0, 1, 2], "z_first": False, "blocks": 1, "pace": 1,
             "rights": [[by_tick(3)], [by_tick(4)], [by_tick(0), by_tick(1)], [by_tick(2)]]},
            {"lefts": [turned("hidden")], "which": [0], "z_first": True, "blocks": 2, "pace": 3, "rights": [[by_tick(5)]]},
        ],
        slot_count, 1, "reduce_weights")
    kv_width = w_key.shape[2]
    gain_part = lax.psum_scatter(gain_total, "shard", scatter_dimension=1, tiled=True)
    gain_sum = lax.psum(gain_part, "rep")
    outs = (
        qkv_sum[:, :model_width],
        qkv_sum[:, model_width:model_width + kv_width],
        qkv_sum[:, model_width + kv_width:],
        out_sum,
        gate_sum,
        up_sum,
        down_sum,
        gain_sum,
    )
    return (acts[None], grad_in[None]) + tuple(out.astype(F32)[None] for out in outs)


def solution(mesh):
    tall = P("section", "shard", None)
    per_slot = P("section", "rep", "shard", None)
    return jax.shard_map(
        body,
        mesh=mesh,
        in_specs=(P("rep", "shard", None), P("rep", "shard", None), P("rep")) + (tall,) * 7 + (P("section", None, "shard"),),
        out_specs=(per_slot, per_slot) + (tall,) * 7 + (P("section", None, "shard"),),
        check_vma=False,
    )
```

```python
import functools, math
import jax
import jax.numpy as jnp
from jax import lax
from jax.sharding import PartitionSpec as P
from jax.experimental import pallas as pl
from jax.experimental.pallas import tpu as pltpu

HEADS = 32
KV_HEADS = 4
HEAD = 64
LOG2E = math.log2(math.e)
NEG_FILL = -1e30
F32, BF16 = jnp.float32, jnp.bfloat16


def mm(a, b):
    return jnp.dot(a, b, preferred_element_type=F32)


MESH_IDS = pl.DeviceIdType.MESH
LANES = 128
BUFS = 26


def remote(src, dst, send_sem, recv_sem, peer):
    return pltpu.make_async_remote_copy(src, dst, send_sem, recv_sem, device_id=peer, device_id_type=MESH_IDS)


def reduce_stages(kind, blocks, delay, segments, place, a_ref, b_ref, bufs):
    n, me, rep, right, core_peer, y_peer = place
    own_core, own_y = lax.rem(rep, 2), rep // 2
    paired = kind == "pair"
    (send_c, own, land_c, keep, send_y, land_y, send_z, land_z, send_f,
     sc_sem, rc_sem, cr_c, sy_sem, ry_sem, cr_y, sz_sem, rz_sem, ly_sem, sfy_sem, sfc_sem,
     rfy_sem, rfc_sem, sfw_sem, rfw_sem) = bufs
    rows = own.shape[2]
    depth = land_z.shape[1]
    span = a_ref.shape[3]
    items = b_ref.shape[2] // LANES * blocks
    starts = [first for _, _, first in segments]
    ends = starts[1:] + [items // blocks]

    def spot_of(out, first, r, p):
        width = out.shape[1] // 4
        column = pl.multiple_of(r * width + (p // blocks - first) * LANES, LANES)
        row = pl.multiple_of(lax.rem(p, blocks) * rows, 16)
        return out.at[pl.ds(row, rows), pl.ds(column, LANES)]

    def each_segment(p, fn):
        for (out, _, first), last in zip(segments, ends):
            if len(segments) == 1:
                fn(lambda r, out=out, first=first: spot_of(out, first, r, p))
                continue
            group = p // blocks

            @pl.when(jnp.logical_and(group >= first, group < last))
            def _(out=out, first=first):
                fn(lambda r: spot_of(out, first, r, p))

    def c_copy(a, s):
        return remote(send_c.at[a], land_c.at[s], sc_sem.at[a], rc_sem.at[s], core_peer)

    def y_copy(a, s):
        return remote(send_y.at[a], land_y.at[s], sy_sem.at[a], ry_sem.at[s], y_peer)

    def z_copy(a, s, p):
        b = lax.rem(p, depth)
        return remote(send_z.at[a], land_z.at[s, b], sz_sem.at[a], rz_sem.at[s, b], right)

    def f_local(a, spot):
        return pltpu.make_async_copy(send_f.at[a], spot(rep), ly_sem.at[a])

    def f_y(a, p, spot):
        return remote(send_f.at[a], spot(rep), sfy_sem.at[a], rfy_sem.at[p], y_peer)

    def f_core(a, p, spot):
        return remote(send_f.at[a], spot(rep), sfc_sem.at[a], rfc_sem.at[p], core_peer)

    def f_turn(a, p, spot):
        there = spot(rep + 2 - 4 * own_y)
        return remote(there, there, sfw_sem.at[a], rfw_sem.at[p], core_peer)

    def stage_zero(a, s, p):
        dest = lax.rem(me + 2 * n - 1 - s, n)
        row = pl.ds(pl.multiple_of((dest * blocks + lax.rem(p, blocks)) * rows, 16), rows)
        which = 0
        for (_, index, first) in segments[1:]:
            which = jnp.where(p // blocks >= first, index, which)
        column = pl.ds(pl.multiple_of(p // blocks * LANES, LANES), LANES)

        def product(r):
            total = None
            for k in range(a_ref.shape[1]):
                term = mm(a_ref[which, k, row, :], b_ref[r, k * span:(k + 1) * span, column])
                total = term if total is None else total + term
            return total
        tiles = range(1 if paired else 2)
        for y in tiles:
            send_c[a, y] = product(2 * y + 1 - own_core).astype(BF16)

        @pl.when(p >= 1)
        def _():
            pl.semaphore_wait(cr_c.at[s], 1)
        c_copy(a, s).start()
        for y in tiles:
            own[a, y] = product(2 * y + own_core)

    def credit(sem, s, p, peer):
        @pl.when(p + 1 < items)
        def _():
            pl.semaphore_signal(sem.at[s], inc=1, device_id=peer, device_id_type=MESH_IDS)

    def finish(a, p, total):
        send_f[a] = total.astype(BF16)

        def send(spot):
            f_y(a, p, spot).start()
            f_core(a, p, spot).start()
            f_local(a, spot).start()
        each_segment(p, send)

    def go_round(a, s, p, ref):
        @pl.when(s > 0)
        def _():
            z_copy(a, s - 1, p).wait_recv()
            ref[...] = ref[...] + land_z[s - 1, lax.rem(p, depth)].astype(F32)

        @pl.when(s < n - 1)
        def _():
            send_z[a] = ref[...].astype(BF16)
            z_copy(a, s, p).start()

        @pl.when(s == n - 1)
        def _():
            finish(a, p, ref[...])

    def stage_one_pair(a, s, p):
        c_copy(a, s).wait()
        own[a, 0] = own[a, 0] + land_c[s, 0].astype(F32)
        credit(cr_c, s, p, core_peer)
        go_round(a, s, p, own.at[a, 0])

    def stage_one_y(a, s, p):
        c_copy(a, s).wait()
        send_y[a] = (own[a, 1 - own_y] + land_c[s, 1 - own_y].astype(F32)).astype(BF16)

        @pl.when(p >= 1)
        def _():
            pl.semaphore_wait(cr_y.at[s], 1)
        y_copy(a, s).start()
        keep[a] = own[a, own_y] + land_c[s, own_y].astype(F32)
        credit(cr_c, s, p, core_peer)

    def stage_two_y(a, s, p):
        y_copy(a, s).wait()
        keep[a] = keep[a] + land_y[s].astype(F32)
        credit(cr_y, s, p, y_peer)
        go_round(a, s, p, keep.at[a])

    def turn_over(a, s, p):
        @pl.when(s < n - 1)
        def _():
            z_copy(a, s, p).wait_send()

        @pl.when(s == n - 1)
        def _():
            def turn(spot):
                f_local(a, spot).wait()
                f_core(a, p, spot).wait_send()
                f_y(a, p, spot).wait()
                f_turn(a, p, spot).start()
            each_segment(p, turn)

    def end_of(a, s, p):
        @pl.when(s == n - 1)
        def _():
            def end(spot):
                f_core(a, p, spot).wait_recv()
                f_turn(a, p, spot).wait()
            each_segment(p, end)

    if paired:
        return items, (stage_zero, stage_one_pair, turn_over, end_of)
    return items, (stage_zero, stage_one_y, stage_two_y, turn_over, end_of)


def gain_steps(place, gain_ref, out_ref, total, land_c, land_y, land_z, sends, lands):
    n, me, _, _, core_peer, y_peer = place
    chunk = out_ref.shape[1]

    def over_core():
        return remote(total, land_c, sends.at[0], lands.at[0], core_peer)

    def over_y():
        return remote(total, land_y, sends.at[1], lands.at[1], y_peer)

    def over_z(d):
        dest = lax.rem(me + d, n)
        part = total.at[:, pl.ds(pl.multiple_of(dest * chunk, LANES), chunk)]
        return remote(part, land_z.at[d - 1], sends.at[d + 1], lands.at[d + 1], {"shard": dest})

    def begin():
        total[...] = gain_ref[...]
        over_core().start()

    def add_core():
        over_core().wait()
        total[...] = total[...] + land_c[...]
        over_y().start()

    def add_y():
        over_y().wait()
        total[...] = total[...] + land_y[...]
        for d in range(1, n):
            over_z(d).start()

    def add_z():
        result = total[:, pl.ds(pl.multiple_of(me * chunk, LANES), chunk)]
        for d in range(1, n):
            over_z(d).wait()
            result = result + land_z[d - 1]
        out_ref[...] = result

    return ((3, begin), (30, add_core), (60, add_y), (90, add_z))


def reduce_kernel(streams, slots, *refs):
    n = lax.axis_size("shard")
    me = lax.axis_index("shard")
    rep = lax.axis_index("rep")
    section = lax.axis_index("section")
    right = {"shard": lax.rem(me + 1, n)}
    core_peer = {"rep": rep + 1 - 2 * lax.rem(rep, 2)}
    y_peer = {"rep": rep + 2 - 4 * (rep // 2)}
    place = (n, me, rep, right, core_peer, y_peer)

    refs = list(refs)
    gain_ref = refs.pop(0)

    def taken(tree):
        return [taken(x) for x in tree] if isinstance(tree, list) else refs.pop(0)
    lefts = [taken(stream["lefts"]) for stream in streams]
    rights = [taken(stream["rights"]) for stream in streams]
    outs = [[refs.pop(0) for _ in stream["rights"]] for stream in streams]
    gain_out = refs.pop(0)
    per = [[refs.pop(0) for _ in range(BUFS)] for _ in streams]
    load_sem = refs.pop(0)
    timed = gain_steps(place, gain_ref, gain_out, *refs)

    barrier = pltpu.get_barrier_semaphore()
    for peer in [{"shard": lax.rem(me + d, n)} for d in range(1, n)] + [core_peer, y_peer]:
        pl.semaphore_signal(barrier, inc=1, device_id=peer, device_id_type=MESH_IDS)

    def load_all(at_section):
        loads = []

        def load(src, dst):
            loads.append(pltpu.make_async_copy(src, dst, load_sem.at[len(loads)]))
            loads[-1].start()

        def tick_of(ticks, j):
            return ticks[slots - j if at_section == 0 else slots - 1 - j]
        for stream, left_refs, right_refs, bufs in zip(streams, lefts, rights, per):
            a_ref, b_ref = bufs[0], bufs[1]
            for k, groups in enumerate(left_refs):
                for g, ticks in enumerate(groups):
                    for j in range(slots):
                        load(tick_of(ticks, j), a_ref.at[k, g * slots + j])
            base = 0
            for segment in right_refs:
                if stream["kind"] == "pair":
                    mine, other = segment
                    quarter = mine[0].shape[1] // 4
                    for c in range(2):
                        column = pl.ds(pl.multiple_of((rep // 2 * 2 + c) * quarter, LANES), quarter)
                        for g, ticks in enumerate((mine, other)):
                            for j in range(slots):
                                tick = tick_of(ticks, j)
                                span = tick.shape[0]
                                at = (g * slots + j) * span
                                load(tick.at[:, column] if g == 0 else tick.at[:, 2 * base + c * quarter:2 * base + (c + 1) * quarter],
                                     b_ref.at[c, at:at + span, base:base + quarter])
                    base += quarter
                    continue
                quarter = sum(ticks[0].shape[1] for ticks in segment) // 4
                for r in range(4):
                    at = 0
                    for ticks in segment:
                        width = ticks[0].shape[1]
                        lo, hi = max(r * quarter, at), min((r + 1) * quarter, at + width)
                        if lo < hi:
                            for j in range(slots):
                                tick = tick_of(ticks, j)
                                span = tick.shape[0]
                                load(tick.at[:, lo - at:hi - at],
                                     b_ref.at[r, j * span:(j + 1) * span, base + lo - r * quarter:base + hi - r * quarter])
                        at += width
                base += quarter
        for copy in loads:
            copy.wait()

    for value in range(2):
        @pl.when(section == value)
        def _(value=value):
            load_all(value)
    pl.semaphore_wait(barrier, n + 1)

    work, last = [], 0
    for stream, segs, bufs in zip(streams, outs, per):
        delay = stream["delay"]
        items, fns = reduce_stages(
            stream["kind"], stream["blocks"], delay,
            [(out, index, first) for out, index, first in zip(segs, stream["which"], stream["firsts"])],
            place, bufs[0], bufs[1], bufs[2:])
        pace = stream["pace"]
        work.append((pace, delay, items, fns))
        last = max(last, pace * (n * (items + n - 1) + (len(fns) - 1) * delay))

    def step(i, carry):
        for k in (4, 3, 2, 1, 0):
            for pace, delay, items, fns in work:
                if k >= len(fns):
                    continue
                v = i // pace - delay * k
                s = lax.rem(v + n * delay * 4, n)
                p = (v - s) // n - s
                fine = jnp.logical_and(jnp.logical_and(v >= 0, lax.rem(i, pace) == 0), jnp.logical_and(p >= 0, p < items))

                @pl.when(fine)
                def _(s=s, p=p, v=v, fn=fns[k], delay=delay):
                    fn(lax.rem(v, delay), s, p)
        for at, fn in timed:
            pl.when(i == at)(fn)
        return carry

    lax.fori_loop(0, last, step, 0)


def reduce_weights(gain, streams, slots, collective_id, name):
    n = lax.axis_size("shard")
    operands, out_shapes, scratch, flops, moved, plans, loads = [], [], [], 0, 0, [], 0
    dma, regular = pltpu.SemaphoreType.DMA, pltpu.SemaphoreType.REGULAR

    def listed(tree):
        if isinstance(tree, list):
            return [listed(x) for x in tree]
        operands.append(tree)
        return None
    left_plans = [listed(stream["lefts"]) for stream in streams]
    right_plans = [listed(stream["rights"]) for stream in streams]
    for stream, left_plan, right_plan in zip(streams, left_plans, right_plans):
        paired = stream["kind"] == "pair"
        blocks, delay = stream["blocks"], stream["delay"]
        height, span = stream["lefts"][0][0][0].shape
        height //= n
        chunks = len(stream["lefts"][0]) * slots
        firsts, at = [], 0
        for segment in stream["rights"]:
            width = segment[0][0].shape[1] if paired else sum(ticks[0].shape[1] for ticks in segment)
            firsts.append(at)
            at += width // 4 // LANES
            out_shapes.append(jax.ShapeDtypeStruct((height, width), BF16))
            flops += 2 * span * slots * height * n * width
            moved += height * width * 4
            loads += 4 * slots * len(segment)
        loads += len(stream["lefts"]) * chunks
        items = at * blocks
        depth = min(items, n + 2)
        tile = (height // blocks, LANES)
        both = 1 if paired else 2
        few = (16, LANES)
        scratch += [
            pltpu.VMEM((len(stream["lefts"]), chunks, height * n, span), BF16),
            pltpu.VMEM((2 * both, chunks * span, at * LANES), BF16),
            pltpu.VMEM((delay, both) + tile, BF16),
            pltpu.VMEM((delay, both) + tile, F32),
            pltpu.VMEM((n, both) + tile, BF16),
            pltpu.VMEM((1,) + few if paired else (delay,) + tile, F32),
            pltpu.VMEM((1,) + few if paired else (delay,) + tile, BF16),
            pltpu.VMEM((1,) + few if paired else (n,) + tile, BF16),
            pltpu.VMEM((delay,) + tile, BF16),
            pltpu.VMEM((n - 1, depth) + tile, BF16),
            pltpu.VMEM((delay,) + tile, BF16),
            dma((delay,)), dma((n,)), regular((n,)),
            dma((delay,)), dma((n,)), regular((n,)),
            dma((delay,)), dma((n - 1, depth)),
            dma((delay,)), dma((delay,)), dma((delay,)),
            dma((items,)), dma((items,)), dma((delay,)), dma((items,)),
        ]
        plans.append({
            "kind": stream["kind"], "blocks": blocks, "delay": delay, "pace": stream["pace"], "which": tuple(stream["which"]),
            "firsts": tuple(firsts), "lefts": left_plan, "rights": right_plan})
    chunk = gain.shape[1] // n
    out_shapes.append(jax.ShapeDtypeStruct((gain.shape[0], chunk), F32))
    scratch += [dma((loads,))] + [pltpu.VMEM(gain.shape, F32)] * 3
    scratch += [pltpu.VMEM((n - 1, gain.shape[0], chunk), F32), dma((n + 1,)), dma((n + 1,))]
    in_vmem = pl.BlockSpec(memory_space=pltpu.VMEM)
    anywhere = pl.BlockSpec(memory_space=pl.ANY)
    return pl.pallas_call(
        functools.partial(reduce_kernel, plans, slots),
        in_specs=[in_vmem] + [anywhere] * len(operands),
        out_specs=[anywhere] * (len(out_shapes) - 1) + [in_vmem],
        out_shape=out_shapes,
        scratch_shapes=scratch,
        compiler_params=pltpu.CompilerParams(
            collective_id=collective_id, has_side_effects=True, vmem_limit_bytes=60 * 1024 * 1024),
        cost_estimate=pl.CostEstimate(flops=flops, bytes_accessed=moved, transcendentals=0),
        name=name,
    )(gain, *operands)


def gather_kernel(splits, *refs):
    n = lax.axis_size("shard")
    me = lax.axis_index("shard")
    rep = lax.axis_index("rep")
    right = {"shard": lax.rem(me + 1, n)}
    left = {"shard": lax.rem(me + n - 1, n)}
    core_peer = {"rep": rep + 1 - 2 * lax.rem(rep, 2)}
    y_rep = rep + 2 - 4 * (rep // 2)
    y_peer = {"rep": y_rep}
    count = len(splits)
    ins, outs = refs[:count], refs[count:2 * count]
    holds = refs[2 * count:3 * count]
    zs, zr, ys, yr, cs, cr, ts, tr, local = refs[3 * count:]

    barrier = pltpu.get_barrier_semaphore()
    for peer in (left, right, core_peer, y_peer):
        pl.semaphore_signal(barrier, inc=1, device_id=peer, device_id_type=MESH_IDS)

    pieces = []
    for k, split in enumerate(splits):
        at = 0
        for width in split:
            pieces.append((k, at, width))
            at += width

    def own_load(k):
        return pltpu.make_async_copy(ins[k], holds[k], local.at[0, k])

    def own_store(k):
        rows = ins[k].shape[0]
        return pltpu.make_async_copy(holds[k], outs[k].at[pl.ds(pl.multiple_of(me * rows, 16), rows), :], local.at[1, k])

    def spot(piece, back, r):
        k, at, width = pieces[piece]
        rows = ins[k].shape[0]
        block = lax.rem(me + n - back, n)
        column = pl.multiple_of(r * (ins[k].shape[1] // 4) + at, LANES)
        return outs[k].at[pl.ds(pl.multiple_of(block * rows, 16), rows), pl.ds(column, width)]

    def z_copy(piece, s):
        k, at, width = pieces[piece]
        there = spot(piece, s, rep)
        column = pl.multiple_of(rep * (ins[k].shape[1] // 4) + at, LANES)
        here = ins[k].at[:, pl.ds(column, width)] if s == 0 else there
        return remote(here, there, zs.at[piece, s], zr.at[piece, s], right)

    def y_copy(piece, s):
        there = spot(piece, s, rep)
        return remote(there, there, ys.at[piece, s - 1], yr.at[piece, s - 1], y_peer)

    def c_copy(piece, s):
        there = spot(piece, s, rep)
        return remote(there, there, cs.at[piece, s - 1], cr.at[piece, s - 1], core_peer)

    def t_copy(piece, s):
        there = spot(piece, s, y_rep)
        return remote(there, there, ts.at[piece, s - 1], tr.at[piece, s - 1], core_peer)

    def turn(piece, s):
        y_copy(piece, s).wait_recv()
        t_copy(piece, s).start()

    pl.semaphore_wait(barrier, 4)
    for piece in range(len(pieces)):
        z_copy(piece, 0).start()
    for k in range(count):
        own_load(k).start()
    for k in range(count):
        own_load(k).wait()
        own_store(k).start()
    before = []
    for s in range(1, n):
        for piece in range(len(pieces)):
            z_copy(piece, s - 1).wait_recv()
            if s < n - 1:
                z_copy(piece, s).start()
            y_copy(piece, s).start()
            c_copy(piece, s).start()
            before.append((piece, s))
            if len(before) > 1:
                turn(*before[-2])
    turn(*before[-1])
    for k in range(count):
        own_store(k).wait()
    for piece, s in before:
        z_copy(piece, s - 1).wait_send()
        y_copy(piece, s).wait_send()
        c_copy(piece, s).wait()
        t_copy(piece, s).wait()


def gather_weights(shards, splits, collective_id, name):
    n = lax.axis_size("shard")
    dma = pltpu.SemaphoreType.DMA
    pieces = sum(len(split) for split in splits)
    pair = dma((pieces, n - 1))
    anywhere = pl.BlockSpec(memory_space=pl.ANY)
    moved = 2 * n * sum(shard.shape[0] * shard.shape[1] for shard in shards)
    return pl.pallas_call(
        functools.partial(gather_kernel, splits),
        in_specs=[anywhere] * len(shards),
        out_specs=[anywhere] * len(shards),
        out_shape=[jax.ShapeDtypeStruct((n * shard.shape[0], shard.shape[1]), BF16) for shard in shards],
        scratch_shapes=[pltpu.VMEM(shard.shape, BF16) for shard in shards] + [pair] * 8 + [dma((2, len(shards)))],
        compiler_params=pltpu.CompilerParams(collective_id=collective_id, has_side_effects=True, vmem_limit_bytes=40 * 1024 * 1024),
        cost_estimate=pl.CostEstimate(flops=0, bytes_accessed=moved * 4, transcendentals=0),
        name=name,
    )(*shards)


def halves(width):
    quarter = width // 4
    first = (quarter // LANES + 1) // 2 * LANES
    return (first, quarter - first) if quarter > first else (quarter,)


EPSILON = 1e-05
FF_TILE = 512


def mm_t(a, b):
    return lax.dot_general(a, b, (((1,), (1,)), ((), ())), preferred_element_type=F32)


def inv_root_of(rows):
    return lax.rsqrt(jnp.mean(rows * rows, axis=-1, keepdims=True) + EPSILON)


def ffn_fwd_kernel(mid_ref, gain_ref, w_g, w_u, w_d, out_ref, normed_turn, hidden_turn, gate_fac, up_fac, acc, normed_ref):
    step = pl.program_id(0)

    @pl.when(step == 0)
    def _():
        mid = mid_ref[...]
        normed_ref[...] = (mid * inv_root_of(mid) * gain_ref[...]).astype(BF16)
        acc[...] = mid
        for at in range(0, mid.shape[1], LANES):
            normed_turn[at:at + LANES, :] = normed_ref[:, at:at + LANES].T

    gate = mm(normed_ref[...], w_g[...])
    up = mm(normed_ref[...], w_u[...])
    sig = jax.nn.sigmoid(gate)
    act = gate * sig
    hidden = (act * up).astype(BF16)
    hidden_turn[...] = hidden.T
    up_fac[...] = act.astype(BF16)
    gate_fac[...] = (up * sig * (1.0 + gate * (1.0 - sig))).astype(BF16)
    acc[...] += mm(hidden, w_d[...])

    @pl.when(step == pl.num_programs(0) - 1)
    def _():
        out_ref[...] = acc[...].astype(BF16)


def ffn_fwd(middle, gain, w_g, w_u, w_d):
    rows, width = middle.shape
    ff = w_g.shape[1]
    whole = pl.BlockSpec((rows, width), lambda i: (0, 0))
    part = pl.BlockSpec((rows, FF_TILE), lambda i: (0, i))
    tall = pl.BlockSpec((width, FF_TILE), lambda i: (0, i))
    wide = jax.ShapeDtypeStruct((rows, ff), BF16)
    return pl.pallas_call(
        ffn_fwd_kernel,
        grid=(ff // FF_TILE,),
        in_specs=[whole, pl.BlockSpec((1, width), lambda i: (0, 0)), tall, tall, pl.BlockSpec((FF_TILE, width), lambda i: (i, 0))],
        out_specs=[whole, pl.BlockSpec((width, rows), lambda i: (0, 0)), pl.BlockSpec((FF_TILE, rows), lambda i: (i, 0)), part, part],
        out_shape=[jax.ShapeDtypeStruct((rows, width), BF16), jax.ShapeDtypeStruct((width, rows), BF16),
                   jax.ShapeDtypeStruct((ff, rows), BF16), wide, wide],
        scratch_shapes=[pltpu.VMEM((rows, width), F32), pltpu.VMEM((rows, width), BF16)],
        compiler_params=pltpu.CompilerParams(vmem_limit_bytes=58 * 1024 * 1024),
        cost_estimate=pl.CostEstimate(flops=6 * rows * width * ff, bytes_accessed=6 * width * ff, transcendentals=rows * ff),
        name="ffn_fwd",
    )(middle, gain, w_g, w_u, w_d)


def ffn_bwd_kernel(grad_ref, mid_ref, gain_ref, gate_fac, up_fac, w_g, w_u, w_d,
                   dgate_ref, dup_ref, dmid_ref, da_ref, dgain_ref, acc):
    step = pl.program_id(0)
    dhidden = mm_t(grad_ref[...], w_d[...])
    dgate = (dhidden * gate_fac[...].astype(F32)).astype(BF16)
    dup = (dhidden * up_fac[...].astype(F32)).astype(BF16)
    dgate_ref[...] = dgate
    dup_ref[...] = dup
    term = mm_t(dgate, w_g[...]) + mm_t(dup, w_u[...])

    @pl.when(step == 0)
    def _():
        acc[...] = term

    @pl.when(step > 0)
    def _():
        acc[...] += term

    @pl.when(step == pl.num_programs(0) - 1)
    def _():
        mid = mid_ref[...]
        root = inv_root_of(mid)
        dnormed = acc[...]
        scaled = dnormed * gain_ref[...]
        dmid = grad_ref[...].astype(F32) + root * scaled - mid * (root * root * root * jnp.mean(scaled * mid, axis=-1, keepdims=True))
        dmid_ref[...] = dmid
        da_ref[...] = dmid.astype(BF16)
        dgain_ref[...] = jnp.sum(dnormed * mid * root, axis=0, keepdims=True)


def ffn_bwd(grad, middle, gain, gate_fac, up_fac, w_g, w_u, w_d):
    rows, width = middle.shape
    ff = w_g.shape[1]
    whole = pl.BlockSpec((rows, width), lambda i: (0, 0))
    flat = pl.BlockSpec((1, width), lambda i: (0, 0))
    part = pl.BlockSpec((rows, FF_TILE), lambda i: (0, i))
    tall = pl.BlockSpec((width, FF_TILE), lambda i: (0, i))
    wide = jax.ShapeDtypeStruct((rows, ff), BF16)
    return pl.pallas_call(
        ffn_bwd_kernel,
        grid=(ff // FF_TILE,),
        in_specs=[whole, whole, flat, part, part, tall, tall, pl.BlockSpec((FF_TILE, width), lambda i: (i, 0))],
        out_specs=[part, part, whole, whole, flat],
        out_shape=[wide, wide, jax.ShapeDtypeStruct((rows, width), F32), jax.ShapeDtypeStruct((rows, width), BF16),
                   jax.ShapeDtypeStruct((1, width), F32)],
        scratch_shapes=[pltpu.VMEM((rows, width), F32)],
        compiler_params=pltpu.CompilerParams(vmem_limit_bytes=58 * 1024 * 1024),
        cost_estimate=pl.CostEstimate(flops=6 * rows * width * ff, bytes_accessed=6 * width * ff, transcendentals=0),
        name="ffn_bwd",
    )(grad, middle, gain, gate_fac, up_fac, w_g, w_u, w_d)


def rotated(rows, cos_ref, sin_ref):
    width = rows.shape[1]
    low_half = lax.rem(lax.broadcasted_iota(jnp.int32, rows.shape, 1), HEAD) < HEAD // 2
    swapped = jnp.where(low_half, pltpu.roll(rows, width - HEAD // 2, 1), pltpu.roll(rows, HEAD // 2, 1))
    reps = width // LANES
    return rows * jnp.tile(cos_ref[...], (1, reps)) + swapped * jnp.tile(sin_ref[...], (1, reps))


def attend_block_kernel(x_ref, gain_ref, cos_ref, sin_ref, w_q, w_kv, w_o,
                        normed_turn, q_ref, kv_ref, attended_turn, lse_ref, mid_ref,
                        normed_ref, attended_ref, wq_ref, wkv_ref, wo_ref, q_turn, acc, top_ref, total_ref, land,
                        load_sem, send_sem, recv_sem):
    n = lax.axis_size("shard")
    me = lax.axis_index("shard")
    rows, width = x_ref.shape
    kv_width = wkv_ref.shape[1] // 2
    group = HEADS // KV_HEADS
    scale = LOG2E * HEAD ** -0.5
    barrier = pltpu.get_barrier_semaphore()
    for d in range(1, n):
        @pl.when(me >= d)
        def _(d=d):
            pl.semaphore_signal(barrier, inc=1, device_id={"shard": me - d}, device_id_type=MESH_IDS)
    loads = [pltpu.make_async_copy(src, dst, load_sem.at[k])
             for k, (src, dst) in enumerate(((w_kv, wkv_ref), (w_q, wq_ref), (w_o, wo_ref)))]
    for load in loads:
        load.start()

    def to_later(d):
        return remote(land.at[0], land.at[d], send_sem.at[d - 1], recv_sem.at[d - 1], {"shard": me + d})

    def from_earlier(d):
        return remote(land.at[0], land.at[d], send_sem.at[d - 1], recv_sem.at[d - 1], {"shard": me - d})

    x = x_ref[...].astype(F32)
    normed_ref[...] = (x * inv_root_of(x) * gain_ref[...]).astype(BF16)
    loads[0].wait()
    kv = mm(normed_ref[...], wkv_ref[...])
    land[0, :, :kv_width] = rotated(kv[:, :kv_width], cos_ref, sin_ref).astype(BF16)
    land[0, :, kv_width:] = kv[:, kv_width:].astype(BF16)
    @pl.when(me < n - 1)
    def _():
        pl.semaphore_wait(barrier, n - 1 - me)

    for d in range(1, n):
        @pl.when(me + d < n)
        def _(d=d):
            to_later(d).start()
    loads[1].wait()
    chunk = 4 * LANES
    for at in range(0, width, chunk):
        q_chunk = rotated(mm(normed_ref[...], wq_ref[:, at:at + chunk]), cos_ref, sin_ref).astype(BF16)
        q_ref[:, at:at + chunk] = q_chunk
        q_turn[at:at + chunk, :] = q_chunk.T

    def heads_of(d):
        for h in range(KV_HEADS):
            key = land[d, :, h * HEAD:(h + 1) * HEAD]
            pair_t = land[d, :, kv_width + h // 2 * LANES:kv_width + (h // 2 + 1) * LANES].T
            value_t = pair_t[h % 2 * HEAD:(h % 2 + 1) * HEAD, :]
            for j in range(h * group, (h + 1) * group):
                yield j, key, value_t

    key_pos = lax.broadcasted_iota(jnp.int32, (rows, rows), 0)
    query_pos = lax.broadcasted_iota(jnp.int32, (rows, rows), 1)
    bias = jnp.where(key_pos <= query_pos, 0.0, NEG_FILL)
    for j, key, value_t in heads_of(0):
        span = slice(j * HEAD, (j + 1) * HEAD)
        scores = mm(key, q_turn[span, :]) * scale + bias
        top = jnp.max(scores, axis=0, keepdims=True)
        prob = jnp.exp2(scores - top)
        top_ref[j:j + 1, :] = top
        total_ref[j:j + 1, :] = jnp.sum(prob, axis=0, keepdims=True)
        acc[span, :] = mm(value_t, prob.astype(BF16))

    def earlier(d, carry):
        from_earlier(d).wait_recv()
        for j, key, value_t in heads_of(d):
            span = slice(j * HEAD, (j + 1) * HEAD)
            scores = mm(key, q_turn[span, :]) * scale
            old = top_ref[j:j + 1, :]
            top = jnp.maximum(old, jnp.max(scores, axis=0, keepdims=True))
            fade = jnp.exp2(old - top)
            prob = jnp.exp2(scores - top)
            top_ref[j:j + 1, :] = top
            total_ref[j:j + 1, :] = total_ref[j:j + 1, :] * fade + jnp.sum(prob, axis=0, keepdims=True)
            acc[span, :] = acc[span, :] * fade + mm(value_t, prob.astype(BF16))
        return carry

    lax.fori_loop(1, me + 1, earlier, 0)
    total = total_ref[...]
    lse_ref[...] = top_ref[...] + jnp.log2(total)
    total_ref[...] = 1.0 / total
    for pair in range(HEADS // 2):
        col = pair * LANES
        halves_t = [acc[col + k * HEAD:col + (k + 1) * HEAD, :] * total_ref[2 * pair + k:2 * pair + k + 1, :] for k in range(2)]
        both_t = jnp.concatenate(halves_t, axis=0).astype(BF16)
        attended_turn[col:col + LANES, :] = both_t
        attended_ref[:, col:col + LANES] = both_t.T
        normed_turn[col:col + LANES, :] = normed_ref[:, col:col + LANES].T
    for d in range(n):
        @pl.when(me >= d)
        def _(d=d):
            kv_ref[d] = land[d]
    loads[2].wait()
    for at in range(0, width, chunk):
        mid_ref[:, at:at + chunk] = x_ref[:, at:at + chunk].astype(F32) + mm(attended_ref[...], wo_ref[:, at:at + chunk])
    for d in range(1, n):
        @pl.when(me + d < n)
        def _(d=d):
            to_later(d).wait_send()


def attend_block(x, gain, cos_table, sin_table, w_q, w_kv, w_o, collective_id):
    n = lax.axis_size("shard")
    rows, width = x.shape
    kv_both = w_kv.shape[1]
    vmem = pl.BlockSpec(memory_space=pltpu.VMEM)
    anywhere = pl.BlockSpec(memory_space=pl.ANY)
    dma = pltpu.SemaphoreType.DMA
    flops = 2 * rows * width * (2 * width + kv_both) + 4 * rows * rows * n * width
    return pl.pallas_call(
        attend_block_kernel,
        in_specs=[vmem] * 4 + [anywhere] * 3,
        out_specs=[vmem] * 6,
        out_shape=[
            jax.ShapeDtypeStruct((width, rows), BF16),
            jax.ShapeDtypeStruct((rows, width), BF16),
            jax.ShapeDtypeStruct((n, rows, kv_both), BF16),
            jax.ShapeDtypeStruct((width, rows), BF16),
            jax.ShapeDtypeStruct((HEADS, rows), F32),
            jax.ShapeDtypeStruct((rows, width), F32),
        ],
        scratch_shapes=[
            pltpu.VMEM((rows, width), BF16), pltpu.VMEM((rows, width), BF16),
            pltpu.VMEM(w_q.shape, BF16), pltpu.VMEM(w_kv.shape, BF16), pltpu.VMEM(w_o.shape, BF16),
            pltpu.VMEM((width, rows), BF16), pltpu.VMEM((width, rows), F32),
            pltpu.VMEM((HEADS, rows), F32), pltpu.VMEM((HEADS, rows), F32),
            pltpu.VMEM((n, rows, kv_both), BF16),
            dma((3,)), dma((n - 1,)), dma((n - 1,)),
        ],
        compiler_params=pltpu.CompilerParams(
            collective_id=collective_id, has_side_effects=True, vmem_limit_bytes=56 * 1024 * 1024),
        cost_estimate=pl.CostEstimate(flops=flops, bytes_accessed=2 * width * (2 * width + kv_both), transcendentals=rows * rows * n * HEADS),
        name="attend_block",
    )(x, gain, cos_table, sin_table, w_q, w_kv, w_o)


def attend_back_kernel(da_ref, dmid_ref, x_ref, gain_ref, cos_ref, sin_ref, q_ref, kv_ref, attended_turn, lse_ref, w_q, w_kv, w_o,
                       dq_ref, dkv_ref, grad_ref, grad_low_ref, dgain_ref,
                       wq_ref, wkv_ref, wo_ref, do_ref, q_turn, do_turn, delta_ref, dq_acc, dkv_acc, dn_ref, send_kv, land_kv,
                       load_sem, send_sem, recv_sem):
    n = lax.axis_size("shard")
    me = lax.axis_index("shard")
    rows, width = x_ref.shape
    kv_width = wkv_ref.shape[1] // 2
    pairs = HEADS // KV_HEADS // 2
    scale = LOG2E * HEAD ** -0.5
    barrier = pltpu.get_barrier_semaphore()
    for d in range(1, n):
        @pl.when(me + d < n)
        def _(d=d):
            pl.semaphore_signal(barrier, inc=1, device_id={"shard": me + d}, device_id_type=MESH_IDS)
    loads = [pltpu.make_async_copy(src, dst, load_sem.at[k])
             for k, (src, dst) in enumerate(((w_o, wo_ref), (w_q, wq_ref), (w_kv, wkv_ref)))]
    for load in loads:
        load.start()

    def to_earlier(d):
        return remote(send_kv.at[d - 1], land_kv.at[d - 1], send_sem.at[d - 1], recv_sem.at[d - 1], {"shard": me - d})

    def from_later(d):
        return remote(send_kv.at[d - 1], land_kv.at[d - 1], send_sem.at[d - 1], recv_sem.at[d - 1], {"shard": me + d})

    chunk = 4 * LANES
    for at in range(0, width, LANES):
        q_turn[at:at + LANES, :] = q_ref[:, at:at + LANES].T
    loads[0].wait()
    for at in range(0, width, chunk):
        do_chunk = mm_t(da_ref[...], wo_ref[at:at + chunk, :]).astype(BF16)
        do_ref[:, at:at + chunk] = do_chunk
        do_turn[at:at + chunk, :] = do_chunk.T
    for j in range(HEADS):
        span = slice(j * HEAD, (j + 1) * HEAD)
        both = attended_turn[span, :].astype(F32) * do_turn[span, :].astype(F32)
        delta_ref[j:j + 1, :] = jnp.sum(both, axis=0, keepdims=True)
    dq_acc[...] = jnp.zeros_like(dq_acc)
    low_lane = lax.broadcasted_iota(jnp.int32, (rows, LANES), 1) < HEAD
    zero_rows = jnp.zeros((rows, LANES), BF16)

    def block(d, bias):
        for h in range(KV_HEADS):
            own = slice(h * HEAD, (h + 1) * HEAD)
            key = kv_ref[d, :, own]
            value = kv_ref[d, :, kv_width + h * HEAD:kv_width + (h + 1) * HEAD]
            key_t = kv_ref[d, :, h // 2 * LANES:(h // 2 + 1) * LANES].T[h % 2 * HEAD:(h % 2 + 1) * HEAD, :]
            dk = jnp.zeros((rows, LANES), F32)
            dv = jnp.zeros((rows, LANES), F32)
            for pair in range(h * pairs, (h + 1) * pairs):
                cols = slice(pair * LANES, (pair + 1) * LANES)
                q_rows = q_ref[:, cols]
                do_rows = do_ref[:, cols]
                for k in range(2):
                    j = 2 * pair + k
                    span = slice(j * HEAD, (j + 1) * HEAD)
                    lane = low_lane if k == 0 else jnp.logical_not(low_lane)
                    scores = mm(key, q_turn[span, :]) * scale
                    if bias is not None:
                        scores = scores + bias
                    prob = jnp.exp2(scores - lse_ref[j:j + 1, :])
                    dprob = mm(value, do_turn[span, :])
                    dscore = (prob * (dprob - delta_ref[j:j + 1, :])).astype(BF16)
                    dq_acc[span, :] += mm(key_t, dscore)
                    dk = dk + mm(dscore, jnp.where(lane, q_rows, zero_rows))
                    dv = dv + mm(prob.astype(BF16), jnp.where(lane, do_rows, zero_rows))
            dkv_acc[:, own] = (dk[:, :HEAD] + dk[:, HEAD:]) * HEAD ** -0.5
            dkv_acc[:, kv_width + h * HEAD:kv_width + (h + 1) * HEAD] = dv[:, :HEAD] + dv[:, HEAD:]

    @pl.when(me > 0)
    def _():
        pl.semaphore_wait(barrier, me)

    def earlier(i, carry):
        d = me - i
        block(d, None)
        send_kv[d - 1] = dkv_acc[...].astype(BF16)
        to_earlier(d).start()
        return carry

    lax.fori_loop(0, me, earlier, 0)
    key_pos = lax.broadcasted_iota(jnp.int32, (rows, rows), 0)
    query_pos = lax.broadcasted_iota(jnp.int32, (rows, rows), 1)
    block(0, jnp.where(key_pos <= query_pos, 0.0, NEG_FILL))

    loads[1].wait()
    loads[2].wait()
    for at in range(0, width, chunk):
        for col in range(at, at + chunk, LANES):
            dq_ref[:, col:col + LANES] = rotated(dq_acc[col:col + LANES, :].T * HEAD ** -0.5, cos_ref, sin_ref).astype(BF16)
    for at in range(0, width, chunk):
        dn_ref[:, at:at + chunk] = mm_t(dq_ref[...], wq_ref[at:at + chunk, :])
    for d in range(1, n):
        @pl.when(me + d < n)
        def _(d=d):
            from_later(d).wait_recv()
            dkv_acc[...] += land_kv[d - 1].astype(F32)
    dkv_ref[:, :kv_width] = rotated(dkv_acc[:, :kv_width], cos_ref, sin_ref).astype(BF16)
    dkv_ref[:, kv_width:] = dkv_acc[:, kv_width:].astype(BF16)
    for at in range(0, width, chunk):
        dn_ref[:, at:at + chunk] += mm_t(dkv_ref[...], wkv_ref[at:at + chunk, :])
    x = x_ref[...].astype(F32)
    root = inv_root_of(x)
    dnormed = dn_ref[...]
    scaled = dnormed * gain_ref[...]
    grad = dmid_ref[...] + root * scaled - x * (root * root * root * jnp.mean(scaled * x, axis=-1, keepdims=True))
    grad_ref[...] = grad
    grad_low_ref[...] = grad.astype(BF16)
    dgain_ref[...] = jnp.sum(dnormed * x * root, axis=0, keepdims=True)
    for d in range(1, n):
        @pl.when(me >= d)
        def _(d=d):
            to_earlier(d).wait_send()


def attend_back(da, dmid, x, gain, cos_table, back_sin, q, kv, attended, lse, w_q, w_kv, w_o, collective_id):
    n = lax.axis_size("shard")
    rows, width = x.shape
    kv_both = w_kv.shape[1]
    vmem = pl.BlockSpec(memory_space=pltpu.VMEM)
    anywhere = pl.BlockSpec(memory_space=pl.ANY)
    dma = pltpu.SemaphoreType.DMA
    flops = 2 * rows * width * (2 * width + kv_both) + 10 * rows * rows * n * width
    return pl.pallas_call(
        attend_back_kernel,
        in_specs=[vmem] * 10 + [anywhere] * 3,
        out_specs=[vmem] * 5,
        out_shape=[
            jax.ShapeDtypeStruct((rows, width), BF16),
            jax.ShapeDtypeStruct((rows, kv_both), BF16),
            jax.ShapeDtypeStruct((rows, width), F32),
            jax.ShapeDtypeStruct((rows, width), BF16),
            jax.ShapeDtypeStruct((1, width), F32),
        ],
        scratch_shapes=[
            pltpu.VMEM(w_q.shape, BF16), pltpu.VMEM(w_kv.shape, BF16), pltpu.VMEM(w_o.shape, BF16),
            pltpu.VMEM((rows, width), BF16), pltpu.VMEM((width, rows), BF16), pltpu.VMEM((width, rows), BF16),
            pltpu.VMEM((HEADS, rows), F32), pltpu.VMEM((width, rows), F32), pltpu.VMEM((rows, kv_both), F32),
            pltpu.VMEM((rows, width), F32),
            pltpu.VMEM((n - 1, rows, kv_both), BF16), pltpu.VMEM((n - 1, rows, kv_both), BF16),
            dma((3,)), dma((n - 1,)), dma((n - 1,)),
        ],
        compiler_params=pltpu.CompilerParams(
            collective_id=collective_id, has_side_effects=True, vmem_limit_bytes=58 * 1024 * 1024),
        cost_estimate=pl.CostEstimate(flops=flops, bytes_accessed=2 * width * (2 * width + kv_both), transcendentals=rows * rows * n * HEADS),
        name="attend_back",
    )(da, dmid, x, gain, cos_table, back_sin, q, kv, attended, lse, w_q, w_kv, w_o)


ROPE_BASE = 10000.0


def angles_for(positions):
    half_dim = HEAD // 2
    inverse = ROPE_BASE ** (-(jnp.arange(half_dim, dtype=F32) * 2.0 / HEAD))
    angle_grid = positions.astype(F32)[:, None] * inverse[None, :]
    return (jnp.cos(angle_grid), jnp.sin(angle_grid))


def passed_along(block, axis, by):
    length = lax.axis_size(axis)
    pairs = [(i, i + by) for i in range(length) if 0 <= i + by < length]
    return lax.ppermute(block, axis, pairs)


def gather_rows(weight):
    parts = lax.axis_size("rep")
    rows = weight.shape[0] // parts
    own = lax.dynamic_slice_in_dim(weight, lax.axis_index("rep") * rows, rows, 0)
    return lax.all_gather(own, ("shard", "rep"), axis=0, tiled=True)


Y_PAIRS = [(0, 2), (2, 0), (1, 3), (3, 1)]


def halves_of(grad_gate, grad_up):
    half = grad_gate.shape[1] // 2
    at = (1 - lax.axis_index("rep") // 2) * half
    parts = [lax.dynamic_slice_in_dim(term, at, half, 1) for term in (grad_gate, grad_up)]
    return lax.ppermute(jnp.concatenate(parts, axis=1), "rep", Y_PAIRS)


def layer_forward(stream_in, weights, tables, pending):
    w_q, w_kv, w_o, w_g, w_u, w_d, gains_wide = weights
    cos_table, sin_table = tables
    normed, queries, kv, attended, lse, middle = attend_block(
        stream_in, gains_wide[0:1], cos_table, sin_table, w_q, w_kv, w_o, 3)
    middle, pending = lax.optimization_barrier((middle, pending))
    result, normed_two, hidden, gate_fac, up_fac = ffn_fwd(middle, gains_wide[1:2], w_g, w_u, w_d)
    kept = {"stream": stream_in, "normed": normed, "queries": queries, "kv": kv, "attended": attended, "lse": lse,
            "middle": middle, "normed_two": normed_two, "hidden": hidden, "gate_fac": gate_fac, "up_fac": up_fac}
    return result, kept, pending


def layer_backward(grad_bf, kept, weights, tables, pending):
    w_q, w_kv, w_o, w_g, w_u, w_d, gains_wide = weights
    cos_table, sin_table = tables
    grad_gate, grad_up, grad_middle, grad_branch, gain_two = ffn_bwd(
        grad_bf, kept["middle"], gains_wide[1:2], kept["gate_fac"], kept["up_fac"], w_g, w_u, w_d)
    grad_branch, pending = lax.optimization_barrier((grad_branch, pending))
    halves_out = halves_of(grad_gate, grad_up)
    grad_query, grad_kv, grad_stream, grad_low, gain_one = attend_back(
        grad_branch, grad_middle, kept["stream"], gains_wide[0:1], cos_table, -sin_table, kept["queries"], kept["kv"],
        kept["attended"], kept["lse"], w_q, w_kv, w_o, 4)
    terms = (grad_query, grad_kv, grad_branch, grad_gate, grad_up, grad_bf, halves_out)
    return grad_stream, grad_low, terms, jnp.concatenate([gain_one, gain_two], axis=0), pending


def body(tokens, cotangent, live_counts, w_query, w_key, w_value, w_out, w_gate, w_up, w_down, norm_gains):
    section = lax.axis_index("section")
    slot_count, span_len, model_width = tokens.shape
    query_pos = lax.axis_index("shard") * span_len + jnp.arange(span_len, dtype=jnp.int32)
    cos_half, sin_half = angles_for(query_pos)
    tables = (jnp.tile(cos_half, (1, 4)), jnp.tile(jnp.concatenate([-sin_half, sin_half], axis=1), (1, 2)))
    live_mask = (jnp.arange(slot_count) < live_counts[0]).astype(F32)
    gain_rows = jnp.pad(norm_gains[0], ((0, 14), (0, -norm_gains.shape[2] % (4 * LANES))))
    shards = [w_query[0], jnp.concatenate([w_key[0], w_value[0]], axis=1), w_out[0], gain_rows, w_gate[0], w_up[0]]
    w_q, w_kv, w_o, gains, w_g, w_u = gather_weights(shards, [halves(shard.shape[1]) for shard in shards], 2, "gather_weights")
    down_shard, w_q = lax.optimization_barrier((w_down[0], w_q))
    w_d = gather_rows(down_shard)
    gain_blocks = gains.reshape(-1, 16, gain_rows.shape[1])[:, :2, :norm_gains.shape[2]]
    gains_wide = gain_blocks.transpose(1, 0, 2).reshape(2, model_width).astype(F32)
    weights = (w_q, w_kv, w_o, w_g, w_u, w_d, gains_wide)
    live_mask = live_mask.astype(BF16)
    zero_slot = jnp.zeros((span_len, model_width), BF16)
    ticks = slot_count + 1
    results, kept_all, others = [], [], []
    pending = []
    received = zero_slot
    for tick in range(ticks):
        slot_in = tokens[tick] * live_mask[tick] if tick < slot_count else zero_slot
        own_in = jnp.where(section == 0, slot_in, received)
        result, kept, pending = layer_forward(own_in, weights, tables, pending)
        others += pending
        pending = [lax.ppermute(kept["normed_two"], "rep", Y_PAIRS)]
        received = passed_along(result, "section", 1)
        results.append(result)
        kept_all.append(kept)
    first = section == 0
    acts = jnp.stack([jnp.where(first, results[j], results[j + 1]) for j in range(slot_count)])
    received = zero_slot
    streams, term_list, gain_total = [], [], 0.0
    for tick in range(ticks):
        slot_cot = cotangent[slot_count - 1 - tick] * live_mask[slot_count - 1 - tick] if tick < slot_count else zero_slot
        grad_bf = jnp.where(first, received, slot_cot)
        grad_stream, grad_low, terms, gain_grad, pending = layer_backward(
            grad_bf, kept_all[ticks - 1 - tick], weights, tables, pending)
        others += pending
        pending = [terms[6]]
        received = passed_along(grad_low, "section", -1)
        streams.append(grad_stream)
        term_list.append(terms)
        gain_total = gain_total + gain_grad
    grad_in = jnp.stack([
        jnp.where(first, streams[slot_count - j], streams[slot_count - 1 - j]) for j in range(slot_count)])

    others += pending
    normed_others, half_others = others[ticks - 1::-1], others[ticks:]

    def kept_by_tick(name):
        return [kept_all[ticks - 1 - tick][name] for tick in range(ticks)]

    def by_tick(index):
        return [terms[index] for terms in term_list]

    gate_sum, up_sum, qkv_sum, out_sum, down_sum, gain_sum = reduce_weights(
        jnp.pad(gain_total, ((0, 6), (0, 0))),
        [
            {"kind": "pair", "blocks": 1, "pace": 1, "delay": 3, "which": [0, 0],
             "lefts": [[kept_by_tick("normed_two"), normed_others]],
             "rights": [[by_tick(3), half_others], [by_tick(4), half_others]]},
            {"kind": "y", "blocks": 1, "pace": 2, "delay": 2, "which": [0, 1],
             "lefts": [[kept_by_tick("normed")], [kept_by_tick("attended")]],
             "rights": [[by_tick(0), by_tick(1)], [by_tick(2)]]},
            {"kind": "y", "blocks": 2, "pace": 2, "delay": 2, "which": [0],
             "lefts": [[kept_by_tick("hidden")]], "rights": [[by_tick(5)]]},
        ],
        slot_count, 1, "reduce_weights")
    kv_width = w_key.shape[2]
    outs = (
        qkv_sum[:, :model_width],
        qkv_sum[:, model_width:model_width + kv_width],
        qkv_sum[:, model_width + kv_width:],
        out_sum,
        gate_sum,
        up_sum,
        down_sum,
        gain_sum[:2],
    )
    return (acts[None], grad_in[None]) + tuple(out.astype(F32)[None] for out in outs)


def solution(mesh):
    tall = P("section", "shard", None)
    per_slot = P("section", "rep", "shard", None)
    return jax.shard_map(
        body,
        mesh=mesh,
        in_specs=(P("rep", "shard", None), P("rep", "shard", None), P("rep")) + (tall,) * 7 + (P("section", None, "shard"),),
        out_specs=(per_slot, per_slot) + (tall,) * 7 + (P("section", None, "shard"),),
        check_vma=False,
    )
```

```python
import functools, math
import jax
import jax.numpy as jnp
from jax import lax
from jax.sharding import PartitionSpec as P
from jax.experimental import pallas as pl
from jax.experimental.pallas import tpu as pltpu

HEADS = 32
KV_HEADS = 4
HEAD = 64
LOG2E = math.log2(math.e)
NEG_FILL = -1e30
F32, BF16 = jnp.float32, jnp.bfloat16


def mm(a, b):
    return jnp.dot(a, b, preferred_element_type=F32)


MESH_IDS = pl.DeviceIdType.MESH
LANES = 128
BUFS = 26


def remote(src, dst, send_sem, recv_sem, peer):
    return pltpu.make_async_remote_copy(src, dst, send_sem, recv_sem, device_id=peer, device_id_type=MESH_IDS)


def reduce_stages(kind, blocks, delay, segments, place, a_ref, b_ref, bufs):
    n, me, rep, right, core_peer, y_peer = place
    own_core, own_y = lax.rem(rep, 2), rep // 2
    paired = kind == "pair"
    (send_c, own, land_c, keep, send_y, land_y, send_z, land_z, send_f,
     sc_sem, rc_sem, cr_c, sy_sem, ry_sem, cr_y, sz_sem, rz_sem, ly_sem, sfy_sem, sfc_sem,
     rfy_sem, rfc_sem, sfw_sem, rfw_sem) = bufs
    rows = own.shape[2]
    depth = land_z.shape[1]
    span = a_ref.shape[3]
    items = b_ref.shape[2] // LANES * blocks
    starts = [first for _, _, first in segments]
    ends = starts[1:] + [items // blocks]

    def spot_of(out, first, r, p):
        width = out.shape[1] // 4
        column = pl.multiple_of(r * width + (p // blocks - first) * LANES, LANES)
        row = pl.multiple_of(lax.rem(p, blocks) * rows, 16)
        return out.at[pl.ds(row, rows), pl.ds(column, LANES)]

    def each_segment(p, fn):
        for (out, _, first), last in zip(segments, ends):
            if len(segments) == 1:
                fn(lambda r, out=out, first=first: spot_of(out, first, r, p))
                continue
            group = p // blocks

            @pl.when(jnp.logical_and(group >= first, group < last))
            def _(out=out, first=first):
                fn(lambda r: spot_of(out, first, r, p))

    def c_copy(a, s):
        return remote(send_c.at[a], land_c.at[s], sc_sem.at[a], rc_sem.at[s], core_peer)

    def y_copy(a, s):
        return remote(send_y.at[a], land_y.at[s], sy_sem.at[a], ry_sem.at[s], y_peer)

    def z_copy(a, s, p):
        b = lax.rem(p, depth)
        return remote(send_z.at[a], land_z.at[s, b], sz_sem.at[a], rz_sem.at[s, b], right)

    def f_local(a, spot):
        return pltpu.make_async_copy(send_f.at[a], spot(rep), ly_sem.at[a])

    def f_y(a, p, spot):
        return remote(send_f.at[a], spot(rep), sfy_sem.at[a], rfy_sem.at[p], y_peer)

    def f_core(a, p, spot):
        return remote(send_f.at[a], spot(rep), sfc_sem.at[a], rfc_sem.at[p], core_peer)

    def f_turn(a, p, spot):
        there = spot(rep + 2 - 4 * own_y)
        return remote(there, there, sfw_sem.at[a], rfw_sem.at[p], core_peer)

    def stage_zero(a, s, p):
        dest = lax.rem(me + 2 * n - 1 - s, n)
        row = pl.ds(pl.multiple_of((dest * blocks + lax.rem(p, blocks)) * rows, 16), rows)
        which = 0
        for (_, index, first) in segments[1:]:
            which = jnp.where(p // blocks >= first, index, which)
        column = pl.ds(pl.multiple_of(p // blocks * LANES, LANES), LANES)

        def product(r):
            total = None
            for k in range(a_ref.shape[1]):
                term = mm(a_ref[which, k, row, :], b_ref[r, k * span:(k + 1) * span, column])
                total = term if total is None else total + term
            return total
        tiles = range(1 if paired else 2)
        for y in tiles:
            send_c[a, y] = product(2 * y + 1 - own_core).astype(BF16)

        @pl.when(p >= 1)
        def _():
            pl.semaphore_wait(cr_c.at[s], 1)
        c_copy(a, s).start()
        for y in tiles:
            own[a, y] = product(2 * y + own_core)

    def credit(sem, s, p, peer):
        @pl.when(p + 1 < items)
        def _():
            pl.semaphore_signal(sem.at[s], inc=1, device_id=peer, device_id_type=MESH_IDS)

    def finish(a, p, total):
        send_f[a] = total.astype(BF16)

        def send(spot):
            f_y(a, p, spot).start()
            f_core(a, p, spot).start()
            f_local(a, spot).start()
        each_segment(p, send)

    def go_round(a, s, p, ref):
        @pl.when(s > 0)
        def _():
            z_copy(a, s - 1, p).wait_recv()
            ref[...] = ref[...] + land_z[s - 1, lax.rem(p, depth)].astype(F32)

        @pl.when(s < n - 1)
        def _():
            send_z[a] = ref[...].astype(BF16)
            z_copy(a, s, p).start()

        @pl.when(s == n - 1)
        def _():
            finish(a, p, ref[...])

    def stage_one_pair(a, s, p):
        c_copy(a, s).wait()
        own[a, 0] = own[a, 0] + land_c[s, 0].astype(F32)
        credit(cr_c, s, p, core_peer)
        go_round(a, s, p, own.at[a, 0])

    def stage_one_y(a, s, p):
        c_copy(a, s).wait()
        send_y[a] = (own[a, 1 - own_y] + land_c[s, 1 - own_y].astype(F32)).astype(BF16)

        @pl.when(p >= 1)
        def _():
            pl.semaphore_wait(cr_y.at[s], 1)
        y_copy(a, s).start()
        keep[a] = own[a, own_y] + land_c[s, own_y].astype(F32)
        credit(cr_c, s, p, core_peer)

    def stage_two_y(a, s, p):
        y_copy(a, s).wait()
        keep[a] = keep[a] + land_y[s].astype(F32)
        credit(cr_y, s, p, y_peer)
        go_round(a, s, p, keep.at[a])

    def turn_over(a, s, p):
        @pl.when(s < n - 1)
        def _():
            z_copy(a, s, p).wait_send()

        @pl.when(s == n - 1)
        def _():
            def turn(spot):
                f_local(a, spot).wait()
                f_core(a, p, spot).wait_send()
                f_y(a, p, spot).wait()
                f_turn(a, p, spot).start()
            each_segment(p, turn)

    def end_of(a, s, p):
        @pl.when(s == n - 1)
        def _():
            def end(spot):
                f_core(a, p, spot).wait_recv()
                f_turn(a, p, spot).wait()
            each_segment(p, end)

    if paired:
        return items, (stage_zero, stage_one_pair, turn_over, end_of)
    return items, (stage_zero, stage_one_y, stage_two_y, turn_over, end_of)


def gain_steps(place, gain_ref, out_ref, total, land_c, land_y, land_z, sends, lands):
    n, me, _, _, core_peer, y_peer = place
    chunk = out_ref.shape[1]

    def over_core():
        return remote(total, land_c, sends.at[0], lands.at[0], core_peer)

    def over_y():
        return remote(total, land_y, sends.at[1], lands.at[1], y_peer)

    def over_z(d):
        dest = lax.rem(me + d, n)
        part = total.at[:, pl.ds(pl.multiple_of(dest * chunk, LANES), chunk)]
        return remote(part, land_z.at[d - 1], sends.at[d + 1], lands.at[d + 1], {"shard": dest})

    def begin():
        total[...] = gain_ref[...]
        over_core().start()

    def add_core():
        over_core().wait()
        total[...] = total[...] + land_c[...]
        over_y().start()

    def add_y():
        over_y().wait()
        total[...] = total[...] + land_y[...]
        for d in range(1, n):
            over_z(d).start()

    def add_z():
        result = total[:, pl.ds(pl.multiple_of(me * chunk, LANES), chunk)]
        for d in range(1, n):
            over_z(d).wait()
            result = result + land_z[d - 1]
        out_ref[...] = result

    return ((3, begin), (30, add_core), (60, add_y), (90, add_z))


def reduce_kernel(streams, slots, *refs):
    n = lax.axis_size("shard")
    me = lax.axis_index("shard")
    rep = lax.axis_index("rep")
    section = lax.axis_index("section")
    right = {"shard": lax.rem(me + 1, n)}
    core_peer = {"rep": rep + 1 - 2 * lax.rem(rep, 2)}
    y_peer = {"rep": rep + 2 - 4 * (rep // 2)}
    place = (n, me, rep, right, core_peer, y_peer)

    refs = list(refs)
    gain_ref = refs.pop(0)

    def taken(tree):
        return [taken(x) for x in tree] if isinstance(tree, list) else refs.pop(0)
    lefts = [taken(stream["lefts"]) for stream in streams]
    rights = [taken(stream["rights"]) for stream in streams]
    outs = [[refs.pop(0) for _ in stream["rights"]] for stream in streams]
    gain_out = refs.pop(0)
    per = [[refs.pop(0) for _ in range(BUFS)] for _ in streams]
    load_sem = refs.pop(0)
    timed = gain_steps(place, gain_ref, gain_out, *refs)

    barrier = pltpu.get_barrier_semaphore()
    for peer in [{"shard": lax.rem(me + d, n)} for d in range(1, n)] + [core_peer, y_peer]:
        pl.semaphore_signal(barrier, inc=1, device_id=peer, device_id_type=MESH_IDS)

    def load_all(at_section):
        loads = []

        def load(src, dst):
            loads.append(pltpu.make_async_copy(src, dst, load_sem.at[len(loads)]))
            loads[-1].start()

        def tick_of(ticks, j):
            return ticks[slots - j if at_section == 0 else slots - 1 - j]
        for stream, left_refs, right_refs, bufs in zip(streams, lefts, rights, per):
            a_ref, b_ref = bufs[0], bufs[1]
            for k, groups in enumerate(left_refs):
                for g, ticks in enumerate(groups):
                    for j in range(slots):
                        load(tick_of(ticks, j), a_ref.at[k, g * slots + j])
            base = 0
            for segment in right_refs:
                if stream["kind"] == "pair":
                    mine, other = segment
                    quarter = mine[0].shape[1] // 4
                    for c in range(2):
                        column = pl.ds(pl.multiple_of((rep // 2 * 2 + c) * quarter, LANES), quarter)
                        for g, ticks in enumerate((mine, other)):
                            for j in range(slots):
                                tick = tick_of(ticks, j)
                                span = tick.shape[0]
                                at = (g * slots + j) * span
                                load(tick.at[:, column] if g == 0 else tick.at[:, 2 * base + c * quarter:2 * base + (c + 1) * quarter],
                                     b_ref.at[c, at:at + span, base:base + quarter])
                    base += quarter
                    continue
                quarter = sum(ticks[0].shape[1] for ticks in segment) // 4
                for r in range(4):
                    at = 0
                    for ticks in segment:
                        width = ticks[0].shape[1]
                        lo, hi = max(r * quarter, at), min((r + 1) * quarter, at + width)
                        if lo < hi:
                            for j in range(slots):
                                tick = tick_of(ticks, j)
                                span = tick.shape[0]
                                load(tick.at[:, lo - at:hi - at],
                                     b_ref.at[r, j * span:(j + 1) * span, base + lo - r * quarter:base + hi - r * quarter])
                        at += width
                base += quarter
        for copy in loads:
            copy.wait()

    for value in range(2):
        @pl.when(section == value)
        def _(value=value):
            load_all(value)
    pl.semaphore_wait(barrier, n + 1)

    work, last = [], 0
    for stream, segs, bufs in zip(streams, outs, per):
        delay = stream["delay"]
        items, fns = reduce_stages(
            stream["kind"], stream["blocks"], delay,
            [(out, index, first) for out, index, first in zip(segs, stream["which"], stream["firsts"])],
            place, bufs[0], bufs[1], bufs[2:])
        pace = stream["pace"]
        work.append((pace, delay, items, fns))
        last = max(last, pace * (n * (items + n - 1) + (len(fns) - 1) * delay))

    def step(i, carry):
        for k in (4, 3, 2, 1, 0):
            for pace, delay, items, fns in work:
                if k >= len(fns):
                    continue
                v = i // pace - delay * k
                s = lax.rem(v + n * delay * 4, n)
                p = (v - s) // n - s
                fine = jnp.logical_and(jnp.logical_and(v >= 0, lax.rem(i, pace) == 0), jnp.logical_and(p >= 0, p < items))

                @pl.when(fine)
                def _(s=s, p=p, v=v, fn=fns[k], delay=delay):
                    fn(lax.rem(v, delay), s, p)
        for at, fn in timed:
            pl.when(i == at)(fn)
        return carry

    lax.fori_loop(0, last, step, 0)


def reduce_weights(gain, streams, slots, collective_id, name):
    n = lax.axis_size("shard")
    operands, out_shapes, scratch, flops, moved, plans, loads = [], [], [], 0, 0, [], 0
    dma, regular = pltpu.SemaphoreType.DMA, pltpu.SemaphoreType.REGULAR

    def listed(tree):
        if isinstance(tree, list):
            return [listed(x) for x in tree]
        operands.append(tree)
        return None
    left_plans = [listed(stream["lefts"]) for stream in streams]
    right_plans = [listed(stream["rights"]) for stream in streams]
    for stream, left_plan, right_plan in zip(streams, left_plans, right_plans):
        paired = stream["kind"] == "pair"
        blocks, delay = stream["blocks"], stream["delay"]
        height, span = stream["lefts"][0][0][0].shape
        height //= n
        chunks = len(stream["lefts"][0]) * slots
        firsts, at = [], 0
        for segment in stream["rights"]:
            width = segment[0][0].shape[1] if paired else sum(ticks[0].shape[1] for ticks in segment)
            firsts.append(at)
            at += width // 4 // LANES
            out_shapes.append(jax.ShapeDtypeStruct((height, width), BF16))
            flops += 2 * span * slots * height * n * width
            moved += height * width * 4
            loads += 4 * slots * len(segment)
        loads += len(stream["lefts"]) * chunks
        items = at * blocks
        depth = min(items, n + 2)
        tile = (height // blocks, LANES)
        both = 1 if paired else 2
        few = (16, LANES)
        scratch += [
            pltpu.VMEM((len(stream["lefts"]), chunks, height * n, span), BF16),
            pltpu.VMEM((2 * both, chunks * span, at * LANES), BF16),
            pltpu.VMEM((delay, both) + tile, BF16),
            pltpu.VMEM((delay, both) + tile, F32),
            pltpu.VMEM((n, both) + tile, BF16),
            pltpu.VMEM((1,) + few if paired else (delay,) + tile, F32),
            pltpu.VMEM((1,) + few if paired else (delay,) + tile, BF16),
            pltpu.VMEM((1,) + few if paired else (n,) + tile, BF16),
            pltpu.VMEM((delay,) + tile, BF16),
            pltpu.VMEM((n - 1, depth) + tile, BF16),
            pltpu.VMEM((delay,) + tile, BF16),
            dma((delay,)), dma((n,)), regular((n,)),
            dma((delay,)), dma((n,)), regular((n,)),
            dma((delay,)), dma((n - 1, depth)),
            dma((delay,)), dma((delay,)), dma((delay,)),
            dma((items,)), dma((items,)), dma((delay,)), dma((items,)),
        ]
        plans.append({
            "kind": stream["kind"], "blocks": blocks, "delay": delay, "pace": stream["pace"], "which": tuple(stream["which"]),
            "firsts": tuple(firsts), "lefts": left_plan, "rights": right_plan})
    chunk = gain.shape[1] // n
    out_shapes.append(jax.ShapeDtypeStruct((gain.shape[0], chunk), F32))
    scratch += [dma((loads,))] + [pltpu.VMEM(gain.shape, F32)] * 3
    scratch += [pltpu.VMEM((n - 1, gain.shape[0], chunk), F32), dma((n + 1,)), dma((n + 1,))]
    in_vmem = pl.BlockSpec(memory_space=pltpu.VMEM)
    anywhere = pl.BlockSpec(memory_space=pl.ANY)
    return pl.pallas_call(
        functools.partial(reduce_kernel, plans, slots),
        in_specs=[in_vmem] + [anywhere] * len(operands),
        out_specs=[anywhere] * (len(out_shapes) - 1) + [in_vmem],
        out_shape=out_shapes,
        scratch_shapes=scratch,
        compiler_params=pltpu.CompilerParams(
            collective_id=collective_id, has_side_effects=True, vmem_limit_bytes=60 * 1024 * 1024),
        cost_estimate=pl.CostEstimate(flops=flops, bytes_accessed=moved, transcendentals=0),
        name=name,
    )(gain, *operands)


def gather_kernel(splits, x_ref, cos_ref, sin_ref, *refs):
    n = lax.axis_size("shard")
    me = lax.axis_index("shard")
    rep = lax.axis_index("rep")
    right = {"shard": lax.rem(me + 1, n)}
    core_peer = {"rep": rep + 1 - 2 * lax.rem(rep, 2)}
    y_rep = rep + 2 - 4 * (rep // 2)
    y_peer = {"rep": y_rep}
    count = len(splits)
    early = 4
    ins, outs, refs = refs[:count], refs[count:2 * count], refs[2 * count:]
    attend_outs, refs = refs[:6], refs[6:]
    attend_refs, refs = refs[:13], refs[13:]
    holds, refs = refs[:count], refs[count:]
    zs, zr, ys, yr, cs, cr, ts, tr, local, gain_blocks, gain_row, gain_sem = refs

    barrier = pltpu.get_barrier_semaphore()
    for peer in [{"shard": lax.rem(me + d, n)} for d in range(1, n)] + [core_peer, y_peer]:
        pl.semaphore_signal(barrier, inc=1, device_id=peer, device_id_type=MESH_IDS)

    pieces = []
    for k, split in enumerate(splits):
        at = 0
        for width in split:
            pieces.append((k, at, width))
            at += width
    first = [piece for piece in range(len(pieces)) if pieces[piece][0] < early]
    second = [piece for piece in range(len(pieces)) if pieces[piece][0] >= early]

    def own_load(k):
        return pltpu.make_async_copy(ins[k], holds[k], local.at[0, k])

    def own_store(k):
        rows = ins[k].shape[0]
        return pltpu.make_async_copy(holds[k], outs[k].at[pl.ds(pl.multiple_of(me * rows, 16), rows), :], local.at[1, k])

    def spot(piece, back, r):
        k, at, width = pieces[piece]
        rows = ins[k].shape[0]
        block = lax.rem(me + n - back, n)
        column = pl.multiple_of(r * (ins[k].shape[1] // 4) + at, LANES)
        return outs[k].at[pl.ds(pl.multiple_of(block * rows, 16), rows), pl.ds(column, width)]

    def z_copy(piece, s):
        k, at, width = pieces[piece]
        there = spot(piece, s, rep)
        column = pl.multiple_of(rep * (ins[k].shape[1] // 4) + at, LANES)
        here = ins[k].at[:, pl.ds(column, width)] if s == 0 else there
        return remote(here, there, zs.at[piece, s], zr.at[piece, s], right)

    def y_copy(piece, s):
        there = spot(piece, s, rep)
        return remote(there, there, ys.at[piece, s - 1], yr.at[piece, s - 1], y_peer)

    def c_copy(piece, s):
        there = spot(piece, s, rep)
        return remote(there, there, cs.at[piece, s - 1], cr.at[piece, s - 1], core_peer)

    def t_copy(piece, s):
        there = spot(piece, s, y_rep)
        return remote(there, there, ts.at[piece, s - 1], tr.at[piece, s - 1], core_peer)

    def begin(group):
        for piece in group:
            z_copy(piece, 0).start()

    def own_rows(which):
        for k in which:
            own_load(k).start()
        for k in which:
            own_load(k).wait()
            own_store(k).start()

    def turn(piece, s):
        y_copy(piece, s).wait_recv()
        t_copy(piece, s).start()

    def pass_on(group, before_last):
        before = []
        for s in range(1, n):
            if s == n - 1:
                before_last()
            for piece in group:
                z_copy(piece, s - 1).wait_recv()
                if s < n - 1:
                    z_copy(piece, s).start()
                y_copy(piece, s).start()
                c_copy(piece, s).start()
                before.append((piece, s))
                if len(before) > 1:
                    turn(*before[-2])
        turn(*before[-1])
        return before

    def arrived(which, before):
        for k in which:
            own_store(k).wait()
        for piece, s in before:
            c_copy(piece, s).wait_recv()
            t_copy(piece, s).wait_recv()

    pl.semaphore_wait(barrier, n + 1)
    begin(first)
    own_rows(range(early))

    def start_second():
        begin(second)
        for k in range(early, count):
            own_load(k).start()
    before = pass_on(first, lambda: None)
    arrived(range(early), before)
    load = pltpu.make_async_copy(outs[3], gain_blocks, gain_sem.at[0])
    load.start()
    load.wait()
    rows = ins[3].shape[0]
    part = x_ref.shape[1] // n
    for k in range(n):
        gain_row[:, k * part:(k + 1) * part] = gain_blocks[k * rows:k * rows + 1, :part].astype(F32)
    attend_steps(lambda: None, start_second, x_ref, gain_row, cos_ref, sin_ref, outs[0], outs[1], outs[2], *attend_outs, *attend_refs)
    for k in range(early, count):
        own_load(k).wait()
        own_store(k).start()
    after = pass_on(second, lambda: None)
    arrived(range(early, count), after)
    for piece, s in before + after:
        z_copy(piece, s - 1).wait_send()
        y_copy(piece, s).wait_send()
        c_copy(piece, s).wait_send()
        t_copy(piece, s).wait_send()


def gather_weights(x, cos_table, sin_table, shards, splits, collective_id, name):
    n = lax.axis_size("shard")
    rows, width = x.shape
    kv_both = shards[1].shape[1]
    dma = pltpu.SemaphoreType.DMA
    pieces = sum(len(split) for split in splits)
    pair = dma((pieces, n - 1))
    anywhere = pl.BlockSpec(memory_space=pl.ANY)
    vmem = pl.BlockSpec(memory_space=pltpu.VMEM)
    moved = 2 * n * sum(shard.shape[0] * shard.shape[1] for shard in shards)
    results = pl.pallas_call(
        functools.partial(gather_kernel, splits),
        in_specs=[vmem] * 3 + [anywhere] * len(shards),
        out_specs=[anywhere] * len(shards) + [vmem] * 6,
        out_shape=[jax.ShapeDtypeStruct((n * shard.shape[0], shard.shape[1]), BF16) for shard in shards]
        + attend_outputs(rows, width, n, kv_both),
        scratch_shapes=attend_scratch(rows, width, n, kv_both) + [pltpu.VMEM(shard.shape, BF16) for shard in shards]
        + [pair] * 8 + [dma((2, len(shards))), pltpu.VMEM((n * shards[3].shape[0], shards[3].shape[1]), BF16),
                        pltpu.VMEM((1, width), F32), dma((1,))],
        compiler_params=pltpu.CompilerParams(collective_id=collective_id, has_side_effects=True, vmem_limit_bytes=60 * 1024 * 1024),
        cost_estimate=pl.CostEstimate(flops=4 * rows * width * width, bytes_accessed=moved * 4, transcendentals=0),
        name=name,
    )(x, cos_table, sin_table, *shards)
    return results[:len(shards)], results[len(shards):]


def halves(width):
    quarter = width // 4
    first = (quarter // LANES + 1) // 2 * LANES
    return (first, quarter - first) if quarter > first else (quarter,)


EPSILON = 1e-05
FF_TILE = 512


def mm_t(a, b):
    return lax.dot_general(a, b, (((1,), (1,)), ((), ())), preferred_element_type=F32)


def inv_root_of(rows):
    return lax.rsqrt(jnp.mean(rows * rows, axis=-1, keepdims=True) + EPSILON)


def ffn_fwd_kernel(mid_ref, gain_ref, w_g, w_u, w_d, out_ref, normed_turn, hidden_turn, gate_fac, up_fac, acc, normed_ref):
    step = pl.program_id(0)

    @pl.when(step == 0)
    def _():
        mid = mid_ref[...]
        normed_ref[...] = (mid * inv_root_of(mid) * gain_ref[...]).astype(BF16)
        acc[...] = mid
        for at in range(0, mid.shape[1], LANES):
            normed_turn[at:at + LANES, :] = normed_ref[:, at:at + LANES].T

    gate = mm(normed_ref[...], w_g[...])
    up = mm(normed_ref[...], w_u[...])
    sig = jax.nn.sigmoid(gate)
    act = gate * sig
    hidden = (act * up).astype(BF16)
    hidden_turn[...] = hidden.T
    up_fac[...] = act.astype(BF16)
    gate_fac[...] = (up * sig * (1.0 + gate * (1.0 - sig))).astype(BF16)
    acc[...] += mm(hidden, w_d[...])

    @pl.when(step == pl.num_programs(0) - 1)
    def _():
        out_ref[...] = acc[...].astype(BF16)


def ffn_fwd(middle, gain, w_g, w_u, w_d):
    rows, width = middle.shape
    ff = w_g.shape[1]
    whole = pl.BlockSpec((rows, width), lambda i: (0, 0))
    part = pl.BlockSpec((rows, FF_TILE), lambda i: (0, i))
    tall = pl.BlockSpec((width, FF_TILE), lambda i: (0, i))
    wide = jax.ShapeDtypeStruct((rows, ff), BF16)
    return pl.pallas_call(
        ffn_fwd_kernel,
        grid=(ff // FF_TILE,),
        in_specs=[whole, pl.BlockSpec((1, width), lambda i: (0, 0)), tall, tall, pl.BlockSpec((FF_TILE, width), lambda i: (i, 0))],
        out_specs=[whole, pl.BlockSpec((width, rows), lambda i: (0, 0)), pl.BlockSpec((FF_TILE, rows), lambda i: (i, 0)), part, part],
        out_shape=[jax.ShapeDtypeStruct((rows, width), BF16), jax.ShapeDtypeStruct((width, rows), BF16),
                   jax.ShapeDtypeStruct((ff, rows), BF16), wide, wide],
        scratch_shapes=[pltpu.VMEM((rows, width), F32), pltpu.VMEM((rows, width), BF16)],
        compiler_params=pltpu.CompilerParams(vmem_limit_bytes=58 * 1024 * 1024),
        cost_estimate=pl.CostEstimate(flops=6 * rows * width * ff, bytes_accessed=6 * width * ff, transcendentals=rows * ff),
        name="ffn_fwd",
    )(middle, gain, w_g, w_u, w_d)


def ffn_bwd_kernel(grad_ref, mid_ref, gain_ref, gate_fac, up_fac, w_g, w_u, w_d,
                   dgate_ref, dup_ref, dmid_ref, da_ref, dgain_ref, acc):
    step = pl.program_id(0)
    dhidden = mm_t(grad_ref[...], w_d[...])
    dgate = (dhidden * gate_fac[...].astype(F32)).astype(BF16)
    dup = (dhidden * up_fac[...].astype(F32)).astype(BF16)
    dgate_ref[...] = dgate
    dup_ref[...] = dup
    term = mm_t(dgate, w_g[...]) + mm_t(dup, w_u[...])

    @pl.when(step == 0)
    def _():
        acc[...] = term

    @pl.when(step > 0)
    def _():
        acc[...] += term

    @pl.when(step == pl.num_programs(0) - 1)
    def _():
        mid = mid_ref[...]
        root = inv_root_of(mid)
        dnormed = acc[...]
        scaled = dnormed * gain_ref[...]
        dmid = grad_ref[...].astype(F32) + root * scaled - mid * (root * root * root * jnp.mean(scaled * mid, axis=-1, keepdims=True))
        dmid_ref[...] = dmid
        da_ref[...] = dmid.astype(BF16)
        dgain_ref[...] = jnp.sum(dnormed * mid * root, axis=0, keepdims=True)


def ffn_bwd(grad, middle, gain, gate_fac, up_fac, w_g, w_u, w_d):
    rows, width = middle.shape
    ff = w_g.shape[1]
    whole = pl.BlockSpec((rows, width), lambda i: (0, 0))
    flat = pl.BlockSpec((1, width), lambda i: (0, 0))
    part = pl.BlockSpec((rows, FF_TILE), lambda i: (0, i))
    tall = pl.BlockSpec((width, FF_TILE), lambda i: (0, i))
    wide = jax.ShapeDtypeStruct((rows, ff), BF16)
    return pl.pallas_call(
        ffn_bwd_kernel,
        grid=(ff // FF_TILE,),
        in_specs=[whole, whole, flat, part, part, tall, tall, pl.BlockSpec((FF_TILE, width), lambda i: (i, 0))],
        out_specs=[part, part, whole, whole, flat],
        out_shape=[wide, wide, jax.ShapeDtypeStruct((rows, width), F32), jax.ShapeDtypeStruct((rows, width), BF16),
                   jax.ShapeDtypeStruct((1, width), F32)],
        scratch_shapes=[pltpu.VMEM((rows, width), F32)],
        compiler_params=pltpu.CompilerParams(vmem_limit_bytes=58 * 1024 * 1024),
        cost_estimate=pl.CostEstimate(flops=6 * rows * width * ff, bytes_accessed=6 * width * ff, transcendentals=0),
        name="ffn_bwd",
    )(grad, middle, gain, gate_fac, up_fac, w_g, w_u, w_d)


def rotated(rows, cos_ref, sin_ref):
    width = rows.shape[1]
    low_half = lax.rem(lax.broadcasted_iota(jnp.int32, rows.shape, 1), HEAD) < HEAD // 2
    swapped = jnp.where(low_half, pltpu.roll(rows, width - HEAD // 2, 1), pltpu.roll(rows, HEAD // 2, 1))
    reps = width // LANES
    return rows * jnp.tile(cos_ref[...], (1, reps)) + swapped * jnp.tile(sin_ref[...], (1, reps))


def attend_steps(greeted, sent, x_ref, gain_ref, cos_ref, sin_ref, w_q, w_kv, w_o,
                 normed_turn, q_ref, kv_ref, attended_turn, lse_ref, mid_ref,
                 normed_ref, attended_ref, wq_ref, wkv_ref, wo_ref, q_turn, acc, top_ref, total_ref, land,
                 load_sem, send_sem, recv_sem):
    n = lax.axis_size("shard")
    me = lax.axis_index("shard")
    rows, width = x_ref.shape
    kv_width = wkv_ref.shape[1] // 2
    group = HEADS // KV_HEADS
    scale = LOG2E * HEAD ** -0.5
    loads = [pltpu.make_async_copy(src, dst, load_sem.at[k])
             for k, (src, dst) in enumerate(((w_kv, wkv_ref), (w_q, wq_ref), (w_o, wo_ref)))]
    for load in loads:
        load.start()

    def to_later(d):
        return remote(land.at[0], land.at[d], send_sem.at[d - 1], recv_sem.at[d - 1], {"shard": me + d})

    def from_earlier(d):
        return remote(land.at[0], land.at[d], send_sem.at[d - 1], recv_sem.at[d - 1], {"shard": me - d})

    x = x_ref[...].astype(F32)
    normed_ref[...] = (x * inv_root_of(x) * gain_ref[...]).astype(BF16)
    loads[0].wait()
    kv = mm(normed_ref[...], wkv_ref[...])
    land[0, :, :kv_width] = rotated(kv[:, :kv_width], cos_ref, sin_ref).astype(BF16)
    land[0, :, kv_width:] = kv[:, kv_width:].astype(BF16)
    greeted()
    for d in range(1, n):
        @pl.when(me + d < n)
        def _(d=d):
            to_later(d).start()
    sent()
    loads[1].wait()
    chunk = 4 * LANES
    for at in range(0, width, chunk):
        q_chunk = rotated(mm(normed_ref[...], wq_ref[:, at:at + chunk]), cos_ref, sin_ref).astype(BF16)
        q_ref[:, at:at + chunk] = q_chunk
        q_turn[at:at + chunk, :] = q_chunk.T

    def heads_of(d):
        for h in range(KV_HEADS):
            key = land[d, :, h * HEAD:(h + 1) * HEAD]
            pair_t = land[d, :, kv_width + h // 2 * LANES:kv_width + (h // 2 + 1) * LANES].T
            value_t = pair_t[h % 2 * HEAD:(h % 2 + 1) * HEAD, :]
            for j in range(h * group, (h + 1) * group):
                yield j, key, value_t

    key_pos = lax.broadcasted_iota(jnp.int32, (rows, rows), 0)
    query_pos = lax.broadcasted_iota(jnp.int32, (rows, rows), 1)
    bias = jnp.where(key_pos <= query_pos, 0.0, NEG_FILL)
    for j, key, value_t in heads_of(0):
        span = slice(j * HEAD, (j + 1) * HEAD)
        scores = mm(key, q_turn[span, :]) * scale + bias
        top = jnp.max(scores, axis=0, keepdims=True)
        prob = jnp.exp2(scores - top)
        top_ref[j:j + 1, :] = top
        total_ref[j:j + 1, :] = jnp.sum(prob, axis=0, keepdims=True)
        acc[span, :] = mm(value_t, prob.astype(BF16))

    def earlier(d, carry):
        from_earlier(d).wait_recv()
        for j, key, value_t in heads_of(d):
            span = slice(j * HEAD, (j + 1) * HEAD)
            scores = mm(key, q_turn[span, :]) * scale
            old = top_ref[j:j + 1, :]
            top = jnp.maximum(old, jnp.max(scores, axis=0, keepdims=True))
            fade = jnp.exp2(old - top)
            prob = jnp.exp2(scores - top)
            top_ref[j:j + 1, :] = top
            total_ref[j:j + 1, :] = total_ref[j:j + 1, :] * fade + jnp.sum(prob, axis=0, keepdims=True)
            acc[span, :] = acc[span, :] * fade + mm(value_t, prob.astype(BF16))
        return carry

    lax.fori_loop(1, me + 1, earlier, 0)
    total = total_ref[...]
    lse_ref[...] = top_ref[...] + jnp.log2(total)
    total_ref[...] = 1.0 / total
    for pair in range(HEADS // 2):
        col = pair * LANES
        halves_t = [acc[col + k * HEAD:col + (k + 1) * HEAD, :] * total_ref[2 * pair + k:2 * pair + k + 1, :] for k in range(2)]
        both_t = jnp.concatenate(halves_t, axis=0).astype(BF16)
        attended_turn[col:col + LANES, :] = both_t
        attended_ref[:, col:col + LANES] = both_t.T
        normed_turn[col:col + LANES, :] = normed_ref[:, col:col + LANES].T
    for d in range(n):
        @pl.when(me >= d)
        def _(d=d):
            kv_ref[d] = land[d]
    loads[2].wait()
    for at in range(0, width, chunk):
        mid_ref[:, at:at + chunk] = x_ref[:, at:at + chunk].astype(F32) + mm(attended_ref[...], wo_ref[:, at:at + chunk])
    for d in range(1, n):
        @pl.when(me + d < n)
        def _(d=d):
            to_later(d).wait_send()


def attend_block_kernel(*refs):
    n = lax.axis_size("shard")
    me = lax.axis_index("shard")
    barrier = pltpu.get_barrier_semaphore()
    for d in range(1, n):
        @pl.when(me >= d)
        def _(d=d):
            pl.semaphore_signal(barrier, inc=1, device_id={"shard": me - d}, device_id_type=MESH_IDS)

    def greeted():
        @pl.when(me < n - 1)
        def _():
            pl.semaphore_wait(barrier, n - 1 - me)
    attend_steps(greeted, lambda: None, *refs)


def attend_scratch(rows, width, n, kv_both):
    dma = pltpu.SemaphoreType.DMA
    return [
        pltpu.VMEM((rows, width), BF16), pltpu.VMEM((rows, width), BF16),
        pltpu.VMEM((width, width), BF16), pltpu.VMEM((width, kv_both), BF16), pltpu.VMEM((width, width), BF16),
        pltpu.VMEM((width, rows), BF16), pltpu.VMEM((width, rows), F32),
        pltpu.VMEM((HEADS, rows), F32), pltpu.VMEM((HEADS, rows), F32),
        pltpu.VMEM((n, rows, kv_both), BF16),
        dma((3,)), dma((n - 1,)), dma((n - 1,)),
    ]


def attend_outputs(rows, width, n, kv_both):
    return [
        jax.ShapeDtypeStruct((width, rows), BF16),
        jax.ShapeDtypeStruct((rows, width), BF16),
        jax.ShapeDtypeStruct((n, rows, kv_both), BF16),
        jax.ShapeDtypeStruct((width, rows), BF16),
        jax.ShapeDtypeStruct((HEADS, rows), F32),
        jax.ShapeDtypeStruct((rows, width), F32),
    ]


def attend_block(x, gain, cos_table, sin_table, w_q, w_kv, w_o, collective_id):
    n = lax.axis_size("shard")
    rows, width = x.shape
    kv_both = w_kv.shape[1]
    vmem = pl.BlockSpec(memory_space=pltpu.VMEM)
    anywhere = pl.BlockSpec(memory_space=pl.ANY)
    flops = 2 * rows * width * (2 * width + kv_both) + 4 * rows * rows * n * width
    return pl.pallas_call(
        attend_block_kernel,
        in_specs=[vmem] * 4 + [anywhere] * 3,
        out_specs=[vmem] * 6,
        out_shape=attend_outputs(rows, width, n, kv_both),
        scratch_shapes=attend_scratch(rows, width, n, kv_both),
        compiler_params=pltpu.CompilerParams(
            collective_id=collective_id, has_side_effects=True, vmem_limit_bytes=56 * 1024 * 1024),
        cost_estimate=pl.CostEstimate(flops=flops, bytes_accessed=2 * width * (2 * width + kv_both), transcendentals=rows * rows * n * HEADS),
        name="attend_block",
    )(x, gain, cos_table, sin_table, w_q, w_kv, w_o)


def attend_back_kernel(da_ref, dmid_ref, x_ref, gain_ref, cos_ref, sin_ref, q_ref, kv_ref, attended_turn, lse_ref, w_q, w_kv, w_o,
                       dq_ref, dkv_ref, grad_ref, grad_low_ref, dgain_ref,
                       wq_ref, wkv_ref, wo_ref, do_ref, q_turn, do_turn, delta_ref, dq_acc, dkv_acc, dn_ref, send_kv, land_kv,
                       load_sem, send_sem, recv_sem):
    n = lax.axis_size("shard")
    me = lax.axis_index("shard")
    rows, width = x_ref.shape
    kv_width = wkv_ref.shape[1] // 2
    pairs = HEADS // KV_HEADS // 2
    scale = LOG2E * HEAD ** -0.5
    barrier = pltpu.get_barrier_semaphore()
    for d in range(1, n):
        @pl.when(me + d < n)
        def _(d=d):
            pl.semaphore_signal(barrier, inc=1, device_id={"shard": me + d}, device_id_type=MESH_IDS)
    loads = [pltpu.make_async_copy(src, dst, load_sem.at[k])
             for k, (src, dst) in enumerate(((w_o, wo_ref), (w_q, wq_ref), (w_kv, wkv_ref)))]
    for load in loads:
        load.start()

    def to_earlier(d):
        return remote(send_kv.at[d - 1], land_kv.at[d - 1], send_sem.at[d - 1], recv_sem.at[d - 1], {"shard": me - d})

    def from_later(d):
        return remote(send_kv.at[d - 1], land_kv.at[d - 1], send_sem.at[d - 1], recv_sem.at[d - 1], {"shard": me + d})

    chunk = 4 * LANES
    for at in range(0, width, LANES):
        q_turn[at:at + LANES, :] = q_ref[:, at:at + LANES].T
    loads[0].wait()
    for at in range(0, width, chunk):
        do_chunk = mm_t(da_ref[...], wo_ref[at:at + chunk, :]).astype(BF16)
        do_ref[:, at:at + chunk] = do_chunk
        do_turn[at:at + chunk, :] = do_chunk.T
    for j in range(HEADS):
        span = slice(j * HEAD, (j + 1) * HEAD)
        both = attended_turn[span, :].astype(F32) * do_turn[span, :].astype(F32)
        delta_ref[j:j + 1, :] = jnp.sum(both, axis=0, keepdims=True)
    dq_acc[...] = jnp.zeros_like(dq_acc)
    low_lane = lax.broadcasted_iota(jnp.int32, (rows, LANES), 1) < HEAD
    zero_rows = jnp.zeros((rows, LANES), BF16)

    def block(d, bias):
        for h in range(KV_HEADS):
            own = slice(h * HEAD, (h + 1) * HEAD)
            key = kv_ref[d, :, own]
            value = kv_ref[d, :, kv_width + h * HEAD:kv_width + (h + 1) * HEAD]
            key_t = kv_ref[d, :, h // 2 * LANES:(h // 2 + 1) * LANES].T[h % 2 * HEAD:(h % 2 + 1) * HEAD, :]
            dk = jnp.zeros((rows, LANES), F32)
            dv = jnp.zeros((rows, LANES), F32)
            for pair in range(h * pairs, (h + 1) * pairs):
                cols = slice(pair * LANES, (pair + 1) * LANES)
                q_rows = q_ref[:, cols]
                do_rows = do_ref[:, cols]
                for k in range(2):
                    j = 2 * pair + k
                    span = slice(j * HEAD, (j + 1) * HEAD)
                    lane = low_lane if k == 0 else jnp.logical_not(low_lane)
                    scores = mm(key, q_turn[span, :]) * scale
                    if bias is not None:
                        scores = scores + bias
                    prob = jnp.exp2(scores - lse_ref[j:j + 1, :])
                    dprob = mm(value, do_turn[span, :])
                    dscore = (prob * (dprob - delta_ref[j:j + 1, :])).astype(BF16)
                    dq_acc[span, :] += mm(key_t, dscore)
                    dk = dk + mm(dscore, jnp.where(lane, q_rows, zero_rows))
                    dv = dv + mm(prob.astype(BF16), jnp.where(lane, do_rows, zero_rows))
            dkv_acc[:, own] = (dk[:, :HEAD] + dk[:, HEAD:]) * HEAD ** -0.5
            dkv_acc[:, kv_width + h * HEAD:kv_width + (h + 1) * HEAD] = dv[:, :HEAD] + dv[:, HEAD:]

    @pl.when(me > 0)
    def _():
        pl.semaphore_wait(barrier, me)

    def earlier(i, carry):
        d = me - i
        block(d, None)
        send_kv[d - 1] = dkv_acc[...].astype(BF16)
        to_earlier(d).start()
        return carry

    lax.fori_loop(0, me, earlier, 0)
    key_pos = lax.broadcasted_iota(jnp.int32, (rows, rows), 0)
    query_pos = lax.broadcasted_iota(jnp.int32, (rows, rows), 1)
    block(0, jnp.where(key_pos <= query_pos, 0.0, NEG_FILL))

    loads[1].wait()
    loads[2].wait()
    for at in range(0, width, chunk):
        for col in range(at, at + chunk, LANES):
            dq_ref[:, col:col + LANES] = rotated(dq_acc[col:col + LANES, :].T * HEAD ** -0.5, cos_ref, sin_ref).astype(BF16)
    for at in range(0, width, chunk):
        dn_ref[:, at:at + chunk] = mm_t(dq_ref[...], wq_ref[at:at + chunk, :])
    for d in range(1, n):
        @pl.when(me + d < n)
        def _(d=d):
            from_later(d).wait_recv()
            dkv_acc[...] += land_kv[d - 1].astype(F32)
    dkv_ref[:, :kv_width] = rotated(dkv_acc[:, :kv_width], cos_ref, sin_ref).astype(BF16)
    dkv_ref[:, kv_width:] = dkv_acc[:, kv_width:].astype(BF16)
    for at in range(0, width, chunk):
        dn_ref[:, at:at + chunk] += mm_t(dkv_ref[...], wkv_ref[at:at + chunk, :])
    x = x_ref[...].astype(F32)
    root = inv_root_of(x)
    dnormed = dn_ref[...]
    scaled = dnormed * gain_ref[...]
    grad = dmid_ref[...] + root * scaled - x * (root * root * root * jnp.mean(scaled * x, axis=-1, keepdims=True))
    grad_ref[...] = grad
    grad_low_ref[...] = grad.astype(BF16)
    dgain_ref[...] = jnp.sum(dnormed * x * root, axis=0, keepdims=True)
    for d in range(1, n):
        @pl.when(me >= d)
        def _(d=d):
            to_earlier(d).wait_send()


def attend_back(da, dmid, x, gain, cos_table, back_sin, q, kv, attended, lse, w_q, w_kv, w_o, collective_id):
    n = lax.axis_size("shard")
    rows, width = x.shape
    kv_both = w_kv.shape[1]
    vmem = pl.BlockSpec(memory_space=pltpu.VMEM)
    anywhere = pl.BlockSpec(memory_space=pl.ANY)
    dma = pltpu.SemaphoreType.DMA
    flops = 2 * rows * width * (2 * width + kv_both) + 10 * rows * rows * n * width
    return pl.pallas_call(
        attend_back_kernel,
        in_specs=[vmem] * 10 + [anywhere] * 3,
        out_specs=[vmem] * 5,
        out_shape=[
            jax.ShapeDtypeStruct((rows, width), BF16),
            jax.ShapeDtypeStruct((rows, kv_both), BF16),
            jax.ShapeDtypeStruct((rows, width), F32),
            jax.ShapeDtypeStruct((rows, width), BF16),
            jax.ShapeDtypeStruct((1, width), F32),
        ],
        scratch_shapes=[
            pltpu.VMEM(w_q.shape, BF16), pltpu.VMEM(w_kv.shape, BF16), pltpu.VMEM(w_o.shape, BF16),
            pltpu.VMEM((rows, width), BF16), pltpu.VMEM((width, rows), BF16), pltpu.VMEM((width, rows), BF16),
            pltpu.VMEM((HEADS, rows), F32), pltpu.VMEM((width, rows), F32), pltpu.VMEM((rows, kv_both), F32),
            pltpu.VMEM((rows, width), F32),
            pltpu.VMEM((n - 1, rows, kv_both), BF16), pltpu.VMEM((n - 1, rows, kv_both), BF16),
            dma((3,)), dma((n - 1,)), dma((n - 1,)),
        ],
        compiler_params=pltpu.CompilerParams(
            collective_id=collective_id, has_side_effects=True, vmem_limit_bytes=58 * 1024 * 1024),
        cost_estimate=pl.CostEstimate(flops=flops, bytes_accessed=2 * width * (2 * width + kv_both), transcendentals=rows * rows * n * HEADS),
        name="attend_back",
    )(da, dmid, x, gain, cos_table, back_sin, q, kv, attended, lse, w_q, w_kv, w_o)


ROPE_BASE = 10000.0


def angles_for(positions):
    half_dim = HEAD // 2
    inverse = ROPE_BASE ** (-(jnp.arange(half_dim, dtype=F32) * 2.0 / HEAD))
    angle_grid = positions.astype(F32)[:, None] * inverse[None, :]
    return (jnp.cos(angle_grid), jnp.sin(angle_grid))


def passed_along(block, axis, by):
    length = lax.axis_size(axis)
    pairs = [(i, i + by) for i in range(length) if 0 <= i + by < length]
    return lax.ppermute(block, axis, pairs)


Y_PAIRS = [(0, 2), (2, 0), (1, 3), (3, 1)]


def halves_of(grad_gate, grad_up):
    half = grad_gate.shape[1] // 2
    at = (1 - lax.axis_index("rep") // 2) * half
    parts = [lax.dynamic_slice_in_dim(term, at, half, 1) for term in (grad_gate, grad_up)]
    return lax.ppermute(jnp.concatenate(parts, axis=1), "rep", Y_PAIRS)


def layer_forward(stream_in, weights, tables, pending, done):
    w_q, w_kv, w_o, w_g, w_u, w_d, gains_wide = weights
    cos_table, sin_table = tables
    normed, queries, kv, attended, lse, middle = done or attend_block(
        stream_in, gains_wide[0:1], cos_table, sin_table, w_q, w_kv, w_o, 3)
    middle, pending = lax.optimization_barrier((middle, pending))
    result, normed_two, hidden, gate_fac, up_fac = ffn_fwd(middle, gains_wide[1:2], w_g, w_u, w_d)
    kept = {"stream": stream_in, "normed": normed, "queries": queries, "kv": kv, "attended": attended, "lse": lse,
            "middle": middle, "normed_two": normed_two, "hidden": hidden, "gate_fac": gate_fac, "up_fac": up_fac}
    return result, kept, pending


def layer_backward(grad_bf, kept, weights, tables, pending):
    w_q, w_kv, w_o, w_g, w_u, w_d, gains_wide = weights
    cos_table, sin_table = tables
    grad_gate, grad_up, grad_middle, grad_branch, gain_two = ffn_bwd(
        grad_bf, kept["middle"], gains_wide[1:2], kept["gate_fac"], kept["up_fac"], w_g, w_u, w_d)
    grad_branch, pending = lax.optimization_barrier((grad_branch, pending))
    halves_out = halves_of(grad_gate, grad_up)
    grad_query, grad_kv, grad_stream, grad_low, gain_one = attend_back(
        grad_branch, grad_middle, kept["stream"], gains_wide[0:1], cos_table, -sin_table, kept["queries"], kept["kv"],
        kept["attended"], kept["lse"], w_q, w_kv, w_o, 4)
    terms = (grad_query, grad_kv, grad_branch, grad_gate, grad_up, grad_bf, halves_out)
    return grad_stream, grad_low, terms, jnp.concatenate([gain_one, gain_two], axis=0), pending


def body(tokens, cotangent, live_counts, w_query, w_key, w_value, w_out, w_gate, w_up, w_down, norm_gains):
    section = lax.axis_index("section")
    slot_count, span_len, model_width = tokens.shape
    query_pos = lax.axis_index("shard") * span_len + jnp.arange(span_len, dtype=jnp.int32)
    cos_half, sin_half = angles_for(query_pos)
    tables = (jnp.tile(cos_half, (1, 4)), jnp.tile(jnp.concatenate([-sin_half, sin_half], axis=1), (1, 2)))
    live_mask = (jnp.arange(slot_count) < live_counts[0]).astype(BF16)
    gain_rows = jnp.pad(norm_gains[0], ((0, 14), (0, -norm_gains.shape[2] % (4 * LANES))))
    shards = [w_query[0], jnp.concatenate([w_key[0], w_value[0]], axis=1), w_out[0], gain_rows, w_gate[0], w_up[0], w_down[0]]
    first_in = jnp.where(section == 0, tokens[0] * live_mask[0], jnp.zeros_like(tokens[0]))
    gathered, attended_first = gather_weights(
        first_in, *tables, shards, [halves(shard.shape[1]) for shard in shards], 2, "gather_weights")
    w_q, w_kv, w_o, gains, w_g, w_u, w_d = gathered
    gain_blocks = gains.reshape(-1, 16, gain_rows.shape[1])[:, :2, :norm_gains.shape[2]]
    gains_wide = gain_blocks.transpose(1, 0, 2).reshape(2, model_width).astype(F32)
    weights = (w_q, w_kv, w_o, w_g, w_u, w_d, gains_wide)
    zero_slot = jnp.zeros((span_len, model_width), BF16)
    ticks = slot_count + 1
    results, kept_all, others = [], [], []
    pending = []
    received = zero_slot
    for tick in range(ticks):
        slot_in = tokens[tick] * live_mask[tick] if tick < slot_count else zero_slot
        own_in = jnp.where(section == 0, slot_in, received) if tick else first_in
        result, kept, pending = layer_forward(own_in, weights, tables, pending, None if tick else attended_first)
        others += pending
        pending = [lax.ppermute(kept["normed_two"], "rep", Y_PAIRS)]
        received = passed_along(result, "section", 1)
        results.append(result)
        kept_all.append(kept)
    first = section == 0
    acts = jnp.stack([jnp.where(first, results[j], results[j + 1]) for j in range(slot_count)])
    received = zero_slot
    streams, term_list, gain_total = [], [], 0.0
    for tick in range(ticks):
        slot_cot = cotangent[slot_count - 1 - tick] * live_mask[slot_count - 1 - tick] if tick < slot_count else zero_slot
        grad_bf = jnp.where(first, received, slot_cot)
        grad_stream, grad_low, terms, gain_grad, pending = layer_backward(
            grad_bf, kept_all[ticks - 1 - tick], weights, tables, pending)
        others += pending
        pending = [terms[6]]
        received = passed_along(grad_low, "section", -1)
        streams.append(grad_stream)
        term_list.append(terms)
        gain_total = gain_total + gain_grad
    grad_in = jnp.stack([
        jnp.where(first, streams[slot_count - j], streams[slot_count - 1 - j]) for j in range(slot_count)])

    others += pending
    normed_others, half_others = others[ticks - 1::-1], others[ticks:]

    def kept_by_tick(name):
        return [kept_all[ticks - 1 - tick][name] for tick in range(ticks)]

    def by_tick(index):
        return [terms[index] for terms in term_list]

    gate_sum, up_sum, qkv_sum, out_sum, down_sum, gain_sum = reduce_weights(
        jnp.pad(gain_total, ((0, 6), (0, 0))),
        [
            {"kind": "pair", "blocks": 1, "pace": 1, "delay": 3, "which": [0, 0],
             "lefts": [[kept_by_tick("normed_two"), normed_others]],
             "rights": [[by_tick(3), half_others], [by_tick(4), half_others]]},
            {"kind": "y", "blocks": 1, "pace": 2, "delay": 2, "which": [0, 1],
             "lefts": [[kept_by_tick("normed")], [kept_by_tick("attended")]],
             "rights": [[by_tick(0), by_tick(1)], [by_tick(2)]]},
            {"kind": "y", "blocks": 2, "pace": 2, "delay": 2, "which": [0],
             "lefts": [[kept_by_tick("hidden")]], "rights": [[by_tick(5)]]},
        ],
        slot_count, 1, "reduce_weights")
    kv_width = w_key.shape[2]
    outs = (
        qkv_sum[:, :model_width],
        qkv_sum[:, model_width:model_width + kv_width],
        qkv_sum[:, model_width + kv_width:],
        out_sum,
        gate_sum,
        up_sum,
        down_sum,
        gain_sum[:2],
    )
    return (acts[None], grad_in[None]) + tuple(out.astype(F32)[None] for out in outs)


def solution(mesh):
    tall = P("section", "shard", None)
    per_slot = P("section", "rep", "shard", None)
    return jax.shard_map(
        body,
        mesh=mesh,
        in_specs=(P("rep", "shard", None), P("rep", "shard", None), P("rep")) + (tall,) * 7 + (P("section", None, "shard"),),
        out_specs=(per_slot, per_slot) + (tall,) * 7 + (P("section", None, "shard"),),
        check_vma=False,
    )
```

```python
import functools, math
import jax
import jax.numpy as jnp
from jax import lax
from jax.sharding import PartitionSpec as P
from jax.experimental import pallas as pl
from jax.experimental.pallas import tpu as pltpu

HEADS = 32
KV_HEADS = 4
HEAD = 64
LOG2E = math.log2(math.e)
NEG_FILL = -1e30
F32, BF16 = jnp.float32, jnp.bfloat16


def mm(a, b):
    return jnp.dot(a, b, preferred_element_type=F32)


MESH_IDS = pl.DeviceIdType.MESH
LANES = 128
BUFS = 26


def remote(src, dst, send_sem, recv_sem, peer):
    return pltpu.make_async_remote_copy(src, dst, send_sem, recv_sem, device_id=peer, device_id_type=MESH_IDS)


def reduce_stages(kind, blocks, delay, segments, place, a_ref, b_ref, bufs):
    n, me, rep, right, core_peer, y_peer = place
    own_core, own_y = lax.rem(rep, 2), rep // 2
    paired = kind == "pair"
    (send_c, own, land_c, keep, send_y, land_y, send_z, land_z, send_f,
     sc_sem, rc_sem, cr_c, sy_sem, ry_sem, cr_y, sz_sem, rz_sem, ly_sem, sfy_sem, sfc_sem,
     rfy_sem, rfc_sem, sfw_sem, rfw_sem) = bufs
    rows = own.shape[2]
    depth = land_z.shape[1]
    span = a_ref.shape[3]
    items = b_ref.shape[2] // LANES * blocks
    starts = [first for _, _, first in segments]
    ends = starts[1:] + [items // blocks]

    def spot_of(out, first, r, p):
        width = out.shape[1] // 4
        column = pl.multiple_of(r * width + (p // blocks - first) * LANES, LANES)
        row = pl.multiple_of(lax.rem(p, blocks) * rows, 16)
        return out.at[pl.ds(row, rows), pl.ds(column, LANES)]

    def each_segment(p, fn):
        for (out, _, first), last in zip(segments, ends):
            if len(segments) == 1:
                fn(lambda r, out=out, first=first: spot_of(out, first, r, p))
                continue
            group = p // blocks

            @pl.when(jnp.logical_and(group >= first, group < last))
            def _(out=out, first=first):
                fn(lambda r: spot_of(out, first, r, p))

    def c_copy(a, s):
        return remote(send_c.at[a], land_c.at[s], sc_sem.at[a], rc_sem.at[s], core_peer)

    def y_copy(a, s):
        return remote(send_y.at[a], land_y.at[s], sy_sem.at[a], ry_sem.at[s], y_peer)

    def z_copy(a, s, p):
        b = lax.rem(p, depth)
        return remote(send_z.at[a], land_z.at[s, b], sz_sem.at[a], rz_sem.at[s, b], right)

    def f_local(a, spot):
        return pltpu.make_async_copy(send_f.at[a], spot(rep), ly_sem.at[a])

    def f_y(a, p, spot):
        return remote(send_f.at[a], spot(rep), sfy_sem.at[a], rfy_sem.at[p], y_peer)

    def f_core(a, p, spot):
        return remote(send_f.at[a], spot(rep), sfc_sem.at[a], rfc_sem.at[p], core_peer)

    def f_turn(a, p, spot):
        there = spot(rep + 2 - 4 * own_y)
        return remote(there, there, sfw_sem.at[a], rfw_sem.at[p], core_peer)

    def stage_zero(a, s, p):
        dest = lax.rem(me + 2 * n - 1 - s, n)
        row = pl.ds(pl.multiple_of((dest * blocks + lax.rem(p, blocks)) * rows, 16), rows)
        which = 0
        for (_, index, first) in segments[1:]:
            which = jnp.where(p // blocks >= first, index, which)
        column = pl.ds(pl.multiple_of(p // blocks * LANES, LANES), LANES)

        def product(r):
            total = None
            for k in range(a_ref.shape[1]):
                term = mm(a_ref[which, k, row, :], b_ref[r, k * span:(k + 1) * span, column])
                total = term if total is None else total + term
            return total
        tiles = range(1 if paired else 2)
        for y in tiles:
            send_c[a, y] = product(2 * y + 1 - own_core).astype(BF16)

        @pl.when(p >= 1)
        def _():
            pl.semaphore_wait(cr_c.at[s], 1)
        c_copy(a, s).start()
        for y in tiles:
            own[a, y] = product(2 * y + own_core)

    def credit(sem, s, p, peer):
        @pl.when(p + 1 < items)
        def _():
            pl.semaphore_signal(sem.at[s], inc=1, device_id=peer, device_id_type=MESH_IDS)

    def finish(a, p, total):
        send_f[a] = total.astype(BF16)

        def send(spot):
            f_y(a, p, spot).start()
            f_core(a, p, spot).start()
            f_local(a, spot).start()
        each_segment(p, send)

    def go_round(a, s, p, ref):
        @pl.when(s > 0)
        def _():
            z_copy(a, s - 1, p).wait_recv()
            ref[...] = ref[...] + land_z[s - 1, lax.rem(p, depth)].astype(F32)

        @pl.when(s < n - 1)
        def _():
            send_z[a] = ref[...].astype(BF16)
            z_copy(a, s, p).start()

        @pl.when(s == n - 1)
        def _():
            finish(a, p, ref[...])

    def stage_one_pair(a, s, p):
        c_copy(a, s).wait()
        own[a, 0] = own[a, 0] + land_c[s, 0].astype(F32)
        credit(cr_c, s, p, core_peer)
        go_round(a, s, p, own.at[a, 0])

    def stage_one_y(a, s, p):
        c_copy(a, s).wait()
        send_y[a] = (own[a, 1 - own_y] + land_c[s, 1 - own_y].astype(F32)).astype(BF16)

        @pl.when(p >= 1)
        def _():
            pl.semaphore_wait(cr_y.at[s], 1)
        y_copy(a, s).start()
        keep[a] = own[a, own_y] + land_c[s, own_y].astype(F32)
        credit(cr_c, s, p, core_peer)

    def stage_two_y(a, s, p):
        y_copy(a, s).wait()
        keep[a] = keep[a] + land_y[s].astype(F32)
        credit(cr_y, s, p, y_peer)
        go_round(a, s, p, keep.at[a])

    def turn_over(a, s, p):
        @pl.when(s < n - 1)
        def _():
            z_copy(a, s, p).wait_send()

        @pl.when(s == n - 1)
        def _():
            def turn(spot):
                f_local(a, spot).wait()
                f_core(a, p, spot).wait_send()
                f_y(a, p, spot).wait()
                f_turn(a, p, spot).start()
            each_segment(p, turn)

    def end_of(a, s, p):
        @pl.when(s == n - 1)
        def _():
            def end(spot):
                f_core(a, p, spot).wait_recv()
                f_turn(a, p, spot).wait()
            each_segment(p, end)

    if paired:
        return items, (stage_zero, stage_one_pair, turn_over, end_of)
    return items, (stage_zero, stage_one_y, stage_two_y, turn_over, end_of)


def gain_steps(place, gain_ref, out_ref, total, land_c, land_y, land_z, sends, lands):
    n, me, _, _, core_peer, y_peer = place
    chunk = out_ref.shape[1]

    def over_core():
        return remote(total, land_c, sends.at[0], lands.at[0], core_peer)

    def over_y():
        return remote(total, land_y, sends.at[1], lands.at[1], y_peer)

    def over_z(d):
        dest = lax.rem(me + d, n)
        part = total.at[:, pl.ds(pl.multiple_of(dest * chunk, LANES), chunk)]
        return remote(part, land_z.at[d - 1], sends.at[d + 1], lands.at[d + 1], {"shard": dest})

    def begin():
        total[...] = gain_ref[...]
        over_core().start()

    def add_core():
        over_core().wait()
        total[...] = total[...] + land_c[...]
        over_y().start()

    def add_y():
        over_y().wait()
        total[...] = total[...] + land_y[...]
        for d in range(1, n):
            over_z(d).start()

    def add_z():
        result = total[:, pl.ds(pl.multiple_of(me * chunk, LANES), chunk)]
        for d in range(1, n):
            over_z(d).wait()
            result = result + land_z[d - 1]
        out_ref[...] = result

    return ((3, begin), (30, add_core), (60, add_y), (90, add_z))


def reduce_kernel(streams, slots, *refs):
    n = lax.axis_size("shard")
    me = lax.axis_index("shard")
    rep = lax.axis_index("rep")
    section = lax.axis_index("section")
    right = {"shard": lax.rem(me + 1, n)}
    core_peer = {"rep": rep + 1 - 2 * lax.rem(rep, 2)}
    y_peer = {"rep": rep + 2 - 4 * (rep // 2)}
    place = (n, me, rep, right, core_peer, y_peer)

    refs = list(refs)
    gain_ref = refs.pop(0)

    def taken(tree):
        return [taken(x) for x in tree] if isinstance(tree, list) else refs.pop(0)
    lefts = [taken(stream["lefts"]) for stream in streams]
    rights = [taken(stream["rights"]) for stream in streams]
    outs = [[refs.pop(0) for _ in stream["rights"]] for stream in streams]
    gain_out = refs.pop(0)
    per = [[refs.pop(0) for _ in range(BUFS)] for _ in streams]
    load_sem = refs.pop(0)
    timed = gain_steps(place, gain_ref, gain_out, *refs)

    barrier = pltpu.get_barrier_semaphore()
    for peer in [{"shard": lax.rem(me + d, n)} for d in range(1, n)] + [core_peer, y_peer]:
        pl.semaphore_signal(barrier, inc=1, device_id=peer, device_id_type=MESH_IDS)

    def load_all(at_section):
        loads = []

        def load(src, dst):
            loads.append(pltpu.make_async_copy(src, dst, load_sem.at[len(loads)]))
            loads[-1].start()

        def tick_of(ticks, j):
            return ticks[slots - j if at_section == 0 else slots - 1 - j]
        for stream, left_refs, right_refs, bufs in zip(streams, lefts, rights, per):
            a_ref, b_ref = bufs[0], bufs[1]
            for k, groups in enumerate(left_refs):
                for g, ticks in enumerate(groups):
                    for j in range(slots):
                        load(tick_of(ticks, j), a_ref.at[k, g * slots + j])
            base = 0
            for segment in right_refs:
                if stream["kind"] == "pair":
                    mine, other = segment
                    quarter = mine[0].shape[1] // 4
                    for c in range(2):
                        column = pl.ds(pl.multiple_of((rep // 2 * 2 + c) * quarter, LANES), quarter)
                        for g, ticks in enumerate((mine, other)):
                            for j in range(slots):
                                tick = tick_of(ticks, j)
                                span = tick.shape[0]
                                at = (g * slots + j) * span
                                load(tick.at[:, column] if g == 0 else tick.at[:, 2 * base + c * quarter:2 * base + (c + 1) * quarter],
                                     b_ref.at[c, at:at + span, base:base + quarter])
                    base += quarter
                    continue
                quarter = sum(ticks[0].shape[1] for ticks in segment) // 4
                for r in range(4):
                    at = 0
                    for ticks in segment:
                        width = ticks[0].shape[1]
                        lo, hi = max(r * quarter, at), min((r + 1) * quarter, at + width)
                        if lo < hi:
                            for j in range(slots):
                                tick = tick_of(ticks, j)
                                span = tick.shape[0]
                                load(tick.at[:, lo - at:hi - at],
                                     b_ref.at[r, j * span:(j + 1) * span, base + lo - r * quarter:base + hi - r * quarter])
                        at += width
                base += quarter
        for copy in loads:
            copy.wait()

    for value in range(2):
        @pl.when(section == value)
        def _(value=value):
            load_all(value)
    pl.semaphore_wait(barrier, n + 1)

    work, last = [], 0
    for stream, segs, bufs in zip(streams, outs, per):
        delay = stream["delay"]
        items, fns = reduce_stages(
            stream["kind"], stream["blocks"], delay,
            [(out, index, first) for out, index, first in zip(segs, stream["which"], stream["firsts"])],
            place, bufs[0], bufs[1], bufs[2:])
        pace = stream["pace"]
        work.append((pace, delay, items, fns))
        last = max(last, pace * (n * (items + n - 1) + (len(fns) - 1) * delay))

    def step(i, carry):
        for k in (4, 3, 2, 1, 0):
            for pace, delay, items, fns in work:
                if k >= len(fns):
                    continue
                v = i // pace - delay * k
                s = lax.rem(v + n * delay * 4, n)
                p = (v - s) // n - s
                fine = jnp.logical_and(jnp.logical_and(v >= 0, lax.rem(i, pace) == 0), jnp.logical_and(p >= 0, p < items))

                @pl.when(fine)
                def _(s=s, p=p, v=v, fn=fns[k], delay=delay):
                    fn(lax.rem(v, delay), s, p)
        for at, fn in timed:
            pl.when(i == at)(fn)
        return carry

    lax.fori_loop(0, last, step, 0)


def reduce_weights(gain, streams, slots, collective_id, name):
    n = lax.axis_size("shard")
    operands, out_shapes, scratch, flops, moved, plans, loads = [], [], [], 0, 0, [], 0
    dma, regular = pltpu.SemaphoreType.DMA, pltpu.SemaphoreType.REGULAR

    def listed(tree):
        if isinstance(tree, list):
            return [listed(x) for x in tree]
        operands.append(tree)
        return None
    left_plans = [listed(stream["lefts"]) for stream in streams]
    right_plans = [listed(stream["rights"]) for stream in streams]
    for stream, left_plan, right_plan in zip(streams, left_plans, right_plans):
        paired = stream["kind"] == "pair"
        blocks, delay = stream["blocks"], stream["delay"]
        height, span = stream["lefts"][0][0][0].shape
        height //= n
        chunks = len(stream["lefts"][0]) * slots
        firsts, at = [], 0
        for segment in stream["rights"]:
            width = segment[0][0].shape[1] if paired else sum(ticks[0].shape[1] for ticks in segment)
            firsts.append(at)
            at += width // 4 // LANES
            out_shapes.append(jax.ShapeDtypeStruct((height, width), BF16))
            flops += 2 * span * slots * height * n * width
            moved += height * width * 4
            loads += 4 * slots * len(segment)
        loads += len(stream["lefts"]) * chunks
        items = at * blocks
        depth = min(items, n + 2)
        tile = (height // blocks, LANES)
        both = 1 if paired else 2
        few = (16, LANES)
        scratch += [
            pltpu.VMEM((len(stream["lefts"]), chunks, height * n, span), BF16),
            pltpu.VMEM((2 * both, chunks * span, at * LANES), BF16),
            pltpu.VMEM((delay, both) + tile, BF16),
            pltpu.VMEM((delay, both) + tile, F32),
            pltpu.VMEM((n, both) + tile, BF16),
            pltpu.VMEM((1,) + few if paired else (delay,) + tile, F32),
            pltpu.VMEM((1,) + few if paired else (delay,) + tile, BF16),
            pltpu.VMEM((1,) + few if paired else (n,) + tile, BF16),
            pltpu.VMEM((delay,) + tile, BF16),
            pltpu.VMEM((n - 1, depth) + tile, BF16),
            pltpu.VMEM((delay,) + tile, BF16),
            dma((delay,)), dma((n,)), regular((n,)),
            dma((delay,)), dma((n,)), regular((n,)),
            dma((delay,)), dma((n - 1, depth)),
            dma((delay,)), dma((delay,)), dma((delay,)),
            dma((items,)), dma((items,)), dma((delay,)), dma((items,)),
        ]
        plans.append({
            "kind": stream["kind"], "blocks": blocks, "delay": delay, "pace": stream["pace"], "which": tuple(stream["which"]),
            "firsts": tuple(firsts), "lefts": left_plan, "rights": right_plan})
    chunk = gain.shape[1] // n
    out_shapes.append(jax.ShapeDtypeStruct((gain.shape[0], chunk), F32))
    scratch += [dma((loads,))] + [pltpu.VMEM(gain.shape, F32)] * 3
    scratch += [pltpu.VMEM((n - 1, gain.shape[0], chunk), F32), dma((n + 1,)), dma((n + 1,))]
    in_vmem = pl.BlockSpec(memory_space=pltpu.VMEM)
    anywhere = pl.BlockSpec(memory_space=pl.ANY)
    return pl.pallas_call(
        functools.partial(reduce_kernel, plans, slots),
        in_specs=[in_vmem] + [anywhere] * len(operands),
        out_specs=[anywhere] * (len(out_shapes) - 1) + [in_vmem],
        out_shape=out_shapes,
        scratch_shapes=scratch,
        compiler_params=pltpu.CompilerParams(
            collective_id=collective_id, has_side_effects=True, vmem_limit_bytes=60 * 1024 * 1024),
        cost_estimate=pl.CostEstimate(flops=flops, bytes_accessed=moved, transcendentals=0),
        name=name,
    )(gain, *operands)


def gather_kernel(splits, x_ref, cos_ref, sin_ref, *refs):
    n = lax.axis_size("shard")
    me = lax.axis_index("shard")
    rep = lax.axis_index("rep")
    right = {"shard": lax.rem(me + 1, n)}
    core_peer = {"rep": rep + 1 - 2 * lax.rem(rep, 2)}
    y_rep = rep + 2 - 4 * (rep // 2)
    y_peer = {"rep": y_rep}
    count = len(splits)
    early = 4
    ins, outs, refs = refs[:count], refs[count:2 * count], refs[2 * count:]
    attend_outs, refs = refs[:6], refs[6:]
    attend_refs, refs = refs[:13], refs[13:]
    holds, refs = refs[:count], refs[count:]
    zs, zr, ys, yr, cs, cr, ts, tr, local, gain_blocks, gain_row, gain_sem = refs

    barrier = pltpu.get_barrier_semaphore()
    for peer in [{"shard": lax.rem(me + d, n)} for d in range(1, n)] + [core_peer, y_peer]:
        pl.semaphore_signal(barrier, inc=1, device_id=peer, device_id_type=MESH_IDS)

    pieces = []
    for k, split in enumerate(splits):
        at = 0
        for width in split:
            pieces.append((k, at, width))
            at += width
    first = [piece for piece in range(len(pieces)) if pieces[piece][0] < early]
    second = [piece for piece in range(len(pieces)) if pieces[piece][0] >= early]

    def own_load(k):
        return pltpu.make_async_copy(ins[k], holds[k], local.at[0, k])

    def own_store(k):
        rows = ins[k].shape[0]
        return pltpu.make_async_copy(holds[k], outs[k].at[pl.ds(pl.multiple_of(me * rows, 16), rows), :], local.at[1, k])

    def spot(piece, back, r):
        k, at, width = pieces[piece]
        rows = ins[k].shape[0]
        block = lax.rem(me + n - back, n)
        column = pl.multiple_of(r * (ins[k].shape[1] // 4) + at, LANES)
        return outs[k].at[pl.ds(pl.multiple_of(block * rows, 16), rows), pl.ds(column, width)]

    def z_copy(piece, s):
        k, at, width = pieces[piece]
        there = spot(piece, s, rep)
        column = pl.multiple_of(rep * (ins[k].shape[1] // 4) + at, LANES)
        here = ins[k].at[:, pl.ds(column, width)] if s == 0 else there
        return remote(here, there, zs.at[piece, s], zr.at[piece, s], right)

    def y_copy(piece, s):
        there = spot(piece, s, rep)
        return remote(there, there, ys.at[piece, s - 1], yr.at[piece, s - 1], y_peer)

    def c_copy(piece, s):
        there = spot(piece, s, rep)
        return remote(there, there, cs.at[piece, s - 1], cr.at[piece, s - 1], core_peer)

    def t_copy(piece, s):
        there = spot(piece, s, y_rep)
        return remote(there, there, ts.at[piece, s - 1], tr.at[piece, s - 1], core_peer)

    def begin(group):
        for piece in group:
            z_copy(piece, 0).start()

    def own_rows(which):
        for k in which:
            own_load(k).start()
        for k in which:
            own_load(k).wait()
            own_store(k).start()

    def turn(piece, s):
        y_copy(piece, s).wait_recv()
        t_copy(piece, s).start()

    def hop(piece, s):
        z_copy(piece, s - 1).wait_recv()
        if s < n - 1:
            z_copy(piece, s).start()
        y_copy(piece, s).start()
        c_copy(piece, s).start()

    def pass_on(group, served):
        order = [(piece, s) for s in range(1, n) for piece in group]
        turned = 0
        for at in range(served, len(order)):
            hop(*order[at])
            while turned < at:
                turn(*order[turned])
                turned += 1
        for at in range(turned, len(order)):
            turn(*order[at])
        return order

    def arrived(which, before):
        for k in which:
            own_store(k).wait()
        for piece, s in before:
            c_copy(piece, s).wait_recv()
            t_copy(piece, s).wait_recv()

    pl.semaphore_wait(barrier, n + 1)
    begin(first)
    own_rows(range(early))

    def start_second():
        begin(second)
        for k in range(early, count):
            own_load(k).start()
    served = []

    def serve(pieces):
        for _ in range(pieces):
            hop(second[len(served)], 1)
            served.append(1)
    before = pass_on(first, 0)
    arrived(range(early), before)
    load = pltpu.make_async_copy(outs[3], gain_blocks, gain_sem.at[0])
    load.start()
    load.wait()
    rows = ins[3].shape[0]
    part = x_ref.shape[1] // n
    for k in range(n):
        gain_row[:, k * part:(k + 1) * part] = gain_blocks[k * rows:k * rows + 1, :part].astype(F32)
    attend_steps(lambda: None, start_second, serve, x_ref, gain_row, cos_ref, sin_ref, outs[0], outs[1], outs[2], *attend_outs, *attend_refs)
    for k in range(early, count):
        own_load(k).wait()
        own_store(k).start()
    after = pass_on(second, len(served))
    arrived(range(early, count), after)
    for piece, s in before + after:
        z_copy(piece, s - 1).wait_send()
        y_copy(piece, s).wait_send()
        c_copy(piece, s).wait_send()
        t_copy(piece, s).wait_send()


def gather_weights(x, cos_table, sin_table, shards, splits, collective_id, name):
    n = lax.axis_size("shard")
    rows, width = x.shape
    kv_both = shards[1].shape[1]
    dma = pltpu.SemaphoreType.DMA
    pieces = sum(len(split) for split in splits)
    pair = dma((pieces, n - 1))
    anywhere = pl.BlockSpec(memory_space=pl.ANY)
    vmem = pl.BlockSpec(memory_space=pltpu.VMEM)
    moved = 2 * n * sum(shard.shape[0] * shard.shape[1] for shard in shards)
    results = pl.pallas_call(
        functools.partial(gather_kernel, splits),
        in_specs=[vmem] * 3 + [anywhere] * len(shards),
        out_specs=[anywhere] * len(shards) + [vmem] * 6,
        out_shape=[jax.ShapeDtypeStruct((n * shard.shape[0], shard.shape[1]), BF16) for shard in shards]
        + attend_outputs(rows, width, n, kv_both),
        scratch_shapes=attend_scratch(rows, width, n, kv_both) + [pltpu.VMEM(shard.shape, BF16) for shard in shards]
        + [pair] * 8 + [dma((2, len(shards))), pltpu.VMEM((n * shards[3].shape[0], shards[3].shape[1]), BF16),
                        pltpu.VMEM((1, width), F32), dma((1,))],
        compiler_params=pltpu.CompilerParams(collective_id=collective_id, has_side_effects=True, vmem_limit_bytes=60 * 1024 * 1024),
        cost_estimate=pl.CostEstimate(flops=4 * rows * width * width, bytes_accessed=moved * 4, transcendentals=0),
        name=name,
    )(x, cos_table, sin_table, *shards)
    return results[:len(shards)], results[len(shards):]


def halves(width):
    quarter = width // 4
    first = (quarter // LANES + 1) // 2 * LANES
    return (first, quarter - first) if quarter > first else (quarter,)


EPSILON = 1e-05
FF_TILE = 512


def mm_t(a, b):
    return lax.dot_general(a, b, (((1,), (1,)), ((), ())), preferred_element_type=F32)


def inv_root_of(rows):
    return lax.rsqrt(jnp.mean(rows * rows, axis=-1, keepdims=True) + EPSILON)


def ffn_fwd_kernel(mid_ref, gain_ref, w_g, w_u, w_d, out_ref, normed_turn, hidden_turn, gate_fac, up_fac, acc, normed_ref):
    step = pl.program_id(0)

    @pl.when(step == 0)
    def _():
        mid = mid_ref[...]
        normed_ref[...] = (mid * inv_root_of(mid) * gain_ref[...]).astype(BF16)
        acc[...] = mid
        for at in range(0, mid.shape[1], LANES):
            normed_turn[at:at + LANES, :] = normed_ref[:, at:at + LANES].T

    gate = mm(normed_ref[...], w_g[...])
    up = mm(normed_ref[...], w_u[...])
    sig = jax.nn.sigmoid(gate)
    act = gate * sig
    hidden = (act * up).astype(BF16)
    hidden_turn[...] = hidden.T
    up_fac[...] = act.astype(BF16)
    gate_fac[...] = (up * sig * (1.0 + gate * (1.0 - sig))).astype(BF16)
    acc[...] += mm(hidden, w_d[...])

    @pl.when(step == pl.num_programs(0) - 1)
    def _():
        out_ref[...] = acc[...].astype(BF16)


def ffn_fwd(middle, gain, w_g, w_u, w_d):
    rows, width = middle.shape
    ff = w_g.shape[1]
    whole = pl.BlockSpec((rows, width), lambda i: (0, 0))
    part = pl.BlockSpec((rows, FF_TILE), lambda i: (0, i))
    tall = pl.BlockSpec((width, FF_TILE), lambda i: (0, i))
    wide = jax.ShapeDtypeStruct((rows, ff), BF16)
    return pl.pallas_call(
        ffn_fwd_kernel,
        grid=(ff // FF_TILE,),
        in_specs=[whole, pl.BlockSpec((1, width), lambda i: (0, 0)), tall, tall, pl.BlockSpec((FF_TILE, width), lambda i: (i, 0))],
        out_specs=[whole, pl.BlockSpec((width, rows), lambda i: (0, 0)), pl.BlockSpec((FF_TILE, rows), lambda i: (i, 0)), part, part],
        out_shape=[jax.ShapeDtypeStruct((rows, width), BF16), jax.ShapeDtypeStruct((width, rows), BF16),
                   jax.ShapeDtypeStruct((ff, rows), BF16), wide, wide],
        scratch_shapes=[pltpu.VMEM((rows, width), F32), pltpu.VMEM((rows, width), BF16)],
        compiler_params=pltpu.CompilerParams(vmem_limit_bytes=58 * 1024 * 1024),
        cost_estimate=pl.CostEstimate(flops=6 * rows * width * ff, bytes_accessed=6 * width * ff, transcendentals=rows * ff),
        name="ffn_fwd",
    )(middle, gain, w_g, w_u, w_d)


def ffn_bwd_kernel(grad_ref, mid_ref, gain_ref, gate_fac, up_fac, w_g, w_u, w_d,
                   dgate_ref, dup_ref, dmid_ref, da_ref, dgain_ref, acc):
    step = pl.program_id(0)
    dhidden = mm_t(grad_ref[...], w_d[...])
    dgate = (dhidden * gate_fac[...].astype(F32)).astype(BF16)
    dup = (dhidden * up_fac[...].astype(F32)).astype(BF16)
    dgate_ref[...] = dgate
    dup_ref[...] = dup
    term = mm_t(dgate, w_g[...]) + mm_t(dup, w_u[...])

    @pl.when(step == 0)
    def _():
        acc[...] = term

    @pl.when(step > 0)
    def _():
        acc[...] += term

    @pl.when(step == pl.num_programs(0) - 1)
    def _():
        mid = mid_ref[...]
        root = inv_root_of(mid)
        dnormed = acc[...]
        scaled = dnormed * gain_ref[...]
        dmid = grad_ref[...].astype(F32) + root * scaled - mid * (root * root * root * jnp.mean(scaled * mid, axis=-1, keepdims=True))
        dmid_ref[...] = dmid
        da_ref[...] = dmid.astype(BF16)
        dgain_ref[...] = jnp.sum(dnormed * mid * root, axis=0, keepdims=True)


def ffn_bwd(grad, middle, gain, gate_fac, up_fac, w_g, w_u, w_d):
    rows, width = middle.shape
    ff = w_g.shape[1]
    whole = pl.BlockSpec((rows, width), lambda i: (0, 0))
    flat = pl.BlockSpec((1, width), lambda i: (0, 0))
    part = pl.BlockSpec((rows, FF_TILE), lambda i: (0, i))
    tall = pl.BlockSpec((width, FF_TILE), lambda i: (0, i))
    wide = jax.ShapeDtypeStruct((rows, ff), BF16)
    return pl.pallas_call(
        ffn_bwd_kernel,
        grid=(ff // FF_TILE,),
        in_specs=[whole, whole, flat, part, part, tall, tall, pl.BlockSpec((FF_TILE, width), lambda i: (i, 0))],
        out_specs=[part, part, whole, whole, flat],
        out_shape=[wide, wide, jax.ShapeDtypeStruct((rows, width), F32), jax.ShapeDtypeStruct((rows, width), BF16),
                   jax.ShapeDtypeStruct((1, width), F32)],
        scratch_shapes=[pltpu.VMEM((rows, width), F32)],
        compiler_params=pltpu.CompilerParams(vmem_limit_bytes=58 * 1024 * 1024),
        cost_estimate=pl.CostEstimate(flops=6 * rows * width * ff, bytes_accessed=6 * width * ff, transcendentals=0),
        name="ffn_bwd",
    )(grad, middle, gain, gate_fac, up_fac, w_g, w_u, w_d)


def rotated(rows, cos_ref, sin_ref):
    width = rows.shape[1]
    low_half = lax.rem(lax.broadcasted_iota(jnp.int32, rows.shape, 1), HEAD) < HEAD // 2
    swapped = jnp.where(low_half, pltpu.roll(rows, width - HEAD // 2, 1), pltpu.roll(rows, HEAD // 2, 1))
    reps = width // LANES
    return rows * jnp.tile(cos_ref[...], (1, reps)) + swapped * jnp.tile(sin_ref[...], (1, reps))


def attend_steps(greeted, sent, serve, x_ref, gain_ref, cos_ref, sin_ref, w_q, w_kv, w_o,
                 normed_turn, q_ref, kv_ref, attended_turn, lse_ref, mid_ref,
                 normed_ref, attended_ref, wq_ref, wkv_ref, wo_ref, q_turn, acc, top_ref, total_ref, land,
                 load_sem, send_sem, recv_sem):
    n = lax.axis_size("shard")
    me = lax.axis_index("shard")
    rows, width = x_ref.shape
    kv_width = wkv_ref.shape[1] // 2
    group = HEADS // KV_HEADS
    scale = LOG2E * HEAD ** -0.5
    loads = [pltpu.make_async_copy(src, dst, load_sem.at[k])
             for k, (src, dst) in enumerate(((w_kv, wkv_ref), (w_q, wq_ref), (w_o, wo_ref)))]
    for load in loads:
        load.start()

    def to_later(d):
        return remote(land.at[0], land.at[d], send_sem.at[d - 1], recv_sem.at[d - 1], {"shard": me + d})

    def from_earlier(d):
        return remote(land.at[0], land.at[d], send_sem.at[d - 1], recv_sem.at[d - 1], {"shard": me - d})

    x = x_ref[...].astype(F32)
    normed_ref[...] = (x * inv_root_of(x) * gain_ref[...]).astype(BF16)
    loads[0].wait()
    kv = mm(normed_ref[...], wkv_ref[...])
    land[0, :, :kv_width] = rotated(kv[:, :kv_width], cos_ref, sin_ref).astype(BF16)
    land[0, :, kv_width:] = kv[:, kv_width:].astype(BF16)
    greeted()
    for d in range(1, n):
        @pl.when(me + d < n)
        def _(d=d):
            to_later(d).start()
    sent()
    loads[1].wait()
    chunk = 4 * LANES
    for at in range(0, width, chunk):
        q_chunk = rotated(mm(normed_ref[...], wq_ref[:, at:at + chunk]), cos_ref, sin_ref).astype(BF16)
        q_ref[:, at:at + chunk] = q_chunk
        q_turn[at:at + chunk, :] = q_chunk.T

    def heads_of(d):
        for h in range(KV_HEADS):
            key = land[d, :, h * HEAD:(h + 1) * HEAD]
            pair_t = land[d, :, kv_width + h // 2 * LANES:kv_width + (h // 2 + 1) * LANES].T
            value_t = pair_t[h % 2 * HEAD:(h % 2 + 1) * HEAD, :]
            for j in range(h * group, (h + 1) * group):
                yield j, key, value_t

    key_pos = lax.broadcasted_iota(jnp.int32, (rows, rows), 0)
    query_pos = lax.broadcasted_iota(jnp.int32, (rows, rows), 1)
    bias = jnp.where(key_pos <= query_pos, 0.0, NEG_FILL)
    for j, key, value_t in heads_of(0):
        span = slice(j * HEAD, (j + 1) * HEAD)
        scores = mm(key, q_turn[span, :]) * scale + bias
        top = jnp.max(scores, axis=0, keepdims=True)
        prob = jnp.exp2(scores - top)
        top_ref[j:j + 1, :] = top
        total_ref[j:j + 1, :] = jnp.sum(prob, axis=0, keepdims=True)
        acc[span, :] = mm(value_t, prob.astype(BF16))

    def earlier(d, carry):
        from_earlier(d).wait_recv()
        for j, key, value_t in heads_of(d):
            span = slice(j * HEAD, (j + 1) * HEAD)
            scores = mm(key, q_turn[span, :]) * scale
            old = top_ref[j:j + 1, :]
            top = jnp.maximum(old, jnp.max(scores, axis=0, keepdims=True))
            fade = jnp.exp2(old - top)
            prob = jnp.exp2(scores - top)
            top_ref[j:j + 1, :] = top
            total_ref[j:j + 1, :] = total_ref[j:j + 1, :] * fade + jnp.sum(prob, axis=0, keepdims=True)
            acc[span, :] = acc[span, :] * fade + mm(value_t, prob.astype(BF16))
        return carry

    serve(1)
    lax.fori_loop(1, me + 1, earlier, 0)
    serve(2)
    total = total_ref[...]
    lse_ref[...] = top_ref[...] + jnp.log2(total)
    total_ref[...] = 1.0 / total
    for pair in range(HEADS // 2):
        col = pair * LANES
        halves_t = [acc[col + k * HEAD:col + (k + 1) * HEAD, :] * total_ref[2 * pair + k:2 * pair + k + 1, :] for k in range(2)]
        both_t = jnp.concatenate(halves_t, axis=0).astype(BF16)
        attended_turn[col:col + LANES, :] = both_t
        attended_ref[:, col:col + LANES] = both_t.T
        normed_turn[col:col + LANES, :] = normed_ref[:, col:col + LANES].T
    for d in range(n):
        @pl.when(me >= d)
        def _(d=d):
            kv_ref[d] = land[d]
    loads[2].wait()
    for at in range(0, width, chunk):
        mid_ref[:, at:at + chunk] = x_ref[:, at:at + chunk].astype(F32) + mm(attended_ref[...], wo_ref[:, at:at + chunk])
    for d in range(1, n):
        @pl.when(me + d < n)
        def _(d=d):
            to_later(d).wait_send()


def attend_block_kernel(*refs):
    n = lax.axis_size("shard")
    me = lax.axis_index("shard")
    barrier = pltpu.get_barrier_semaphore()
    for d in range(1, n):
        @pl.when(me >= d)
        def _(d=d):
            pl.semaphore_signal(barrier, inc=1, device_id={"shard": me - d}, device_id_type=MESH_IDS)

    def greeted():
        @pl.when(me < n - 1)
        def _():
            pl.semaphore_wait(barrier, n - 1 - me)
    attend_steps(greeted, lambda: None, lambda pieces: None, *refs)


def attend_scratch(rows, width, n, kv_both):
    dma = pltpu.SemaphoreType.DMA
    return [
        pltpu.VMEM((rows, width), BF16), pltpu.VMEM((rows, width), BF16),
        pltpu.VMEM((width, width), BF16), pltpu.VMEM((width, kv_both), BF16), pltpu.VMEM((width, width), BF16),
        pltpu.VMEM((width, rows), BF16), pltpu.VMEM((width, rows), F32),
        pltpu.VMEM((HEADS, rows), F32), pltpu.VMEM((HEADS, rows), F32),
        pltpu.VMEM((n, rows, kv_both), BF16),
        dma((3,)), dma((n - 1,)), dma((n - 1,)),
    ]


def attend_outputs(rows, width, n, kv_both):
    return [
        jax.ShapeDtypeStruct((width, rows), BF16),
        jax.ShapeDtypeStruct((rows, width), BF16),
        jax.ShapeDtypeStruct((n, rows, kv_both), BF16),
        jax.ShapeDtypeStruct((width, rows), BF16),
        jax.ShapeDtypeStruct((HEADS, rows), F32),
        jax.ShapeDtypeStruct((rows, width), F32),
    ]


def attend_block(x, gain, cos_table, sin_table, w_q, w_kv, w_o, collective_id):
    n = lax.axis_size("shard")
    rows, width = x.shape
    kv_both = w_kv.shape[1]
    vmem = pl.BlockSpec(memory_space=pltpu.VMEM)
    anywhere = pl.BlockSpec(memory_space=pl.ANY)
    flops = 2 * rows * width * (2 * width + kv_both) + 4 * rows * rows * n * width
    return pl.pallas_call(
        attend_block_kernel,
        in_specs=[vmem] * 4 + [anywhere] * 3,
        out_specs=[vmem] * 6,
        out_shape=attend_outputs(rows, width, n, kv_both),
        scratch_shapes=attend_scratch(rows, width, n, kv_both),
        compiler_params=pltpu.CompilerParams(
            collective_id=collective_id, has_side_effects=True, vmem_limit_bytes=56 * 1024 * 1024),
        cost_estimate=pl.CostEstimate(flops=flops, bytes_accessed=2 * width * (2 * width + kv_both), transcendentals=rows * rows * n * HEADS),
        name="attend_block",
    )(x, gain, cos_table, sin_table, w_q, w_kv, w_o)


def attend_back_kernel(da_ref, dmid_ref, x_ref, gain_ref, cos_ref, sin_ref, q_ref, kv_ref, attended_turn, lse_ref, w_q, w_kv, w_o,
                       dq_ref, dkv_ref, grad_ref, grad_low_ref, dgain_ref,
                       wq_ref, wkv_ref, wo_ref, do_ref, q_turn, do_turn, delta_ref, dq_acc, dkv_acc, dn_ref, send_kv, land_kv,
                       load_sem, send_sem, recv_sem):
    n = lax.axis_size("shard")
    me = lax.axis_index("shard")
    rows, width = x_ref.shape
    kv_width = wkv_ref.shape[1] // 2
    pairs = HEADS // KV_HEADS // 2
    scale = LOG2E * HEAD ** -0.5
    barrier = pltpu.get_barrier_semaphore()
    for d in range(1, n):
        @pl.when(me + d < n)
        def _(d=d):
            pl.semaphore_signal(barrier, inc=1, device_id={"shard": me + d}, device_id_type=MESH_IDS)
    loads = [pltpu.make_async_copy(src, dst, load_sem.at[k])
             for k, (src, dst) in enumerate(((w_o, wo_ref), (w_q, wq_ref), (w_kv, wkv_ref)))]
    for load in loads:
        load.start()

    def to_earlier(d):
        return remote(send_kv.at[d - 1], land_kv.at[d - 1], send_sem.at[d - 1], recv_sem.at[d - 1], {"shard": me - d})

    def from_later(d):
        return remote(send_kv.at[d - 1], land_kv.at[d - 1], send_sem.at[d - 1], recv_sem.at[d - 1], {"shard": me + d})

    chunk = 4 * LANES
    for at in range(0, width, LANES):
        q_turn[at:at + LANES, :] = q_ref[:, at:at + LANES].T
    loads[0].wait()
    for at in range(0, width, chunk):
        do_chunk = mm_t(da_ref[...], wo_ref[at:at + chunk, :]).astype(BF16)
        do_ref[:, at:at + chunk] = do_chunk
        do_turn[at:at + chunk, :] = do_chunk.T
    for j in range(HEADS):
        span = slice(j * HEAD, (j + 1) * HEAD)
        both = attended_turn[span, :].astype(F32) * do_turn[span, :].astype(F32)
        delta_ref[j:j + 1, :] = jnp.sum(both, axis=0, keepdims=True)
    dq_acc[...] = jnp.zeros_like(dq_acc)
    low_lane = lax.broadcasted_iota(jnp.int32, (rows, LANES), 1) < HEAD
    zero_rows = jnp.zeros((rows, LANES), BF16)

    def block(d, bias):
        for h in range(KV_HEADS):
            own = slice(h * HEAD, (h + 1) * HEAD)
            key = kv_ref[d, :, own]
            value = kv_ref[d, :, kv_width + h * HEAD:kv_width + (h + 1) * HEAD]
            key_t = kv_ref[d, :, h // 2 * LANES:(h // 2 + 1) * LANES].T[h % 2 * HEAD:(h % 2 + 1) * HEAD, :]
            dk = jnp.zeros((rows, LANES), F32)
            dv = jnp.zeros((rows, LANES), F32)
            for pair in range(h * pairs, (h + 1) * pairs):
                cols = slice(pair * LANES, (pair + 1) * LANES)
                q_rows = q_ref[:, cols]
                do_rows = do_ref[:, cols]
                for k in range(2):
                    j = 2 * pair + k
                    span = slice(j * HEAD, (j + 1) * HEAD)
                    lane = low_lane if k == 0 else jnp.logical_not(low_lane)
                    scores = mm(key, q_turn[span, :]) * scale
                    if bias is not None:
                        scores = scores + bias
                    prob = jnp.exp2(scores - lse_ref[j:j + 1, :])
                    dprob = mm(value, do_turn[span, :])
                    dscore = (prob * (dprob - delta_ref[j:j + 1, :])).astype(BF16)
                    dq_acc[span, :] += mm(key_t, dscore)
                    dk = dk + mm(dscore, jnp.where(lane, q_rows, zero_rows))
                    dv = dv + mm(prob.astype(BF16), jnp.where(lane, do_rows, zero_rows))
            dkv_acc[:, own] = (dk[:, :HEAD] + dk[:, HEAD:]) * HEAD ** -0.5
            dkv_acc[:, kv_width + h * HEAD:kv_width + (h + 1) * HEAD] = dv[:, :HEAD] + dv[:, HEAD:]

    @pl.when(me > 0)
    def _():
        pl.semaphore_wait(barrier, me)

    def earlier(i, carry):
        d = me - i
        block(d, None)
        send_kv[d - 1] = dkv_acc[...].astype(BF16)
        to_earlier(d).start()
        return carry

    lax.fori_loop(0, me, earlier, 0)
    key_pos = lax.broadcasted_iota(jnp.int32, (rows, rows), 0)
    query_pos = lax.broadcasted_iota(jnp.int32, (rows, rows), 1)
    block(0, jnp.where(key_pos <= query_pos, 0.0, NEG_FILL))

    loads[1].wait()
    loads[2].wait()
    for at in range(0, width, chunk):
        for col in range(at, at + chunk, LANES):
            dq_ref[:, col:col + LANES] = rotated(dq_acc[col:col + LANES, :].T * HEAD ** -0.5, cos_ref, sin_ref).astype(BF16)
    for at in range(0, width, chunk):
        dn_ref[:, at:at + chunk] = mm_t(dq_ref[...], wq_ref[at:at + chunk, :])
    for d in range(1, n):
        @pl.when(me + d < n)
        def _(d=d):
            from_later(d).wait_recv()
            dkv_acc[...] += land_kv[d - 1].astype(F32)
    dkv_ref[:, :kv_width] = rotated(dkv_acc[:, :kv_width], cos_ref, sin_ref).astype(BF16)
    dkv_ref[:, kv_width:] = dkv_acc[:, kv_width:].astype(BF16)
    for at in range(0, width, chunk):
        dn_ref[:, at:at + chunk] += mm_t(dkv_ref[...], wkv_ref[at:at + chunk, :])
    x = x_ref[...].astype(F32)
    root = inv_root_of(x)
    dnormed = dn_ref[...]
    scaled = dnormed * gain_ref[...]
    grad = dmid_ref[...] + root * scaled - x * (root * root * root * jnp.mean(scaled * x, axis=-1, keepdims=True))
    grad_ref[...] = grad
    grad_low_ref[...] = grad.astype(BF16)
    dgain_ref[...] = jnp.sum(dnormed * x * root, axis=0, keepdims=True)
    for d in range(1, n):
        @pl.when(me >= d)
        def _(d=d):
            to_earlier(d).wait_send()


def attend_back(da, dmid, x, gain, cos_table, back_sin, q, kv, attended, lse, w_q, w_kv, w_o, collective_id):
    n = lax.axis_size("shard")
    rows, width = x.shape
    kv_both = w_kv.shape[1]
    vmem = pl.BlockSpec(memory_space=pltpu.VMEM)
    anywhere = pl.BlockSpec(memory_space=pl.ANY)
    dma = pltpu.SemaphoreType.DMA
    flops = 2 * rows * width * (2 * width + kv_both) + 10 * rows * rows * n * width
    return pl.pallas_call(
        attend_back_kernel,
        in_specs=[vmem] * 10 + [anywhere] * 3,
        out_specs=[vmem] * 5,
        out_shape=[
            jax.ShapeDtypeStruct((rows, width), BF16),
            jax.ShapeDtypeStruct((rows, kv_both), BF16),
            jax.ShapeDtypeStruct((rows, width), F32),
            jax.ShapeDtypeStruct((rows, width), BF16),
            jax.ShapeDtypeStruct((1, width), F32),
        ],
        scratch_shapes=[
            pltpu.VMEM(w_q.shape, BF16), pltpu.VMEM(w_kv.shape, BF16), pltpu.VMEM(w_o.shape, BF16),
            pltpu.VMEM((rows, width), BF16), pltpu.VMEM((width, rows), BF16), pltpu.VMEM((width, rows), BF16),
            pltpu.VMEM((HEADS, rows), F32), pltpu.VMEM((width, rows), F32), pltpu.VMEM((rows, kv_both), F32),
            pltpu.VMEM((rows, width), F32),
            pltpu.VMEM((n - 1, rows, kv_both), BF16), pltpu.VMEM((n - 1, rows, kv_both), BF16),
            dma((3,)), dma((n - 1,)), dma((n - 1,)),
        ],
        compiler_params=pltpu.CompilerParams(
            collective_id=collective_id, has_side_effects=True, vmem_limit_bytes=58 * 1024 * 1024),
        cost_estimate=pl.CostEstimate(flops=flops, bytes_accessed=2 * width * (2 * width + kv_both), transcendentals=rows * rows * n * HEADS),
        name="attend_back",
    )(da, dmid, x, gain, cos_table, back_sin, q, kv, attended, lse, w_q, w_kv, w_o)


ROPE_BASE = 10000.0


def angles_for(positions):
    half_dim = HEAD // 2
    inverse = ROPE_BASE ** (-(jnp.arange(half_dim, dtype=F32) * 2.0 / HEAD))
    angle_grid = positions.astype(F32)[:, None] * inverse[None, :]
    return (jnp.cos(angle_grid), jnp.sin(angle_grid))


def passed_along(block, axis, by):
    length = lax.axis_size(axis)
    pairs = [(i, i + by) for i in range(length) if 0 <= i + by < length]
    return lax.ppermute(block, axis, pairs)


Y_PAIRS = [(0, 2), (2, 0), (1, 3), (3, 1)]


def halves_of(grad_gate, grad_up):
    half = grad_gate.shape[1] // 2
    at = (1 - lax.axis_index("rep") // 2) * half
    parts = [lax.dynamic_slice_in_dim(term, at, half, 1) for term in (grad_gate, grad_up)]
    return lax.ppermute(jnp.concatenate(parts, axis=1), "rep", Y_PAIRS)


def layer_forward(stream_in, weights, tables, pending, done):
    w_q, w_kv, w_o, w_g, w_u, w_d, gains_wide = weights
    cos_table, sin_table = tables
    normed, queries, kv, attended, lse, middle = done or attend_block(
        stream_in, gains_wide[0:1], cos_table, sin_table, w_q, w_kv, w_o, 3)
    middle, pending = lax.optimization_barrier((middle, pending))
    result, normed_two, hidden, gate_fac, up_fac = ffn_fwd(middle, gains_wide[1:2], w_g, w_u, w_d)
    kept = {"stream": stream_in, "normed": normed, "queries": queries, "kv": kv, "attended": attended, "lse": lse,
            "middle": middle, "normed_two": normed_two, "hidden": hidden, "gate_fac": gate_fac, "up_fac": up_fac}
    return result, kept, pending


def layer_backward(grad_bf, kept, weights, tables, pending):
    w_q, w_kv, w_o, w_g, w_u, w_d, gains_wide = weights
    cos_table, sin_table = tables
    grad_gate, grad_up, grad_middle, grad_branch, gain_two = ffn_bwd(
        grad_bf, kept["middle"], gains_wide[1:2], kept["gate_fac"], kept["up_fac"], w_g, w_u, w_d)
    grad_branch, pending = lax.optimization_barrier((grad_branch, pending))
    halves_out = halves_of(grad_gate, grad_up)
    grad_query, grad_kv, grad_stream, grad_low, gain_one = attend_back(
        grad_branch, grad_middle, kept["stream"], gains_wide[0:1], cos_table, -sin_table, kept["queries"], kept["kv"],
        kept["attended"], kept["lse"], w_q, w_kv, w_o, 4)
    terms = (grad_query, grad_kv, grad_branch, grad_gate, grad_up, grad_bf, halves_out)
    return grad_stream, grad_low, terms, jnp.concatenate([gain_one, gain_two], axis=0), pending


def body(tokens, cotangent, live_counts, w_query, w_key, w_value, w_out, w_gate, w_up, w_down, norm_gains):
    section = lax.axis_index("section")
    slot_count, span_len, model_width = tokens.shape
    query_pos = lax.axis_index("shard") * span_len + jnp.arange(span_len, dtype=jnp.int32)
    cos_half, sin_half = angles_for(query_pos)
    tables = (jnp.tile(cos_half, (1, 4)), jnp.tile(jnp.concatenate([-sin_half, sin_half], axis=1), (1, 2)))
    live_mask = (jnp.arange(slot_count) < live_counts[0]).astype(BF16)
    gain_rows = jnp.pad(norm_gains[0], ((0, 14), (0, -norm_gains.shape[2] % (4 * LANES))))
    shards = [w_query[0], jnp.concatenate([w_key[0], w_value[0]], axis=1), w_out[0], gain_rows, w_gate[0], w_up[0], w_down[0]]
    first_in = jnp.where(section == 0, tokens[0] * live_mask[0], jnp.zeros_like(tokens[0]))
    gathered, attended_first = gather_weights(
        first_in, *tables, shards, [halves(shard.shape[1]) for shard in shards], 2, "gather_weights")
    w_q, w_kv, w_o, gains, w_g, w_u, w_d = gathered
    gain_blocks = gains.reshape(-1, 16, gain_rows.shape[1])[:, :2, :norm_gains.shape[2]]
    gains_wide = gain_blocks.transpose(1, 0, 2).reshape(2, model_width).astype(F32)
    weights = (w_q, w_kv, w_o, w_g, w_u, w_d, gains_wide)
    zero_slot = jnp.zeros((span_len, model_width), BF16)
    ticks = slot_count + 1
    results, kept_all, others = [], [], []
    pending = []
    received = zero_slot
    for tick in range(ticks):
        slot_in = tokens[tick] * live_mask[tick] if tick < slot_count else zero_slot
        own_in = jnp.where(section == 0, slot_in, received) if tick else first_in
        result, kept, pending = layer_forward(own_in, weights, tables, pending, None if tick else attended_first)
        others += pending
        pending = [lax.ppermute(kept["normed_two"], "rep", Y_PAIRS)]
        received = passed_along(result, "section", 1)
        results.append(result)
        kept_all.append(kept)
    first = section == 0
    acts = jnp.stack([jnp.where(first, results[j], results[j + 1]) for j in range(slot_count)])
    received = zero_slot
    streams, term_list, gain_total = [], [], 0.0
    for tick in range(ticks):
        slot_cot = cotangent[slot_count - 1 - tick] * live_mask[slot_count - 1 - tick] if tick < slot_count else zero_slot
        grad_bf = jnp.where(first, received, slot_cot)
        grad_stream, grad_low, terms, gain_grad, pending = layer_backward(
            grad_bf, kept_all[ticks - 1 - tick], weights, tables, pending)
        others += pending
        pending = [terms[6]]
        received = passed_along(grad_low, "section", -1)
        streams.append(grad_stream)
        term_list.append(terms)
        gain_total = gain_total + gain_grad
    grad_in = jnp.stack([
        jnp.where(first, streams[slot_count - j], streams[slot_count - 1 - j]) for j in range(slot_count)])

    others += pending
    normed_others, half_others = others[ticks - 1::-1], others[ticks:]

    def kept_by_tick(name):
        return [kept_all[ticks - 1 - tick][name] for tick in range(ticks)]

    def by_tick(index):
        return [terms[index] for terms in term_list]

    gate_sum, up_sum, qkv_sum, out_sum, down_sum, gain_sum = reduce_weights(
        jnp.pad(gain_total, ((0, 6), (0, 0))),
        [
            {"kind": "pair", "blocks": 1, "pace": 1, "delay": 3, "which": [0, 0],
             "lefts": [[kept_by_tick("normed_two"), normed_others]],
             "rights": [[by_tick(3), half_others], [by_tick(4), half_others]]},
            {"kind": "y", "blocks": 1, "pace": 2, "delay": 2, "which": [0, 1],
             "lefts": [[kept_by_tick("normed")], [kept_by_tick("attended")]],
             "rights": [[by_tick(0), by_tick(1)], [by_tick(2)]]},
            {"kind": "y", "blocks": 2, "pace": 2, "delay": 2, "which": [0],
             "lefts": [[kept_by_tick("hidden")]], "rights": [[by_tick(5)]]},
        ],
        slot_count, 1, "reduce_weights")
    kv_width = w_key.shape[2]
    outs = (
        qkv_sum[:, :model_width],
        qkv_sum[:, model_width:model_width + kv_width],
        qkv_sum[:, model_width + kv_width:],
        out_sum,
        gate_sum,
        up_sum,
        down_sum,
        gain_sum[:2],
    )
    return (acts[None], grad_in[None]) + tuple(out.astype(F32)[None] for out in outs)


def solution(mesh):
    tall = P("section", "shard", None)
    per_slot = P("section", "rep", "shard", None)
    return jax.shard_map(
        body,
        mesh=mesh,
        in_specs=(P("rep", "shard", None), P("rep", "shard", None), P("rep")) + (tall,) * 7 + (P("section", None, "shard"),),
        out_specs=(per_slot, per_slot) + (tall,) * 7 + (P("section", None, "shard"),),
        check_vma=False,
    )
```
